32 devices in a mesh: dp: 8 (over z, x), tensor: 4 (over y, core).
Axes of the slice: x: 2, y: 2, z: 4, core: 2. Of those that a mesh axis runs over, the one named last changes fastest.
Arguments:
- tokens: bfloat16 [16384, 768], P(('dp', 'tensor')), may hold values from -6 to 6
- cotangent: bfloat16 [16384, 768], P(('dp', 'tensor')), may hold values from -6 to 6
- w_query: float32 [768, 768], P('dp', 'tensor'), may hold values from -0.0546875 to 0.0546875
- w_key: float32 [768, 768], P('dp', 'tensor'), may hold values from -0.21875 to 0.21875
- w_value: float32 [768, 768], P('dp', 'tensor'), may hold values from -0.21875 to 0.21875
- w_proj: float32 [768, 768], P('tensor', 'dp'), may hold values from -1.25 to 1.25
- w_inner: float32 [768, 3072], P('dp', 'tensor'), may hold values from -0.21875 to 0.21875
- w_outer: float32 [3072, 768], P('tensor', 'dp'), may hold values from -0.15625 to 0.15625
- gain_attn: float32 [768], replicated, may hold values from 0.5 to 1.5
- gain_ffn: float32 [768], replicated, may hold values from 0.5 to 1.5
- rel_table: float32 [32, 12], replicated, may hold values from -4 to 4
- lengths: int32 [8, 2], P('dp'), may hold values from 512 to 1536, as said below
- deal: int32 [16384], P(('dp', 'tensor')), may hold values from 0 to 511, as said below
- buckets: int32 [257], replicated, may hold values from 0 to 31
Outputs:
- output: bfloat16 [16384, 768], P(('dp', 'tensor'))
- grad_tokens: bfloat16 [16384, 768], P(('dp', 'tensor'))
- grad_query: float32 [768, 768], P('dp', 'tensor')
- grad_key: float32 [768, 768], P('dp', 'tensor')
- grad_value: float32 [768, 768], P('dp', 'tensor')
- grad_proj: float32 [768, 768], P('tensor', 'dp')
- grad_inner: float32 [768, 3072], P('dp', 'tensor')
- grad_outer: float32 [3072, 768], P('tensor', 'dp')
- grad_gain_attn: float32 [768], replicated
- grad_gain_ffn: float32 [768], replicated
- grad_table: float32 [32, 12], replicated
The draws below stay inside these ranges and needn't reach their ends.
Inputs may be any that keep to these rules, and one draw needn't show every extreme that they name: `deal`: each device's 512 consecutive entries are an ordering of 0 to 511. The two lengths of a group sum to 2048; some group holds one of 1536.
All inputs are finite; a program needn't handle non-finite values.
Results may differ from the reference program's by a relative error of at most 0.018.
Values may be sent and summed in bfloat16 or wider, within the bound.
No kernel may reach another device: no remote copies, remote signals or barrier semaphores. Data moves between devices by JAX's collectives and lax.ppermute only.
A program may use at most 256 MiB of HBM per device.

```python
import jax
import jax.numpy as jnp
from jax import lax

D = 768
HEADS = 12
HEAD_DIM = 64
FF = 3072
NBUCKET = 32
MAXDIST = 128
TOK_DEV = 512
SEQ_MIN = 512
GROUPS = 8
GROUP_DEVS = 4
GROUP_TOK = 2048
TOKENS = 16384
SLOT = 64
OFFSETS = 257


def draw_lengths(key, part):
    first = jax.random.randint(jax.random.fold_in(key, 11), (GROUPS,), SEQ_MIN, GROUP_TOK - SEQ_MIN + 1, dtype=jnp.int32)
    chosen = jax.random.randint(jax.random.fold_in(key, 12), (), 0, GROUPS, dtype=jnp.int32)
    first = jnp.where(jnp.arange(GROUPS, dtype=jnp.int32) == chosen, jnp.int32(GROUP_TOK - SEQ_MIN), first)
    return jnp.stack([first, jnp.int32(GROUP_TOK) - first], axis=1).astype(jnp.int32)


def draw_deal(key, part):
    blocks = TOKENS // TOK_DEV
    subkeys = jax.random.split(jax.random.fold_in(key, 21), blocks)
    orders = jax.vmap(lambda single: jax.random.permutation(single, TOK_DEV).astype(jnp.int32))(subkeys)
    return orders.reshape(TOKENS).astype(jnp.int32)


def touch_ends(values, stream_key, smallest, top_value):
    dims = values.shape
    spot = [jax.random.randint(jax.random.fold_in(stream_key, axis), (), 0, dims[axis]) for axis in range(len(dims))]
    values = values.at[tuple(spot)].set(smallest)
    longest = dims.index(max(dims))
    spot[longest] = (spot[longest] + 1) % dims[longest]
    return values.at[tuple(spot)].set(top_value)


def shard_levels(stream_key, shape, shards, smallest, top_value):
    level, own = 1.0, jax.random.fold_in(stream_key, 6)
    for dim, parts in shards:
        draws = jnp.exp(jax.random.uniform(jax.random.fold_in(own, dim), (parts,), jnp.float32, smallest / len(shards), top_value / len(shards)))
        level = level * jnp.repeat(draws, shape[dim] // parts).reshape([-1 if axis == dim else 1 for axis in range(len(shape))])
    return level


def centred(own_key, extent, spread, limit, cuts=(), kind=jnp.bfloat16):
    values = spread * jax.random.normal(own_key, extent, jnp.float32)
    if cuts:
        values = values * shard_levels(own_key, extent, cuts, -0.22, 0.18)
    return jnp.clip(values, -limit, limit).astype(kind)


def setup_inputs(seed: int = 0) -> dict:
    key_of = jax.random.split(jax.random.key(seed), 15)
    tokens = centred(key_of[0], (TOKENS, D), 1.0, 6.0, ((0, 32),))
    cotangent = centred(key_of[1], (TOKENS, D), 1.0, 6.0, ((0, 32),))
    w_query = centred(key_of[2], (D, HEADS * HEAD_DIM), (16 * D) ** -0.5, 0.0546875, ((0, 8), (1, 4)), jnp.float32)
    w_key = centred(key_of[3], (D, HEADS * HEAD_DIM), D ** -0.5, 0.21875, ((0, 8), (1, 4)), jnp.float32)
    w_value = centred(key_of[4], (D, HEADS * HEAD_DIM), D ** -0.5, 0.21875, ((0, 8), (1, 4)), jnp.float32)
    w_proj = centred(key_of[5], (HEADS * HEAD_DIM, D), (HEADS * HEAD_DIM // 32) ** -0.5, 1.25, ((0, 4), (1, 8)), jnp.float32)
    w_inner = centred(key_of[6], (D, FF), D ** -0.5, 0.21875, ((0, 8), (1, 4)), jnp.float32)
    w_outer = centred(key_of[7], (FF, D), (FF // 2) ** -0.5, 0.15625, ((0, 4), (1, 8)), jnp.float32)
    gain_attn = jnp.clip(1.0 + 0.1 * jax.random.normal(key_of[8], (D,), jnp.float32), 0.5, 1.5)
    gain_ffn = jnp.clip(1.0 + 0.1 * jax.random.normal(key_of[9], (D,), jnp.float32), 0.5, 1.5)
    rel_table = centred(key_of[10], (NBUCKET, HEADS), 1.0, 4.0, (), jnp.float32)
    lengths = draw_lengths(jax.random.fold_in(key_of[14], 71), 0)
    deal = draw_deal(jax.random.fold_in(key_of[14], 71), 0)
    buckets = touch_ends(jax.random.randint(key_of[13], (OFFSETS,), 0, NBUCKET), jax.random.fold_in(key_of[13], 1), 0, NBUCKET - 1).astype(jnp.int32)
    return {"tokens": tokens, "cotangent": cotangent, "w_query": w_query, "w_key": w_key, "w_value": w_value, "w_proj": w_proj, "w_inner": w_inner, "w_outer": w_outer, "gain_attn": gain_attn, "gain_ffn": gain_ffn, "rel_table": rel_table, "lengths": lengths, "deal": deal, "buckets": buckets}


@jax.custom_vjp
def low(v):
    return lax.optimization_barrier(v.astype(jnp.bfloat16)).astype(jnp.float32)

@jax.custom_vjp
def low_back(v):
    return v

def low_keep(v):
    return (low(v), None)

def low_pass(kept, grad):
    return (grad,)

def back_keep(v):
    return (v, None)

def back_low(kept, grad):
    return (low(grad),)
low.defvjp(low_keep, low_pass)
low_back.defvjp(back_keep, back_low)
EPS = 1e-06
NEG = -1000000000.0

def matmul(left, right):
    return jnp.dot(left, right, precision=lax.Precision.HIGHEST)

def rms_norm(values, gain):
    scale = lax.rsqrt(lax.optimization_barrier(jnp.mean(values * values, axis=-1, keepdims=True)) + jnp.asarray(EPS, values.dtype))
    return values * scale * gain

def activate(values):
    return jax.nn.gelu(values, approximate=True)

def group_layer(rows, lens, params, buckets):
    w_query, w_key, w_value, w_proj, w_inner, w_outer, gain_attn, gain_ffn, rel_table = params
    count = rows.shape[0]
    place = jnp.arange(count, dtype=jnp.int32)
    first_len = lens[0].astype(jnp.int32)
    second = (place >= first_len).astype(jnp.int32)
    within = (place - second * first_len).astype(jnp.int32)
    same = second[:, None] == second[None, :]
    gap = (within[None, :] - within[:, None]).astype(jnp.int32)
    offset = (jnp.clip(gap, jnp.int32(-MAXDIST), jnp.int32(MAXDIST)) + jnp.int32(MAXDIST)).astype(jnp.int32)
    bias = jnp.transpose(rel_table[buckets[offset]], (2, 0, 1))
    normed_one = low(rms_norm(rows, gain_attn))
    queries = low(low_back(matmul(normed_one, w_query))).reshape(count, HEADS, HEAD_DIM)
    keys_all = low(low_back(matmul(normed_one, w_key))).reshape(count, HEADS, HEAD_DIM)
    values_all = low(low_back(matmul(normed_one, w_value))).reshape(count, HEADS, HEAD_DIM)
    scores = jnp.einsum('qhd,khd->hqk', queries, keys_all, precision=lax.Precision.HIGHEST) + bias
    scores = low_back(scores)
    scores = jnp.where(same[None], scores, jnp.full_like(scores, NEG))
    top = lax.optimization_barrier(jnp.max(scores, axis=-1, keepdims=True))
    exponent = jnp.exp(scores - top)
    chance = exponent / lax.optimization_barrier(jnp.sum(exponent, axis=-1, keepdims=True))
    mixed = jnp.einsum('hqk,khd->qhd', low(chance), values_all, precision=lax.Precision.HIGHEST)
    mixed = low(low_back(mixed)).reshape(count, HEADS * HEAD_DIM)
    middle = rows + low_back(matmul(mixed, w_proj))
    normed_two = low(rms_norm(middle, gain_ffn))
    before = low_back(matmul(normed_two, w_inner))
    hidden = low(activate(before))
    return middle + low_back(matmul(hidden, w_outer))

def deal_rows(flat, deal):
    width = flat.shape[-1]
    source = flat.reshape(GROUPS, GROUP_DEVS, TOK_DEV, width)
    order = deal.astype(jnp.int32).reshape(GROUPS, GROUP_DEVS, TOK_DEV)
    sent = jnp.take_along_axis(source, order[..., None], axis=2)
    sent = sent.reshape(GROUPS, GROUP_DEVS, GROUPS, SLOT, width)
    return sent.transpose(2, 1, 0, 3, 4).reshape(GROUPS, GROUP_TOK, width)

def undeal_rows(grouped, deal):
    width = grouped.shape[-1]
    back = grouped.reshape(GROUPS, GROUP_DEVS, GROUPS, SLOT, width).transpose(2, 1, 0, 3, 4)
    back = back.reshape(GROUPS * GROUP_DEVS, TOK_DEV, width)
    order = deal.astype(jnp.int32).reshape(GROUPS * GROUP_DEVS, TOK_DEV)
    counting = jnp.broadcast_to(jnp.arange(TOK_DEV, dtype=jnp.int32)[None, :], (GROUPS * GROUP_DEVS, TOK_DEV))
    blocks = jnp.broadcast_to(jnp.arange(GROUPS * GROUP_DEVS, dtype=jnp.int32)[:, None], (GROUPS * GROUP_DEVS, TOK_DEV))
    inverse = jnp.zeros((GROUPS * GROUP_DEVS, TOK_DEV), jnp.int32).at[blocks, order].set(counting)
    return jnp.take_along_axis(back, inverse[..., None], axis=1).reshape(TOKENS, width)

def reference(tokens, cotangent, w_query, w_key, w_value, w_proj, w_inner, w_outer, gain_attn, gain_ffn, rel_table, lengths, deal, buckets):
    rows = deal_rows(tokens.astype(jnp.float32), deal)
    grads_in = deal_rows(cotangent.astype(jnp.float32), deal)
    lens_all = lengths.astype(jnp.int32)
    bucket_map = buckets.astype(jnp.int32)

    def forward(rows_all, wq, wk, wv, wo, wi, wf, gone, gtwo, table):
        params = (low(wq), low(wk), low(wv), low(wo), low(wi), low(wf), gone, gtwo, table)
        step = jax.checkpoint(group_layer)
        return lax.map(lambda pair: step(pair[0], pair[1], params, bucket_map), (rows_all, lens_all))
    result, pullback = jax.vjp(forward, rows, w_query, w_key, w_value, w_proj, w_inner, w_outer, gain_attn, gain_ffn, rel_table)
    grads = pullback(grads_in)
    output = undeal_rows(result, deal).astype(jnp.bfloat16)
    grad_tokens = undeal_rows(grads[0], deal).astype(jnp.bfloat16)
    return (output, grad_tokens, grads[1], grads[2], grads[3], grads[4], grads[5], grads[6], grads[7], grads[8], grads[9])
```

```python
import functools

import jax
import jax.numpy as jnp
from jax import lax
from jax.experimental import pallas as pl
from jax.experimental.pallas import tpu as pltpu
from jax.sharding import PartitionSpec as P

HEAD_DIM = 64
MAXDIST = 128
TILE = 256
KINDS = 5
EPS = 1e-06
NEG = -1000000000.0
BF16 = jnp.bfloat16
F32 = jnp.float32
VMEM = pl.BlockSpec(memory_space=pltpu.VMEM)
SMEM = pl.BlockSpec(memory_space=pltpu.SMEM)


def mm(left, right):
    return jnp.dot(left, right, preferred_element_type=F32)


def contract(left, left_dim, right, right_dim):
    return lax.dot_general(
        left, right, (((left_dim,), (right_dim,)), ((), ())), preferred_element_type=F32
    )


def row_norm(values):
    scale = lax.rsqrt(jnp.mean(values * values, axis=-1, keepdims=True) + EPS)
    return (values * scale, scale)


def norm_back(upstream, normed, scale, gain):
    scaled = upstream * gain
    inner = jnp.mean(scaled * normed, axis=-1, keepdims=True)
    return (scale * (scaled - normed * inner), jnp.sum(upstream * normed, axis=0))


def tile_start(tile, rows_dev, me):
    per_slot = rows_dev // TILE
    return pl.multiple_of((((tile // per_slot) ^ me) * per_slot + tile % per_slot) * TILE, TILE)


def build_bias(base_ref, bias_ref, heads):
    for i in range(heads * KINDS):
        row = base_ref[i : i + 1, :]
        if i % KINDS in (0, KINDS - 1):
            bias_ref[i] = jnp.broadcast_to(row[:, :1], (TILE, TILE))
        else:
            full = jnp.broadcast_to(row, (TILE, 2 * TILE))
            bias_ref[i] = pltpu.roll(full, 0, 1, stride=1, stride_axis=0)[:, TILE:]


def segment_rows(width, first_len, start, same, other):
    shape = (HEAD_DIM, width)
    low = start + lax.broadcasted_iota(jnp.int32, shape, 1) < first_len
    row = lax.broadcasted_iota(jnp.int32, shape, 0)
    first = jnp.where(low, same, other)
    second = jnp.where(low, other, same)
    return jnp.where(row == 0, first, jnp.where(row == 1, second, 0.0)).astype(BF16)


def segment_all(rows, rows_dev, first_len, me, same, other):
    slots = rows // rows_dev
    return jnp.concatenate(
        [
            segment_rows(rows_dev, first_len, (s ^ me) * rows_dev, same, other)
            for s in range(slots)
        ],
        axis=1,
    )


def tile_range(tile, first_len, tiles):
    start = tile * TILE
    low = jnp.where(start >= first_len, first_len // TILE, 0)
    high = jnp.where(start + TILE <= first_len, (first_len + TILE - 1) // TILE, tiles)
    return low, high


def attend_kernel(
    heads, rows_dev, info_ref, base_ref, qkv_ref, out_ref, wide_ref, lse_ref, key_ref, score_ref, bias_ref
):
    rows = qkv_ref.shape[1]
    cols = heads * HEAD_DIM
    first_len, me = info_ref[0, 0], info_ref[0, 2]
    tiles = rows // TILE
    build_bias(base_ref, bias_ref, heads)
    key_seg = segment_all(rows, rows_dev, first_len, me, 1.0, 0.0)
    for h in range(heads):
        key_ref[h] = jnp.concatenate(
            [qkv_ref[cols + h * HEAD_DIM : cols + (h + 1) * HEAD_DIM, :], key_seg], axis=0
        ).T

    def query_tile(qb, carry):
        qs = pl.ds(tile_start(qb, rows_dev, me), TILE)
        query_seg = segment_rows(TILE, first_len, qb * TILE, 0.0, NEG)
        queries = [
            jnp.concatenate([qkv_ref[h * HEAD_DIM : (h + 1) * HEAD_DIM, qs], query_seg], axis=0)
            for h in range(heads)
        ]
        low, high = tile_range(qb, first_len, tiles)

        def score_tile(kb, tops):
            ks = pl.ds(tile_start(kb, rows_dev, me), TILE)
            kind = jnp.clip(kb - qb, -2, 2) + 2
            out = []
            for h in range(heads):
                s = mm(key_ref[h, ks, :], queries[h]) + bias_ref[h * KINDS + kind]
                score_ref[h, ks, :] = s
                out.append(jnp.maximum(tops[h], jnp.max(s.reshape(TILE // 8, 8, TILE), axis=0)))
            return tuple(out)

        tops = lax.fori_loop(
            low, high, score_tile, tuple(jnp.full((8, TILE), -3e38, F32) for _ in range(heads))
        )
        tops = [jnp.max(t, axis=0, keepdims=True) for t in tops]

        def value_tile(kb, sums):
            ks = pl.ds(tile_start(kb, rows_dev, me), TILE)
            out = []
            for h in range(heads):
                total, acc = sums[h]
                p = jnp.exp(score_ref[h, ks, :] - tops[h])
                total = total + jnp.sum(p.reshape(TILE // 8, 8, TILE), axis=0)
                values = qkv_ref[2 * cols + h * HEAD_DIM : 2 * cols + (h + 1) * HEAD_DIM, ks]
                out.append((total, acc + mm(values, p.astype(BF16))))
            return tuple(out)

        zero = (jnp.zeros((8, TILE), F32), jnp.zeros((HEAD_DIM, TILE), F32))
        sums = lax.fori_loop(low, high, value_tile, (zero,) * heads)
        for h in range(heads):
            total, acc = sums[h]
            total = jnp.sum(total, axis=0, keepdims=True)
            mixed = acc * (1.0 / total)
            hs = slice(h * HEAD_DIM, (h + 1) * HEAD_DIM)
            wide_ref[hs, qs] = mixed
            out_ref[hs, qs] = mixed.astype(BF16)
            lse_ref[h : h + 1, qs] = tops[h] + jnp.log(total)
        return carry

    lax.fori_loop(0, tiles, query_tile, 0)


def attend(info, base, qkv, rows_dev):
    rows = qkv.shape[1]
    heads = qkv.shape[0] // (3 * HEAD_DIM)
    cols = heads * HEAD_DIM
    return pl.pallas_call(
        functools.partial(attend_kernel, heads, rows_dev),
        out_shape=(
            jax.ShapeDtypeStruct((cols, rows), BF16),
            jax.ShapeDtypeStruct((cols, rows), F32),
            jax.ShapeDtypeStruct((heads, rows), F32),
        ),
        in_specs=[SMEM, VMEM, VMEM],
        out_specs=(VMEM, VMEM, VMEM),
        scratch_shapes=[
            pltpu.VMEM((heads, rows, 2 * HEAD_DIM), BF16),
            pltpu.VMEM((heads, rows, TILE), F32),
            pltpu.VMEM((heads * KINDS, TILE, TILE), F32),
        ],
        compiler_params=pltpu.CompilerParams(vmem_limit_bytes=32 << 20),
        cost_estimate=pl.CostEstimate(
            flops=4 * cols * rows * rows, bytes_accessed=4 * cols * rows * 4, transcendentals=heads * rows * rows
        ),
        name="attend",
    )(info, base, qkv)


def diagonal_sums(values):
    values = jnp.concatenate([jnp.zeros_like(values), values], axis=1)
    count = TILE
    while count > 1:
        count //= 2
        values = values[:count] + pltpu.roll(values[count:], 2 * TILE - count, 1)
    return values


def attend_back_kernel(
    heads,
    rows_dev,
    info_ref,
    base_ref,
    qkv_ref,
    wide_ref,
    lse_ref,
    grad_ref,
    out_ref,
    diag_ref,
    key_ref,
    query_ref,
    value_rows,
    query_rows,
    grad_rows,
    key_acc,
    value_acc,
    bias_ref,
    table_ref,
):
    rows = qkv_ref.shape[1]
    cols = heads * HEAD_DIM
    first_len, me = info_ref[0, 0], info_ref[0, 2]
    tiles = rows // TILE
    build_bias(base_ref, bias_ref, heads)
    key_seg = segment_all(rows, rows_dev, first_len, me, 1.0, 0.0)
    query_seg = segment_all(rows, rows_dev, first_len, me, 0.0, NEG)
    q_of = [slice(h * HEAD_DIM, (h + 1) * HEAD_DIM) for h in range(heads)]
    k_of = [slice(cols + h * HEAD_DIM, cols + (h + 1) * HEAD_DIM) for h in range(heads)]
    v_of = [slice(2 * cols + h * HEAD_DIM, 2 * cols + (h + 1) * HEAD_DIM) for h in range(heads)]
    for h in range(heads):
        queries = qkv_ref[q_of[h], :]
        key_ref[h] = jnp.concatenate([qkv_ref[k_of[h], :], key_seg], axis=0).T
        query_ref[h] = jnp.concatenate([queries, query_seg], axis=0)
        query_rows[h] = queries.T
        value_rows[h] = qkv_ref[v_of[h], :].T
        grad_rows[h] = grad_ref[q_of[h], :].T
    key_acc[...] = jnp.zeros_like(key_acc)
    value_acc[...] = jnp.zeros_like(value_acc)
    table_ref[...] = jnp.zeros_like(table_ref)

    def query_tile(qb, carry):
        qs = pl.ds(tile_start(qb, rows_dev, me), TILE)
        low, high = tile_range(qb, first_len, tiles)
        grads = [grad_ref[q_of[h], qs] for h in range(heads)]
        inner = [
            jnp.sum(grads[h].astype(F32) * wide_ref[q_of[h], qs], axis=0, keepdims=True)
            for h in range(heads)
        ]
        lse = [lse_ref[h : h + 1, qs] for h in range(heads)]

        def key_tile(kb, sums):
            ks = pl.ds(tile_start(kb, rows_dev, me), TILE)
            kind = jnp.clip(kb - qb, -2, 2) + 2
            out = []
            for h in range(heads):
                s = mm(key_ref[h, ks, :], query_ref[h, :, qs]) + bias_ref[h * KINDS + kind]
                p = jnp.exp(s - lse[h])
                dp = mm(value_rows[h, ks, :], grads[h])
                ds = p * (dp - inner[h])
                table_ref[h * KINDS + kind] += ds
                low_ds, low_p = ds.astype(BF16), p.astype(BF16)
                out.append(sums[h] + mm(qkv_ref[k_of[h], ks], low_ds))
                key_acc[h, ks, :] += mm(low_ds, query_rows[h, qs, :])
                value_acc[h, ks, :] += mm(low_p, grad_rows[h, qs, :])
            return tuple(out)

        sums = lax.fori_loop(
            low, high, key_tile, tuple(jnp.zeros((HEAD_DIM, TILE), F32) for _ in range(heads))
        )
        for h in range(heads):
            out_ref[q_of[h], qs] = sums[h].astype(BF16)
        return carry

    lax.fori_loop(0, tiles, query_tile, 0)
    for h in range(heads):
        out_ref[k_of[h], :] = key_acc[h].T.astype(BF16)
        out_ref[v_of[h], :] = value_acc[h].T.astype(BF16)
    for i in range(heads * KINDS):
        if i % KINDS in (0, KINDS - 1):
            total = jnp.sum(table_ref[i], axis=0, keepdims=True)
            diag_ref[i : i + 1, :] = jnp.concatenate([total, jnp.zeros_like(total)], axis=1)
        else:
            diag_ref[i : i + 1, :] = diagonal_sums(table_ref[i])


def attend_back(info, base, qkv, wide, lse, grad, rows_dev):
    rows = qkv.shape[1]
    heads = qkv.shape[0] // (3 * HEAD_DIM)
    cols = heads * HEAD_DIM
    return pl.pallas_call(
        functools.partial(attend_back_kernel, heads, rows_dev),
        out_shape=(
            jax.ShapeDtypeStruct((3 * cols, rows), BF16),
            jax.ShapeDtypeStruct((heads * KINDS, 2 * TILE), F32),
        ),
        in_specs=[SMEM, VMEM, VMEM, VMEM, VMEM, VMEM],
        out_specs=(VMEM, VMEM),
        scratch_shapes=[
            pltpu.VMEM((heads, rows, 2 * HEAD_DIM), BF16),
            pltpu.VMEM((heads, 2 * HEAD_DIM, rows), BF16),
            pltpu.VMEM((heads, rows, HEAD_DIM), BF16),
            pltpu.VMEM((heads, rows, HEAD_DIM), BF16),
            pltpu.VMEM((heads, rows, HEAD_DIM), BF16),
            pltpu.VMEM((heads, rows, HEAD_DIM), F32),
            pltpu.VMEM((heads, rows, HEAD_DIM), F32),
            pltpu.VMEM((heads * KINDS, TILE, TILE), F32),
            pltpu.VMEM((heads * KINDS, TILE, TILE), F32),
        ],
        compiler_params=pltpu.CompilerParams(vmem_limit_bytes=48 << 20),
        cost_estimate=pl.CostEstimate(
            flops=10 * cols * rows * rows, bytes_accessed=4 * cols * rows * 4, transcendentals=heads * rows * rows
        ),
        name="attend_back",
    )(info, base, qkv, wide, lse, grad)


def ffn_kernel(first, hidden, normed_ref, grad_ref, w_ref, hid_ref, pre_ref, own_ref, send_ref):
    half = own_ref.shape[0]
    blocks = normed_ref.shape[0] // TILE
    root, cubic = 0.7978845608028654, 0.044715

    def tile(i, carry):
        rs = pl.ds(pl.multiple_of(lax.rem(i, blocks) * TILE, TILE), TILE)
        js = pl.multiple_of(lax.div(i, blocks) * TILE, TILE)
        a = mm(normed_ref[rs, :], w_ref[:, pl.ds(first + js, TILE)])
        dh = mm(grad_ref[rs, :], w_ref[:, pl.ds(first + hidden + js, TILE)])
        square = a * a
        t = jnp.tanh(root * a * (1.0 + cubic * square))
        cdf = 0.5 * (1.0 + t)
        slope = cdf + 0.5 * a * (1.0 - t * t) * (root * (1.0 + 3.0 * cubic * square))
        hid_ref[rs, pl.ds(js, TILE)] = (a * cdf).astype(BF16)
        pre_ref[rs, pl.ds(js, TILE)] = (dh * slope).astype(BF16)
        return carry

    lax.fori_loop(0, blocks * (hidden // TILE), tile, 0)
    for r in range(blocks):
        back = contract(pre_ref[r * TILE : (r + 1) * TILE, :], 1, w_ref[:, first : first + hidden], 1)
        if r * TILE < half:
            own_ref[r * TILE : (r + 1) * TILE, :] = back
        else:
            send_ref[r * TILE - half : (r + 1) * TILE - half, :] = back.astype(BF16)


def ffn(normed, grad, weights, first, hidden):
    rows, width = normed.shape
    return pl.pallas_call(
        functools.partial(ffn_kernel, first, hidden),
        out_shape=(
            jax.ShapeDtypeStruct((rows, hidden), BF16),
            jax.ShapeDtypeStruct((rows, hidden), BF16),
            jax.ShapeDtypeStruct((rows // 2, width), F32),
            jax.ShapeDtypeStruct((rows // 2, width), BF16),
        ),
        in_specs=[VMEM, VMEM, VMEM],
        out_specs=(VMEM, VMEM, VMEM, VMEM),
        compiler_params=pltpu.CompilerParams(vmem_limit_bytes=40 << 20),
        cost_estimate=pl.CostEstimate(
            flops=6 * rows * width * hidden, bytes_accessed=20 << 20, transcendentals=rows * hidden
        ),
        name="ffn",
    )(normed, grad, weights)


def bias_rows(line):
    heads = line.shape[0]
    pad = 3 * TILE
    rev = jnp.flip(line, axis=1)
    left = jnp.broadcast_to(rev[:, :1], (heads, pad))
    right = jnp.broadcast_to(rev[:, -1:], (heads, pad + 2 * TILE))
    ext = jnp.concatenate([left, rev, right], axis=1)
    begin = [pad + MAXDIST - TILE - TILE * d for d in range(-2, 3)]
    rows = [ext[:, b : b + 2 * TILE] for b in begin]
    return jnp.stack(rows, axis=1).reshape(heads * KINDS, 2 * TILE)


def line_index():
    kind = lax.broadcasted_iota(jnp.int32, (KINDS, 2 * TILE), 0) - 2
    lane = lax.broadcasted_iota(jnp.int32, (KINDS, 2 * TILE), 1)
    near = jnp.clip(TILE + TILE * kind - lane, -MAXDIST, MAXDIST)
    far = jnp.where(kind < 0, -MAXDIST, MAXDIST)
    return (jnp.where(jnp.abs(kind) == 2, far, near) + MAXDIST).reshape(KINDS * 2 * TILE)


def on_device(
    tokens,
    cotangent,
    w_query,
    w_key,
    w_value,
    w_proj,
    w_inner,
    w_outer,
    gain_attn,
    gain_ffn,
    rel_table,
    lengths,
    deal,
    buckets,
):
    rows_dev = tokens.shape[0]
    tensor_size = lax.axis_size("tensor")
    dp_size = lax.axis_size("dp")
    me = lax.axis_index("tensor")
    heads = w_query.shape[1] // HEAD_DIM
    cols = heads * HEAD_DIM
    hidden = w_inner.shape[1]
    width = tokens.shape[1]
    pair = 2 * rows_dev

    def swap(values, bit):
        return lax.ppermute(values, "tensor", [(i, i ^ bit) for i in range(tensor_size)])

    def deal_out(values):
        return lax.all_to_all(values, "dp", split_axis=0, concat_axis=0, tiled=True)

    def total_sum(values):
        for bit in (1, 2):
            values = values + swap(values, bit)
        step = 1
        while step < dp_size:
            values = values + lax.ppermute(values, "dp", [(i, i ^ step) for i in range(dp_size)])
            step *= 2
        return values

    proj_t = w_proj.T.astype(BF16)
    outer_t = w_outer.T.astype(BF16)
    inner = w_inner.astype(BF16)
    own_pack = jnp.concatenate([proj_t, inner, outer_t], axis=1)
    other_pack = swap(own_pack, 2)
    parts = []
    for begin, size in ((0, cols), (cols, hidden), (cols + hidden, hidden)):
        parts += [own_pack[:, begin : begin + size], other_pack[:, begin : begin + size]]
    full_qkv = lax.all_gather(
        jnp.concatenate([w_query, w_key, w_value], axis=1).astype(BF16), "dp", axis=0, tiled=True
    )
    weights = lax.all_gather(jnp.concatenate(parts, axis=1), "dp", axis=0, tiled=True)
    proj_cols = 2 * cols
    full_proj = weights[:, :proj_cols]

    inverse_order = (
        jnp.zeros((rows_dev,), jnp.int32).at[deal].set(jnp.arange(rows_dev, dtype=jnp.int32))
    )
    low_rows = deal_out(jnp.take(tokens, deal, axis=0))
    chosen_grads, low_rows = lax.optimization_barrier((jnp.take(cotangent, deal, axis=0), low_rows))
    low_grads = deal_out(chosen_grads)
    residual = low_rows.astype(F32)

    onehot_buckets = (
        buckets[:, None] == jnp.arange(rel_table.shape[0], dtype=jnp.int32)[None, :]
    ).astype(F32)
    head_table = lax.dynamic_slice_in_dim(rel_table, me * heads, heads, 1)
    offset_bias = jnp.dot(onehot_buckets, head_table, precision=lax.Precision.HIGHEST).T
    base = bias_rows(offset_bias)
    info = jnp.concatenate([lengths, jnp.full((1, 1), me, jnp.int32)], axis=1)

    normed_one, scale_one = row_norm(residual)
    slot0 = (normed_one * gain_attn).astype(BF16)
    slot2 = swap(slot0, 2)
    slot1 = swap(slot0, 1)
    slot3 = swap(slot2, 1)
    gathered_one = jnp.concatenate([slot0, slot1, slot2, slot3], axis=0)
    qkv = contract(full_qkv, 0, gathered_one, 1).astype(BF16)
    mixed, mixed_wide, lse = attend(info, base, qkv, rows_dev)
    mixed_pair = jnp.concatenate([mixed[:, :pair], swap(mixed[:, pair:], 2)], axis=0)
    to_core = contract(mixed_pair[:, rows_dev:], 0, full_proj, 1).astype(BF16)
    from_core = swap(to_core, 1)
    middle = (
        residual + contract(mixed_pair[:, :rows_dev], 0, full_proj, 1) + from_core.astype(F32)
    )

    normed_two, scale_two = row_norm(middle)
    low_two = (normed_two * gain_ffn).astype(BF16)
    pair_two = jnp.concatenate([low_two, swap(low_two, 1)], axis=0)
    pair_grads = jnp.concatenate([low_grads, swap(low_grads, 1)], axis=0)
    hid, pre, back_own, back_send = ffn(pair_two, pair_grads, weights, proj_cols, 2 * hidden)
    grad_two = back_own + swap(back_send, 1).astype(F32)
    grad_mid_norm, gain_two_grad = norm_back(grad_two, normed_two, scale_two, gain_ffn)
    grad_middle = low_grads.astype(F32) + grad_mid_norm
    low_middle = grad_middle.astype(BF16)
    pair_middle = jnp.concatenate([low_middle, swap(low_middle, 1)], axis=0)
    grad_mixed_pair = contract(full_proj, 0, pair_middle, 1).astype(BF16)
    grad_mixed = jnp.concatenate(
        [grad_mixed_pair[:cols], swap(grad_mixed_pair[cols:], 2)], axis=1
    )

    full_outer = weights[:, proj_cols + 2 * hidden :]
    out_send = swap(contract(hid[rows_dev:], 1, full_outer, 1).astype(BF16), 1)
    result_rows = middle + contract(hid[:rows_dev], 1, full_outer, 1) + out_send.astype(F32)
    back_rows = deal_out(result_rows.astype(BF16))

    grad_pack = jnp.concatenate(
        [
            contract(pair_middle, 0, mixed_pair, 1).astype(BF16),
            contract(pair_two, 0, pre, 0).astype(BF16),
            contract(pair_grads, 0, hid, 0).astype(BF16),
        ],
        axis=1,
    )
    shard_pack = lax.psum_scatter(grad_pack, "dp", scatter_dimension=0, tiled=True)
    keep, give, begin = [], [], 0
    for size in (cols, hidden, hidden):
        keep.append(shard_pack[:, begin : begin + size])
        give.append(shard_pack[:, begin + size : begin + 2 * size])
        begin += 2 * size
    keep = jnp.concatenate(keep, axis=1).astype(F32)
    taken = swap(jnp.concatenate(give, axis=1), 2).astype(F32)
    shard_rest = keep + taken

    grad_qkv, diagonals = attend_back(info, base, qkv, mixed_wide, lse, grad_mixed, rows_dev)
    grad_one_slots = [
        contract(grad_qkv[:, s * rows_dev : (s + 1) * rows_dev], 0, full_qkv, 1) for s in range(4)
    ]
    grad_far = grad_one_slots[2] + swap(grad_one_slots[3].astype(BF16), 1).astype(F32)
    grad_near = grad_one_slots[0] + swap(grad_one_slots[1].astype(BF16), 1).astype(F32)
    grad_one = grad_near + swap(grad_far.astype(BF16), 2).astype(F32)
    grad_qkv_w = deal_out(contract(gathered_one, 0, grad_qkv, 1).astype(BF16))
    shard_qkv = jnp.sum(grad_qkv_w.reshape(dp_size, width // dp_size, 3 * cols).astype(F32), axis=0)
    grad_norm_one, gain_one_grad = norm_back(grad_one, normed_one, scale_one, gain_attn)
    grad_rows = grad_middle + grad_norm_one
    back_grads = deal_out(grad_rows.astype(BF16))

    offset_count = 2 * MAXDIST + 1
    onehot_line = (
        line_index()[:, None] == jnp.arange(offset_count, dtype=jnp.int32)[None, :]
    ).astype(F32)
    offset_total = jnp.dot(
        diagonals.reshape(heads, KINDS * 2 * TILE), onehot_line, precision=lax.Precision.HIGHEST
    )
    table_heads = jnp.dot(onehot_buckets.T, offset_total.T, precision=lax.Precision.HIGHEST)
    table_full = lax.dynamic_update_slice_in_dim(
        jnp.zeros(rel_table.shape, F32), table_heads, me * heads, 1
    )
    small = total_sum(
        jnp.concatenate([gain_one_grad, gain_two_grad, table_full.reshape(-1)]).reshape(-1, 128)
    ).reshape(-1)
    return (
        jnp.take(back_rows, inverse_order, axis=0),
        jnp.take(back_grads, inverse_order, axis=0),
        shard_qkv[:, :cols],
        shard_qkv[:, cols : 2 * cols],
        shard_qkv[:, 2 * cols :],
        shard_rest[:, :cols].T,
        shard_rest[:, cols : cols + hidden],
        shard_rest[:, cols + hidden :].T,
        small[:width],
        small[width : 2 * width],
        small[2 * width :].reshape(rel_table.shape),
    )


def solution(mesh):
    rows = P(("dp", "tensor"), None)
    inward, outward = P("dp", "tensor"), P("tensor", "dp")
    weights = (inward, inward, inward, outward, inward, outward)
    return jax.shard_map(
        on_device,
        mesh=mesh,
        in_specs=(rows, rows, *weights, P(), P(), P(), P("dp", None), P(("dp", "tensor")), P()),
        out_specs=(rows, rows, *weights, P(), P(), P()),
        check_vma=False,
    )
```

```python
import functools

import jax
import jax.numpy as jnp
from jax import lax
from jax.experimental import pallas as pl
from jax.experimental.pallas import tpu as pltpu
from jax.sharding import PartitionSpec as P

HEAD_DIM = 64
MAXDIST = 128
TILE = 256
KINDS = 5
EPS = 1e-06
NEG = -1000000000.0
BF16 = jnp.bfloat16
F32 = jnp.float32
VMEM = pl.BlockSpec(memory_space=pltpu.VMEM)
SMEM = pl.BlockSpec(memory_space=pltpu.SMEM)


def cost(microseconds):
    return pl.CostEstimate(
        flops=int(microseconds * 8e8), bytes_accessed=int(microseconds * 2e6), transcendentals=0
    )


def mm(left, right):
    return jnp.dot(left, right, preferred_element_type=F32)


def contract(left, left_dim, right, right_dim):
    return lax.dot_general(
        left, right, (((left_dim,), (right_dim,)), ((), ())), preferred_element_type=F32
    )


def row_norm(values):
    scale = lax.rsqrt(jnp.mean(values * values, axis=-1, keepdims=True) + EPS)
    return (values * scale, scale)


def norm_back(upstream, normed, scale, gain):
    scaled = upstream * gain
    inner = jnp.mean(scaled * normed, axis=-1, keepdims=True)
    return (scale * (scaled - normed * inner), jnp.sum(upstream * normed, axis=0))


def after(*values):
    return lax.optimization_barrier(values)


def ring_order(size):
    return [*range(0, size, 2), *range(size - 1, 0, -2)]


def tile_start(tile, rows_dev, me):
    per_slot = rows_dev // TILE
    return pl.multiple_of((((tile // per_slot) ^ me) * per_slot + tile % per_slot) * TILE, TILE)


def build_bias(base_ref, bias_ref, heads):
    for i in range(heads * KINDS):
        row = base_ref[i : i + 1, :]
        if i % KINDS in (0, KINDS - 1):
            bias_ref[i] = jnp.broadcast_to(row[:, :1], (TILE, TILE))
        else:
            full = jnp.broadcast_to(row, (TILE, 2 * TILE))
            bias_ref[i] = pltpu.roll(full, 0, 1, stride=1, stride_axis=0)[:, TILE:]


def pack_kernel(inner_ref, query_ref, key_ref, value_ref, proj_ref, outer_ref, first_ref, rest_ref):
    hidden = inner_ref.shape[1]
    proj = proj_ref[...].T
    first = [query_ref[...], key_ref[...], value_ref[...], proj]
    first_ref[...] = jnp.concatenate(first, axis=1).astype(BF16)
    rest_ref[:, :hidden] = inner_ref[...].astype(BF16)
    rest_ref[:, hidden : 2 * hidden] = outer_ref[...].T.astype(BF16)
    rest_ref[:, 2 * hidden :] = proj.astype(BF16)


def pack_weights(inner, query, key, value, proj, outer):
    rows, hidden = inner.shape
    cols = query.shape[1]
    return pl.pallas_call(
        pack_kernel,
        out_shape=(
            jax.ShapeDtypeStruct((rows, 4 * cols), BF16),
            jax.ShapeDtypeStruct((rows, 2 * hidden + cols), BF16),
        ),
        in_specs=[VMEM] * 6,
        out_specs=(VMEM, VMEM),
        cost_estimate=cost(2),
        name="pack_weights",
    )(inner, query, key, value, proj, outer)


def unring_kernel(ring, cuts, found_ref, *out_refs):
    size = found_ref.shape[0] // len(ring)
    for p, d in enumerate(ring):
        for cut, out_ref in zip(cuts, out_refs):
            block = found_ref[p * size : (p + 1) * size, cut : cut + out_ref.shape[1]]
            out_ref[d * size : (d + 1) * size, :] = block


def unring(found, ring, widths):
    rows = found.shape[0]
    size = rows // len(ring)
    cuts = [sum(widths[:i]) for i in range(len(widths))]
    if size % 16:
        back = [found[ring.index(d) * size :][:size] for d in range(len(ring))]
        whole = jnp.concatenate(back, axis=0)
        return [whole[:, c : c + w] for c, w in zip(cuts, widths)]
    return pl.pallas_call(
        functools.partial(unring_kernel, ring, cuts),
        out_shape=tuple(jax.ShapeDtypeStruct((rows, w), found.dtype) for w in widths),
        in_specs=[VMEM],
        out_specs=(VMEM,) * len(widths),
        cost_estimate=cost(2),
        name="unring",
    )(found)


def store_ringed(out_ref, ring, begin, end, values):
    size = values.shape[0] // len(ring)
    if size % 16:
        out_ref[:, begin:end] = values
    else:
        for p, d in enumerate(ring):
            out_ref[p * size : (p + 1) * size, begin:end] = values[d * size : (d + 1) * size, :]


def ringed(values, ring):
    size = values.shape[0] // len(ring)
    if size % 16 == 0:
        return values
    return jnp.concatenate([values[d * size :][:size] for d in ring], axis=0)


def segment_rows(width, first_len, start, same, other):
    shape = (HEAD_DIM, width)
    low = start + lax.broadcasted_iota(jnp.int32, shape, 1) < first_len
    row = lax.broadcasted_iota(jnp.int32, shape, 0)
    first = jnp.where(low, same, other)
    second = jnp.where(low, other, same)
    return jnp.where(row == 0, first, jnp.where(row == 1, second, 0.0)).astype(BF16)


def segment_all(rows, rows_dev, first_len, me, same, other):
    slots = rows // rows_dev
    return jnp.concatenate(
        [
            segment_rows(rows_dev, first_len, (s ^ me) * rows_dev, same, other)
            for s in range(slots)
        ],
        axis=1,
    )


def tile_range(tile, first_len, tiles):
    start = tile * TILE
    low = jnp.where(start >= first_len, first_len // TILE, 0)
    high = jnp.where(start + TILE <= first_len, (first_len + TILE - 1) // TILE, tiles)
    return low, high


def over_tiles(low, high, body, carry, sizes=(4, 2, 1)):
    at = low
    for size in sizes:
        count = (high - at) // size

        def step(i, c, at=at, size=size):
            return body(tuple(at + size * i + j for j in range(size)), c)

        carry = lax.fori_loop(0, count, step, carry)
        at = at + size * count
    return carry


def attend_kernel(
    heads,
    rows_dev,
    info_ref,
    base_ref,
    w_ref,
    slot0_ref,
    slot1_ref,
    slot2_ref,
    slot3_ref,
    near_ref,
    far_ref,
    wide_ref,
    lse_ref,
    qkv_ref,
    key_ref,
    score_ref,
    bias_ref,
):
    rows = qkv_ref.shape[1]
    cols = heads * HEAD_DIM
    w_rows = w_ref[:, : 3 * cols].T
    for i, slot_ref in enumerate((slot0_ref, slot1_ref, slot2_ref, slot3_ref)):
        for begin in range(0, rows_dev, TILE):
            part = contract(w_rows, 1, slot_ref[begin : begin + TILE, :], 1)
            at = i * rows_dev + begin
            qkv_ref[:, at : at + TILE] = part.astype(BF16)
    first_len, me = info_ref[0, 0], info_ref[0, 2]
    tiles = rows // TILE
    build_bias(base_ref, bias_ref, heads)
    key_seg = segment_all(rows, rows_dev, first_len, me, 1.0, 0.0)
    for h in range(heads):
        key_ref[h] = jnp.concatenate(
            [qkv_ref[cols + h * HEAD_DIM : cols + (h + 1) * HEAD_DIM, :], key_seg], axis=0
        ).T

    def query_tile(qb, carry):
        qs = pl.ds(tile_start(qb, rows_dev, me), TILE)
        query_seg = segment_rows(TILE, first_len, qb * TILE, 0.0, NEG)
        queries = [
            jnp.concatenate([qkv_ref[h * HEAD_DIM : (h + 1) * HEAD_DIM, qs], query_seg], axis=0)
            for h in range(heads)
        ]
        low, high = tile_range(qb, first_len, tiles)

        def score_tiles(kbs, tops):
            kss = [pl.ds(tile_start(kb, rows_dev, me), TILE) for kb in kbs]
            kinds = [jnp.clip(kb - qb, -2, 2) + 2 for kb in kbs]
            ss = [[mm(key_ref[h, ks, :], queries[h]) for h in range(heads)] for ks in kss]
            tops = list(tops)
            for i, ks in enumerate(kss):
                for h in range(heads):
                    s = ss[i][h] + bias_ref[h * KINDS + kinds[i]]
                    score_ref[h, ks, :] = s
                    tops[h] = jnp.maximum(tops[h], jnp.max(s.reshape(TILE // 8, 8, TILE), axis=0))
            return tuple(tops)

        tops = over_tiles(low, high, score_tiles, (jnp.full((8, TILE), -3e38, F32),) * heads)
        tops = [jnp.max(t, axis=0, keepdims=True) for t in tops]

        def value_tiles(kbs, sums):
            kss = [pl.ds(tile_start(kb, rows_dev, me), TILE) for kb in kbs]
            sums = list(sums)
            ps = []
            for ks in kss:
                for h in range(heads):
                    p = jnp.exp(score_ref[h, ks, :] - tops[h])
                    total, acc = sums[h]
                    sums[h] = (total + jnp.sum(p.reshape(TILE // 8, 8, TILE), axis=0), acc)
                    ps.append(p.astype(BF16))
            for i, ks in enumerate(kss):
                for h in range(heads):
                    values = qkv_ref[2 * cols + h * HEAD_DIM : 2 * cols + (h + 1) * HEAD_DIM, ks]
                    total, acc = sums[h]
                    sums[h] = (total, acc + mm(values, ps[i * heads + h]))
            return tuple(sums)

        zero = (jnp.zeros((8, TILE), F32), jnp.zeros((HEAD_DIM, TILE), F32))
        sums = over_tiles(low, high, value_tiles, (zero,) * heads)
        for h in range(heads):
            total, acc = sums[h]
            total = jnp.sum(total, axis=0, keepdims=True)
            mixed = acc * (1.0 / total)
            hs = slice(h * HEAD_DIM, (h + 1) * HEAD_DIM)
            wide_ref[hs, qs] = mixed
            lse_ref[h : h + 1, qs] = tops[h] + jnp.log(total)
        return carry

    lax.fori_loop(0, tiles, query_tile, 0)
    near_ref[...] = wide_ref[:, : rows // 2].astype(BF16)
    far_ref[...] = wide_ref[:, rows // 2 :].astype(BF16)


def attend(info, base, weights, slots):
    rows_dev = slots[0].shape[0]
    rows = rows_dev * len(slots)
    cols = weights.shape[1] // 4
    heads = cols // HEAD_DIM
    return pl.pallas_call(
        functools.partial(attend_kernel, heads, rows_dev),
        out_shape=(
            jax.ShapeDtypeStruct((cols, rows // 2), BF16),
            jax.ShapeDtypeStruct((cols, rows // 2), BF16),
            jax.ShapeDtypeStruct((cols, rows), F32),
            jax.ShapeDtypeStruct((heads, rows), F32),
            jax.ShapeDtypeStruct((3 * cols, rows), BF16),
        ),
        in_specs=[SMEM] + [VMEM] * 6,
        out_specs=(VMEM,) * 5,
        scratch_shapes=[
            pltpu.VMEM((heads, rows, 2 * HEAD_DIM), BF16),
            pltpu.VMEM((heads, rows, TILE), F32),
            pltpu.VMEM((heads * KINDS, TILE, TILE), F32),
        ],
        compiler_params=pltpu.CompilerParams(vmem_limit_bytes=58 << 20),
        cost_estimate=cost(25),
        name="attend",
    )(info, base, weights, *slots)


def diagonal_sums(values):
    values = jnp.concatenate([jnp.zeros_like(values), values], axis=1)
    count = TILE
    while count > 1:
        count //= 2
        values = values[:count] + pltpu.roll(values[count:], 2 * TILE - count, 1)
    return values


def attend_back_kernel(
    heads,
    rows_dev,
    info_ref,
    base_ref,
    qkv_ref,
    wide_ref,
    lse_ref,
    grad_ref,
    out_ref,
    diag_ref,
    key_ref,
    query_ref,
    value_rows,
    query_rows,
    grad_rows,
    key_acc,
    value_acc,
    bias_ref,
    table_ref,
):
    rows = qkv_ref.shape[1]
    cols = heads * HEAD_DIM
    first_len, me = info_ref[0, 0], info_ref[0, 2]
    tiles = rows // TILE
    build_bias(base_ref, bias_ref, heads)
    key_seg = segment_all(rows, rows_dev, first_len, me, 1.0, 0.0)
    query_seg = segment_all(rows, rows_dev, first_len, me, 0.0, NEG)
    q_of = [slice(h * HEAD_DIM, (h + 1) * HEAD_DIM) for h in range(heads)]
    k_of = [slice(cols + h * HEAD_DIM, cols + (h + 1) * HEAD_DIM) for h in range(heads)]
    v_of = [slice(2 * cols + h * HEAD_DIM, 2 * cols + (h + 1) * HEAD_DIM) for h in range(heads)]
    for h in range(heads):
        queries = qkv_ref[q_of[h], :]
        key_ref[h] = jnp.concatenate([qkv_ref[k_of[h], :], key_seg], axis=0).T
        query_ref[h] = jnp.concatenate([queries, query_seg], axis=0)
        query_rows[h] = queries.T
        value_rows[h] = qkv_ref[v_of[h], :].T
        grad_rows[h] = grad_ref[q_of[h], :].T
    key_acc[...] = jnp.zeros_like(key_acc)
    value_acc[...] = jnp.zeros_like(value_acc)
    table_ref[...] = jnp.zeros_like(table_ref)

    def query_tile(qb, carry):
        qs = pl.ds(tile_start(qb, rows_dev, me), TILE)
        low, high = tile_range(qb, first_len, tiles)
        grads = [grad_ref[q_of[h], qs] for h in range(heads)]
        inner = [
            jnp.sum(grads[h].astype(F32) * wide_ref[q_of[h], qs], axis=0, keepdims=True)
            for h in range(heads)
        ]
        lse = [lse_ref[h : h + 1, qs] for h in range(heads)]

        def tiles_at(kbs, sums):
            kss = [pl.ds(tile_start(kb, rows_dev, me), TILE) for kb in kbs]
            kinds = [jnp.clip(kb - qb, -2, 2) + 2 for kb in kbs]
            ss = [[mm(key_ref[h, ks, :], query_ref[h, :, qs]) for h in range(heads)] for ks in kss]
            dps = [[mm(value_rows[h, ks, :], grads[h]) for h in range(heads)] for ks in kss]
            lows = []
            for i in range(len(kbs)):
                for h in range(heads):
                    p = jnp.exp(ss[i][h] + bias_ref[h * KINDS + kinds[i]] - lse[h])
                    ds = p * (dps[i][h] - inner[h])
                    table_ref[h * KINDS + kinds[i]] += ds
                    lows.append((p.astype(BF16), ds.astype(BF16)))
            sums = list(sums)
            for i, ks in enumerate(kss):
                for h in range(heads):
                    low_p, low_ds = lows[i * heads + h]
                    value_acc[h, ks, :] += mm(low_p, grad_rows[h, qs, :])
                    key_acc[h, ks, :] += mm(low_ds, query_rows[h, qs, :])
                    sums[h] = sums[h] + mm(qkv_ref[k_of[h], ks], low_ds)
            return tuple(sums)

        sums = tuple(jnp.zeros((HEAD_DIM, TILE), F32) for _ in range(heads))
        sums = over_tiles(low, high, tiles_at, sums, (2, 1))
        for h in range(heads):
            out_ref[q_of[h], qs] = sums[h].astype(BF16)
        return carry

    lax.fori_loop(0, tiles, query_tile, 0)
    for h in range(heads):
        out_ref[k_of[h], :] = key_acc[h].astype(BF16).T
        out_ref[v_of[h], :] = value_acc[h].astype(BF16).T
    for i in range(heads * KINDS):
        if i % KINDS in (0, KINDS - 1):
            total = jnp.sum(table_ref[i], axis=0, keepdims=True)
            diag_ref[i : i + 1, :] = jnp.concatenate([total, jnp.zeros_like(total)], axis=1)
        else:
            diag_ref[i : i + 1, :] = diagonal_sums(table_ref[i])


def attend_back(info, base, qkv, wide, lse, grad, rows_dev):
    rows = qkv.shape[1]
    heads = qkv.shape[0] // (3 * HEAD_DIM)
    cols = heads * HEAD_DIM
    return pl.pallas_call(
        functools.partial(attend_back_kernel, heads, rows_dev),
        out_shape=(
            jax.ShapeDtypeStruct((3 * cols, rows), BF16),
            jax.ShapeDtypeStruct((heads * KINDS, 2 * TILE), F32),
        ),
        in_specs=[SMEM, VMEM, VMEM, VMEM, VMEM, VMEM],
        out_specs=(VMEM, VMEM),
        scratch_shapes=[
            pltpu.VMEM((heads, rows, 2 * HEAD_DIM), BF16),
            pltpu.VMEM((heads, 2 * HEAD_DIM, rows), BF16),
            pltpu.VMEM((heads, rows, HEAD_DIM), BF16),
            pltpu.VMEM((heads, rows, HEAD_DIM), BF16),
            pltpu.VMEM((heads, rows, HEAD_DIM), BF16),
            pltpu.VMEM((heads, rows, HEAD_DIM), F32),
            pltpu.VMEM((heads, rows, HEAD_DIM), F32),
            pltpu.VMEM((heads * KINDS, TILE, TILE), F32),
            pltpu.VMEM((heads * KINDS, TILE, TILE), F32),
        ],
        compiler_params=pltpu.CompilerParams(vmem_limit_bytes=58 << 20),
        cost_estimate=cost(45),
        name="attend_back",
    )(info, base, qkv, wide, lse, grad)


def out_proj_kernel(own_ref, other_ref, w_own_ref, w_other_ref, near_ref, send_ref):
    half = near_ref.shape[0]
    for begin in range(0, 2 * half, TILE):
        part = contract(own_ref[:, begin : begin + TILE], 0, w_own_ref[...], 1)
        part = part + contract(other_ref[:, begin : begin + TILE], 0, w_other_ref[...], 1)
        if begin < half:
            near_ref[begin : begin + TILE, :] = part
        else:
            send_ref[begin - half : begin - half + TILE, :] = part.astype(BF16)


def out_proj(own, other, w_own, w_other):
    half, width = own.shape[1] // 2, w_own.shape[0]
    return pl.pallas_call(
        out_proj_kernel,
        out_shape=(
            jax.ShapeDtypeStruct((half, width), F32),
            jax.ShapeDtypeStruct((half, width), BF16),
        ),
        in_specs=[VMEM] * 4,
        out_specs=(VMEM, VMEM),
        cost_estimate=cost(3),
        name="out_proj",
    )(own, other, w_own, w_other)


def mixed_grads_kernel(middle0, middle1, w_own_ref, w_other_ref, own_ref, send_ref):
    half = middle0.shape[0]
    for w_ref, out_ref in ((w_other_ref, send_ref), (w_own_ref, own_ref)):
        w_rows = w_ref[...].T
        for i, middle_ref in enumerate((middle0, middle1)):
            part = contract(w_rows, 1, middle_ref[...], 1)
            out_ref[:, i * half : (i + 1) * half] = part.astype(BF16)


def mixed_grads(middle, w_own, w_other):
    shape = jax.ShapeDtypeStruct((w_own.shape[1], 2 * middle[0].shape[0]), BF16)
    return pl.pallas_call(
        mixed_grads_kernel,
        out_shape=(shape, shape),
        in_specs=[VMEM] * 4,
        out_specs=(VMEM, VMEM),
        cost_estimate=cost(3),
        name="mixed_grads",
    )(*middle, w_own, w_other)


def ffn_kernel(
    normed0,
    normed1,
    grad0,
    grad1,
    front_ref,
    other_ref,
    outer_ref,
    hid_ref,
    pre_ref,
    own_ref,
    send_ref,
    kept_ref,
    acc_ref,
):
    half = own_ref.shape[0]
    step, steps = pl.program_id(0), pl.num_programs(0)
    per_part = kept_ref.shape[1] // TILE
    root, cubic = 0.7978845608028654, 0.044715
    places = [
        (normed_ref, grad_ref, begin, i * half + begin)
        for i, (normed_ref, grad_ref) in enumerate(((normed0, grad0), (normed1, grad1)))
        for begin in range(0, half, TILE)
    ]

    def tile(inner_ref, index):
        js = slice(index * TILE, (index + 1) * TILE)
        firsts = []
        for normed_ref, grad_ref, begin, _ in places:
            rs = slice(begin, begin + TILE)
            a = mm(normed_ref[rs, :], inner_ref[:, js])
            firsts.append((a, mm(grad_ref[rs, :], outer_ref[...])))
        for (a, dh), (_, _, _, at) in zip(firsts, places):
            rs = slice(at, at + TILE)
            square = a * a
            t = jnp.tanh(root * a * (1.0 + cubic * square))
            cdf = 0.5 * (1.0 + t)
            slope = cdf + 0.5 * a * (1.0 - t * t) * (root * (1.0 + 3.0 * cubic * square))
            pre = (dh * slope).astype(BF16)
            hid_ref[rs, :] = (a * cdf).astype(BF16)
            pre_ref[rs, :] = pre
            kept_ref[rs, js] = pre

    for part, inner_ref in enumerate((front_ref, other_ref)):
        for index in range(per_part):

            @pl.when(step == part * per_part + index)
            def _(inner_ref=inner_ref, index=index, part=part):
                tile(inner_ref, index)
                if index < per_part - 1:
                    return
                for _, _, _, at in places:
                    rs = slice(at, at + TILE)
                    back = contract(kept_ref[rs, :], 1, inner_ref[...], 1)
                    if part == 0:
                        acc_ref[rs, :] = back
                    elif at < half:
                        own_ref[rs, :] = acc_ref[rs, :] + back
                    else:
                        low = (acc_ref[rs, :] + back).astype(BF16)
                        send_ref[at - half : at - half + TILE, :] = low


def ffn(normed, grads, front, other_front, outers):
    half, width = normed[0].shape
    rows, hidden = 2 * half, outers.shape[1]
    whole = pl.BlockSpec((half, width), lambda j: (0, 0))
    part = pl.BlockSpec((width, hidden // 2), lambda j: (0, 0))
    return pl.pallas_call(
        ffn_kernel,
        grid=(hidden // TILE,),
        out_shape=(
            jax.ShapeDtypeStruct((rows, hidden), BF16),
            jax.ShapeDtypeStruct((rows, hidden), BF16),
            jax.ShapeDtypeStruct((half, width), F32),
            jax.ShapeDtypeStruct((half, width), BF16),
        ),
        in_specs=[whole] * 4 + [part] * 2 + [pl.BlockSpec((width, TILE), lambda j: (0, j))],
        out_specs=(
            pl.BlockSpec((rows, TILE), lambda j: (0, j)),
            pl.BlockSpec((rows, TILE), lambda j: (0, j)),
            whole,
            whole,
        ),
        scratch_shapes=[pltpu.VMEM((rows, hidden // 2), BF16), pltpu.VMEM((rows, width), F32)],
        compiler_params=pltpu.CompilerParams(vmem_limit_bytes=40 << 20),
        cost_estimate=cost(14),
        name="ffn",
    )(*normed, *grads, front, other_front, outers)


def weight_grads_kernel(
    ring,
    middle0,
    middle1,
    normed0,
    normed1,
    grad0,
    grad1,
    mixed0,
    mixed1,
    own_ref,
    other_ref,
    pre_ref,
    hid_ref,
    out_ref,
    gain_ref,
    left_ref,
    gain_acc,
):
    step = pl.program_id(0)
    half, width = middle0.shape

    def load(first_ref, second_ref):
        left_ref[:, :half] = first_ref[...].T
        left_ref[:, half:] = second_ref[...].T

    def inner(w_ref):
        values = mm(left_ref[...], pre_ref[...])
        store_ringed(out_ref, ring, 0, values.shape[1], values.astype(BF16))
        terms = values * w_ref[...].astype(F32)
        lanes = gain_acc.shape[1]
        parts = [terms[:, b : b + lanes] for b in range(0, values.shape[1], lanes)]
        return functools.reduce(jnp.add, parts)

    @pl.when(step == 0)
    def _():
        load(normed0, normed1)
        gain_acc[...] = inner(own_ref)

    @pl.when(step == 1)
    def _():
        total = gain_acc[...] + inner(other_ref)
        gain_ref[...] = jnp.sum(total.T, axis=0, keepdims=True)

    @pl.when(step == 2)
    def _():
        load(grad0, grad1)

    @pl.when((step == 2) | (step == 3))
    def _():
        values = mm(left_ref[...], hid_ref[...])
        store_ringed(out_ref, ring, 0, values.shape[1], values.astype(BF16))

    @pl.when(step == 4)
    def _():
        load(middle0, middle1)
        both = jnp.concatenate([mixed0[...], mixed1[...]], axis=0)
        values = contract(left_ref[...], 1, both, 1)
        store_ringed(out_ref, ring, 0, values.shape[1], values.astype(BF16))


def weight_grads(ring, middle, normed, grads, mixed, front, other_front, pre, hid):
    half, width = middle[0].shape
    rows, hidden = pre.shape
    cols = mixed[0].shape[0]
    block = hidden // 2
    whole = pl.BlockSpec((half, width), lambda j: (0, 0))
    mix = pl.BlockSpec((cols, rows), lambda j: (0, 0))
    part = pl.BlockSpec((width, block), lambda j: (0, 0))
    return pl.pallas_call(
        functools.partial(weight_grads_kernel, ring),
        grid=(5,),
        out_shape=(
            jax.ShapeDtypeStruct((width, 2 * hidden + 2 * cols), BF16),
            jax.ShapeDtypeStruct((1, width), F32),
        ),
        in_specs=[whole] * 6
        + [mix] * 2
        + [part] * 2
        + [
            pl.BlockSpec((rows, block), lambda j: (0, jnp.minimum(j, 1))),
            pl.BlockSpec((rows, block), lambda j: (0, jnp.clip(j - 2, 0, 1))),
        ],
        out_specs=(
            pl.BlockSpec((width, block), lambda j: (0, j)),
            pl.BlockSpec((1, width), lambda j: (0, 0)),
        ),
        scratch_shapes=[pltpu.VMEM((width, rows), BF16), pltpu.VMEM((width, 128), F32)],
        compiler_params=pltpu.CompilerParams(vmem_limit_bytes=48 << 20),
        cost_estimate=cost(12),
        name="weight_grads",
    )(*middle, *normed, *grads, *mixed, front, other_front, pre, hid)


def grad_rows_kernel(own_slot, send_slot, grad_ref, w_ref, own_ref, send_ref):
    rows_dev = own_ref.shape[0]
    for begin in range(0, rows_dev, TILE):
        at = send_slot * rows_dev + begin
        part = contract(grad_ref[:, at : at + TILE], 0, w_ref[:, : grad_ref.shape[0]], 1)
        send_ref[begin : begin + TILE, :] = part.astype(BF16)
    for begin in range(0, rows_dev, TILE):
        at = own_slot * rows_dev + begin
        own_ref[begin : begin + TILE, :] = contract(grad_ref[:, at : at + TILE], 0, w_ref[:, : grad_ref.shape[0]], 1)


def grad_rows_of(grad_qkv, weights, own_slot, send_slot, rows_dev):
    width = weights.shape[0]
    return pl.pallas_call(
        functools.partial(grad_rows_kernel, own_slot, send_slot),
        out_shape=(
            jax.ShapeDtypeStruct((rows_dev, width), F32),
            jax.ShapeDtypeStruct((rows_dev, width), BF16),
        ),
        in_specs=[VMEM] * 2,
        out_specs=(VMEM,) * 2,
        compiler_params=pltpu.CompilerParams(vmem_limit_bytes=58 << 20),
        cost_estimate=cost(4),
        name="grad_rows",
    )(grad_qkv, weights)


def qkv_grads_kernel(
    ring, grad_ref, slot0_ref, slot1_ref, slot2_ref, slot3_ref, w_ref, out_ref, gain_ref
):
    rows_dev = slot0_ref.shape[0]
    total = 0.0
    for i, slot_ref in enumerate((slot0_ref, slot1_ref, slot2_ref, slot3_ref)):
        total = total + mm(grad_ref[:, i * rows_dev : (i + 1) * rows_dev], slot_ref[...])
    gain_ref[...] = jnp.sum(total * w_ref[:, : total.shape[0]].T.astype(F32), axis=0, keepdims=True)
    store_ringed(out_ref, ring, 0, out_ref.shape[1], total.T.astype(BF16))


def qkv_grads(ring, grad_qkv, slots, weights):
    width = slots[0].shape[1]
    return pl.pallas_call(
        functools.partial(qkv_grads_kernel, ring),
        out_shape=(
            jax.ShapeDtypeStruct((width, grad_qkv.shape[0]), BF16),
            jax.ShapeDtypeStruct((1, width), F32),
        ),
        in_specs=[VMEM] * 6,
        out_specs=(VMEM, VMEM),
        compiler_params=pltpu.CompilerParams(vmem_limit_bytes=58 << 20),
        cost_estimate=cost(5),
        name="qkv_grads",
    )(grad_qkv, *slots, weights)


def bias_rows(line):
    heads = line.shape[0]
    pad = 3 * TILE
    rev = jnp.flip(line, axis=1)
    left = jnp.broadcast_to(rev[:, :1], (heads, pad))
    right = jnp.broadcast_to(rev[:, -1:], (heads, pad + 2 * TILE))
    ext = jnp.concatenate([left, rev, right], axis=1)
    begin = [pad + MAXDIST - TILE - TILE * d for d in range(-2, 3)]
    rows = [ext[:, b : b + 2 * TILE] for b in begin]
    return jnp.stack(rows, axis=1).reshape(heads * KINDS, 2 * TILE)


def line_index():
    kind = lax.broadcasted_iota(jnp.int32, (KINDS, 2 * TILE), 0) - 2
    lane = lax.broadcasted_iota(jnp.int32, (KINDS, 2 * TILE), 1)
    near = jnp.clip(TILE + TILE * kind - lane, -MAXDIST, MAXDIST)
    far = jnp.where(kind < 0, -MAXDIST, MAXDIST)
    return (jnp.where(jnp.abs(kind) == 2, far, near) + MAXDIST).reshape(KINDS * 2 * TILE)


def on_device(
    tokens,
    cotangent,
    w_query,
    w_key,
    w_value,
    w_proj,
    w_inner,
    w_outer,
    gain_attn,
    gain_ffn,
    rel_table,
    lengths,
    deal,
    buckets,
):
    rows_dev = tokens.shape[0]
    tensor_size = lax.axis_size("tensor")
    dp_size = lax.axis_size("dp")
    me = lax.axis_index("tensor")
    heads = w_query.shape[1] // HEAD_DIM
    cols = heads * HEAD_DIM
    hidden = w_inner.shape[1]
    width = tokens.shape[1]
    pair = 2 * rows_dev

    def swap(values, bit):
        return lax.ppermute(values, "tensor", [(i, i ^ bit) for i in range(tensor_size)])

    def deal_out(values):
        return lax.all_to_all(values, "dp", split_axis=0, concat_axis=0, tiled=True)

    def pick(values, order):
        return values.at[order].get(mode="promise_in_bounds", unique_indices=True)

    def total_sum(values):
        for bit in (1, 2):
            values = values + swap(values, bit)
        step = 1
        while step < dp_size:
            values = values + lax.ppermute(values, "dp", [(i, i ^ step) for i in range(dp_size)])
            step *= 2
        return values

    ring = ring_order(dp_size)
    both = ("dp", "tensor")
    ring_groups = [[d * tensor_size + t for d in ring] for t in range(tensor_size)]

    def gather(values, widths):
        found = lax.all_gather(values, both, axis=0, tiled=True, axis_index_groups=ring_groups)
        return unring(found, ring, widths)

    def scatter_sum(values):
        return lax.psum_scatter(
            ringed(values, ring), both, scatter_dimension=0, tiled=True, axis_index_groups=ring_groups
        )

    own_front, own_rest = pack_weights(w_inner, w_query, w_key, w_value, w_proj, w_outer)
    (front,) = gather(own_front, (4 * cols,))
    tokens, _ = after(tokens, own_front)
    chosen_rows = pick(tokens, deal)
    low_rows = deal_out(chosen_rows)
    early_rest, _ = after(own_rest, chosen_rows)
    other_rest = swap(early_rest, 2)
    rest = [
        part
        for begin in (0, hidden)
        for part in (own_rest[:, begin : begin + hidden], other_rest[:, begin : begin + hidden])
    ]
    inner_own, inner_other, outers, proj_other = gather(
        jnp.concatenate([*rest, other_rest[:, 2 * hidden :]], axis=1),
        (hidden, hidden, 2 * hidden, cols),
    )
    inverse_order = (
        jnp.zeros((rows_dev,), jnp.int32).at[deal].set(jnp.arange(rows_dev, dtype=jnp.int32))
    )
    chosen_grads = pick(cotangent, deal)
    low_rows, inverse_order, chosen_grads = after(low_rows, inverse_order, chosen_grads)
    residual = low_rows.astype(F32)
    normed_one, scale_one = row_norm(residual)
    slot0 = (normed_one * gain_attn).astype(BF16)
    slot2 = swap(slot0, 2)
    slot1 = swap(slot0, 1)
    slot3 = swap(slot2, 1)
    slots = (slot0, slot1, slot2, slot3)
    chosen_grads, _ = after(chosen_grads, slot0)
    low_grads = deal_out(chosen_grads)
    proj_own = front[:, 3 * cols :]

    onehot_buckets = (
        buckets[:, None] == jnp.arange(rel_table.shape[0], dtype=jnp.int32)[None, :]
    ).astype(F32)
    head_table = lax.dynamic_slice_in_dim(rel_table, me * heads, heads, 1)
    offset_bias = jnp.dot(onehot_buckets, head_table, precision=lax.Precision.HIGHEST).T
    base = bias_rows(offset_bias)
    info = jnp.concatenate([lengths, jnp.full((1, 1), me, jnp.int32)], axis=1)

    mixed_own, mixed_far, mixed_wide, lse, qkv = attend(info, base, front, slots)
    mixed_other = swap(mixed_far, 2)
    near, to_core = out_proj(mixed_own, mixed_other, proj_own, proj_other)
    middle = residual + near + swap(to_core, 1).astype(F32)

    normed_two, scale_two = row_norm(middle)
    low_two = (normed_two * gain_ffn).astype(BF16)
    pair_two = (low_two, swap(low_two, 1))
    pair_grads = (low_grads, swap(low_grads, 1))
    hid, pre, back_own, back_send = ffn(pair_two, pair_grads, inner_own, inner_other, outers)
    grad_two = back_own + swap(back_send, 1).astype(F32)
    grad_mid_norm, _ = norm_back(grad_two, normed_two, scale_two, gain_ffn)
    grad_middle = low_grads.astype(F32) + grad_mid_norm
    low_middle = grad_middle.astype(BF16)
    pair_middle = (low_middle, swap(low_middle, 1))
    grad_own, to_other = mixed_grads(pair_middle, proj_own, proj_other)
    grad_mixed = jnp.concatenate([grad_own, swap(to_other, 2)], axis=1)

    out_send = swap(contract(hid[rows_dev:], 1, outers, 1).astype(BF16), 1)
    result_rows = middle + contract(hid[:rows_dev], 1, outers, 1) + out_send.astype(F32)
    back_rows = deal_out(result_rows.astype(BF16))

    pair_hid, _ = after(hid, to_other)
    grad_pack, gain_two = weight_grads(
        ring,
        pair_middle,
        pair_two,
        pair_grads,
        (mixed_own, mixed_other),
        inner_own,
        inner_other,
        pre,
        pair_hid,
    )
    shard_pack = scatter_sum(grad_pack)
    keep, give, begin = [], [], 0
    for size in (hidden, hidden, cols):
        keep.append(shard_pack[:, begin : begin + size])
        give.append(shard_pack[:, begin + size : begin + 2 * size])
        begin += 2 * size
    keep = jnp.concatenate(keep, axis=1).astype(F32)
    taken = swap(jnp.concatenate(give, axis=1), 2)

    grad_mixed, _ = after(grad_mixed, grad_pack)
    grad_qkv, diagonals = attend_back(info, base, qkv, mixed_wide, lse, grad_mixed, rows_dev)
    grad_qkv, back_rows = after(grad_qkv, back_rows)
    far_own, far_send = grad_rows_of(grad_qkv, front, 2, 3, rows_dev)
    grad_far = (far_own + swap(far_send, 1).astype(F32)).astype(BF16)
    later_qkv, _ = after(grad_qkv, grad_far)
    near_own, near_send = grad_rows_of(later_qkv, front, 0, 1, rows_dev)
    low_qkv_w, gain_one = qkv_grads(ring, later_qkv, slots, front)
    shard_qkv = scatter_sum(low_qkv_w).astype(F32)
    grad_one = near_own + swap(near_send, 1).astype(F32) + swap(grad_far, 2).astype(F32)
    grad_norm_one, _ = norm_back(grad_one, normed_one, scale_one, gain_attn)
    low_grad_rows = (grad_middle + grad_norm_one).astype(BF16)

    offset_count = 2 * MAXDIST + 1
    onehot_line = (
        line_index()[:, None] == jnp.arange(offset_count, dtype=jnp.int32)[None, :]
    ).astype(F32)
    offset_total = jnp.dot(
        diagonals.reshape(heads, KINDS * 2 * TILE), onehot_line, precision=lax.Precision.HIGHEST
    )
    table_heads = jnp.dot(onehot_buckets.T, offset_total.T, precision=lax.Precision.HIGHEST)
    table_full = lax.dynamic_update_slice_in_dim(
        jnp.zeros(rel_table.shape, F32), table_heads, me * heads, 1
    )
    small = total_sum(
        jnp.concatenate(
            [gain_one[0] / gain_attn, gain_two[0] / gain_ffn, table_full.reshape(-1)]
        ).reshape(-1, 128)
    ).reshape(-1)
    low_grad_rows, small, taken = after(low_grad_rows, small, taken)
    back_grads = deal_out(low_grad_rows)
    shard_rest = keep + taken.astype(F32)
    return (
        pick(back_rows, inverse_order),
        pick(back_grads, inverse_order),
        shard_qkv[:, :cols],
        shard_qkv[:, cols : 2 * cols],
        shard_qkv[:, 2 * cols :],
        shard_rest[:, 2 * hidden :].T,
        shard_rest[:, :hidden],
        shard_rest[:, hidden : 2 * hidden].T,
        small[:width],
        small[width : 2 * width],
        small[2 * width :].reshape(rel_table.shape),
    )


def solution(mesh):
    rows = P(("dp", "tensor"), None)
    inward, outward = P("dp", "tensor"), P("tensor", "dp")
    weights = (inward, inward, inward, outward, inward, outward)
    return jax.shard_map(
        on_device,
        mesh=mesh,
        in_specs=(rows, rows, *weights, P(), P(), P(), P("dp", None), P(("dp", "tensor")), P()),
        out_specs=(rows, rows, *weights, P(), P(), P()),
        check_vma=False,
    )
```

```python
import functools

import jax
import jax.numpy as jnp
from jax import lax
from jax.experimental import pallas as pl
from jax.experimental.pallas import tpu as pltpu
from jax.sharding import PartitionSpec as P

HEAD_DIM = 64
MAXDIST = 128
TILE = 256
KINDS = 5
EPS = 1e-06
NEG = -1000000000.0
BF16 = jnp.bfloat16
F32 = jnp.float32
VMEM = pl.BlockSpec(memory_space=pltpu.VMEM)
SMEM = pl.BlockSpec(memory_space=pltpu.SMEM)


SHORT = pl.CostEstimate(flops=1 << 20, bytes_accessed=1 << 16, transcendentals=0)


LONG = pl.CostEstimate(flops=3 << 33, bytes_accessed=1 << 26, transcendentals=1 << 23)


def mm(left, right):
    return jnp.dot(left, right, preferred_element_type=F32)


def contract(left, left_dim, right, right_dim):
    return lax.dot_general(
        left, right, (((left_dim,), (right_dim,)), ((), ())), preferred_element_type=F32
    )


def after(*values):
    return lax.optimization_barrier(values)


def ring_order(size):
    return [*range(0, size, 2), *range(size - 1, 0, -2)]


def tile_start(tile, rows_dev, me):
    per_slot = rows_dev // TILE
    return pl.multiple_of((((tile // per_slot) ^ me) * per_slot + tile % per_slot) * TILE, TILE)


def build_bias(base_ref, bias_ref, heads):
    for i in range(heads * KINDS):
        row = base_ref[i : i + 1, :]
        if i % KINDS in (0, KINDS - 1):
            bias_ref[i] = jnp.broadcast_to(row[:, :1], (TILE, TILE))
        else:
            full = jnp.broadcast_to(row, (TILE, 2 * TILE))
            bias_ref[i] = pltpu.roll(full, 0, 1, stride=1, stride_axis=0)[:, TILE:]


def pack_kernel(inner_ref, query_ref, key_ref, value_ref, proj_ref, outer_ref, first_ref, rest_ref):
    hidden = inner_ref.shape[1]
    first = [query_ref[...], key_ref[...], value_ref[...], outer_ref[...], proj_ref[...]]
    first_ref[...] = jnp.concatenate(first, axis=1).astype(BF16)
    rest_ref[...] = inner_ref[...].astype(BF16)


def pack_weights(inner, query, key, value, proj, outer):
    rows, hidden = inner.shape
    cols = query.shape[1]
    return pl.pallas_call(
        pack_kernel,
        out_shape=(
            jax.ShapeDtypeStruct((rows, 4 * cols + hidden), BF16),
            jax.ShapeDtypeStruct((rows, hidden), BF16),
        ),
        in_specs=[VMEM] * 6,
        out_specs=(VMEM, VMEM),
        cost_estimate=SHORT,
        name="pack_weights",
    )(inner, query, key, value, proj, outer)


def unring_kernel(ring, spans, found_ref, *out_refs):
    size = found_ref.shape[0] // len(ring)
    for (begin, end, turned), out_ref in zip(spans, out_refs):
        if turned:
            blocks = [
                found_ref[ring.index(d) * size : (ring.index(d) + 1) * size, begin:end]
                for d in range(len(ring))
            ]
            out_ref[...] = jnp.concatenate(blocks, axis=0).T
        else:
            for p, d in enumerate(ring):
                block = found_ref[p * size : (p + 1) * size, begin:end]
                out_ref[d * size : (d + 1) * size, :] = block


def unring(found, ring, spans):
    rows = found.shape[0]
    size = rows // len(ring)
    if size % 16:
        back = [found[ring.index(d) * size :][:size] for d in range(len(ring))]
        whole = jnp.concatenate(back, axis=0)
        parts = [whole[:, begin:end] for begin, end, _ in spans]
        return [part.T if span[2] else part for part, span in zip(parts, spans)]
    shapes = [(end - begin, rows) if turned else (rows, end - begin) for begin, end, turned in spans]
    return pl.pallas_call(
        functools.partial(unring_kernel, ring, spans),
        out_shape=tuple(jax.ShapeDtypeStruct(shape, found.dtype) for shape in shapes),
        in_specs=[VMEM],
        out_specs=(VMEM,) * len(spans),
        cost_estimate=SHORT,
        name="unring",
    )(found)


def store_ringed(out_ref, ring, begin, end, values):
    size = values.shape[0] // len(ring)
    if size % 16:
        out_ref[:, begin:end] = values
    else:
        for p, d in enumerate(ring):
            out_ref[p * size : (p + 1) * size, begin:end] = values[d * size : (d + 1) * size, :]


def ringed(values, ring):
    size = values.shape[0] // len(ring)
    if size % 16 == 0:
        return values
    return jnp.concatenate([values[d * size :][:size] for d in ring], axis=0)


def segment_rows(width, first_len, start, same, other):
    shape = (HEAD_DIM, width)
    low = start + lax.broadcasted_iota(jnp.int32, shape, 1) < first_len
    row = lax.broadcasted_iota(jnp.int32, shape, 0)
    first = jnp.where(low, same, other)
    second = jnp.where(low, other, same)
    return jnp.where(row == 0, first, jnp.where(row == 1, second, 0.0)).astype(BF16)


def segment_all(rows, rows_dev, first_len, me, same, other):
    slots = rows // rows_dev
    return jnp.concatenate(
        [
            segment_rows(rows_dev, first_len, (s ^ me) * rows_dev, same, other)
            for s in range(slots)
        ],
        axis=1,
    )


def tile_range(tile, first_len, tiles):
    start = tile * TILE
    low = jnp.where(start >= first_len, first_len // TILE, 0)
    high = jnp.where(start + TILE <= first_len, (first_len + TILE - 1) // TILE, tiles)
    return low, high


def over_tiles(low, high, body, carry, sizes=(4, 2, 1)):
    at = low
    for size in sizes:
        count = (high - at) // size

        def step(i, c, at=at, size=size):
            return body(tuple(at + size * i + j for j in range(size)), c)

        carry = lax.fori_loop(0, count, step, carry)
        at = at + size * count
    return carry


def attend_rows(
    heads, rows_dev, first_slot, info_ref, qkv_ref, key_ref, out_ref, wide_ref, lse_ref, score_ref, bias_ref
):
    rows = qkv_ref.shape[1]
    cols = heads * HEAD_DIM
    first_len, me = info_ref[0, 0], info_ref[0, 2]
    tiles = rows // TILE
    per_slot = rows_dev // TILE

    def query_tile(i, carry):
        qb = ((first_slot + i // per_slot) ^ me) * per_slot + i % per_slot
        qs = pl.ds(pl.multiple_of(first_slot * rows_dev + i * TILE, TILE), TILE)
        at = pl.ds(pl.multiple_of(i * TILE, TILE), TILE)
        query_seg = segment_rows(TILE, first_len, qb * TILE, 0.0, NEG)
        queries = [
            jnp.concatenate([qkv_ref[h * HEAD_DIM : (h + 1) * HEAD_DIM, qs], query_seg], axis=0)
            for h in range(heads)
        ]
        low, high = tile_range(qb, first_len, tiles)

        def score_tiles(kbs, tops):
            kss = [pl.ds(tile_start(kb, rows_dev, me), TILE) for kb in kbs]
            kinds = [jnp.clip(kb - qb, -2, 2) + 2 for kb in kbs]
            ss = [[mm(key_ref[h, ks, :], queries[h]) for h in range(heads)] for ks in kss]
            tops = list(tops)
            for i, ks in enumerate(kss):
                for h in range(heads):
                    s = ss[i][h] + bias_ref[h * KINDS + kinds[i]]
                    score_ref[h, ks, :] = s
                    tops[h] = jnp.maximum(tops[h], jnp.max(s.reshape(TILE // 8, 8, TILE), axis=0))
            return tuple(tops)

        tops = over_tiles(low, high, score_tiles, (jnp.full((8, TILE), -3e38, F32),) * heads)
        tops = [jnp.max(t, axis=0, keepdims=True) for t in tops]

        def value_tiles(kbs, sums):
            kss = [pl.ds(tile_start(kb, rows_dev, me), TILE) for kb in kbs]
            sums = list(sums)
            ps = []
            for ks in kss:
                for h in range(heads):
                    p = jnp.exp(score_ref[h, ks, :] - tops[h])
                    total, acc = sums[h]
                    sums[h] = (total + jnp.sum(p.reshape(TILE // 8, 8, TILE), axis=0), acc)
                    ps.append(p.astype(BF16))
            for i, ks in enumerate(kss):
                for h in range(heads):
                    values = qkv_ref[2 * cols + h * HEAD_DIM : 2 * cols + (h + 1) * HEAD_DIM, ks]
                    total, acc = sums[h]
                    sums[h] = (total, acc + mm(values, ps[i * heads + h]))
            return tuple(sums)

        zero = (jnp.zeros((8, TILE), F32), jnp.zeros((HEAD_DIM, TILE), F32))
        sums = over_tiles(low, high, value_tiles, (zero,) * heads)
        for h in range(heads):
            total, acc = sums[h]
            total = jnp.sum(total, axis=0, keepdims=True)
            mixed = acc * (1.0 / total)
            hs = slice(h * HEAD_DIM, (h + 1) * HEAD_DIM)
            wide_ref[hs, at] = mixed
            out_ref[hs, at] = mixed.astype(BF16)
            lse_ref[h : h + 1, at] = tops[h] + jnp.log(total)
        return carry

    lax.fori_loop(0, tiles // 2, query_tile, 0)


def attend_far_kernel(
    heads,
    rows_dev,
    info_ref,
    base_ref,
    w_ref,
    slot0_ref,
    slot1_ref,
    slot2_ref,
    slot3_ref,
    out_ref,
    wide_ref,
    lse_ref,
    qkv_ref,
    key_ref,
    score_ref,
    bias_ref,
):
    rows = qkv_ref.shape[1]
    cols = heads * HEAD_DIM
    w_rows = w_ref[:, : 3 * cols].T
    for i, slot_ref in enumerate((slot0_ref, slot1_ref, slot2_ref, slot3_ref)):
        for begin in range(0, rows_dev, TILE):
            part = contract(w_rows, 1, slot_ref[begin : begin + TILE, :], 1)
            at = i * rows_dev + begin
            qkv_ref[:, at : at + TILE] = part.astype(BF16)
    build_bias(base_ref, bias_ref, heads)
    key_seg = segment_all(rows, rows_dev, info_ref[0, 0], info_ref[0, 2], 1.0, 0.0)
    for h in range(heads):
        key_ref[h] = jnp.concatenate(
            [qkv_ref[cols + h * HEAD_DIM : cols + (h + 1) * HEAD_DIM, :], key_seg], axis=0
        ).T
    far = rows // rows_dev // 2
    attend_rows(
        heads, rows_dev, far, info_ref, qkv_ref, key_ref, out_ref, wide_ref, lse_ref, score_ref, bias_ref
    )


def attend_near_kernel(
    heads, rows_dev, info_ref, base_ref, qkv_ref, key_ref, out_ref, wide_ref, lse_ref, score_ref, bias_ref
):
    build_bias(base_ref, bias_ref, heads)
    attend_rows(
        heads, rows_dev, 0, info_ref, qkv_ref, key_ref, out_ref, wide_ref, lse_ref, score_ref, bias_ref
    )


def attend_shapes(heads, rows):
    cols = heads * HEAD_DIM
    return (
        jax.ShapeDtypeStruct((cols, rows // 2), BF16),
        jax.ShapeDtypeStruct((cols, rows // 2), F32),
        jax.ShapeDtypeStruct((heads, rows // 2), F32),
    )


def attend_scratch(heads, rows):
    return [
        pltpu.VMEM((heads, rows, TILE), F32),
        pltpu.VMEM((heads * KINDS, TILE, TILE), F32),
    ]


def attend_far(info, base, weights, slots):
    rows_dev = slots[0].shape[0]
    rows = rows_dev * len(slots)
    cols = weights.shape[1] // 3
    heads = cols // HEAD_DIM
    return pl.pallas_call(
        functools.partial(attend_far_kernel, heads, rows_dev),
        out_shape=attend_shapes(heads, rows)
        + (
            jax.ShapeDtypeStruct((3 * cols, rows), BF16),
            jax.ShapeDtypeStruct((heads, rows, 2 * HEAD_DIM), BF16),
        ),
        in_specs=[SMEM] + [VMEM] * 6,
        out_specs=(VMEM,) * 5,
        scratch_shapes=attend_scratch(heads, rows),
        compiler_params=pltpu.CompilerParams(vmem_limit_bytes=58 << 20),
        cost_estimate=SHORT,
        name="attend_far",
    )(info, base, weights, *slots)


def attend_near(info, base, qkv, keys, rows_dev):
    heads, rows = keys.shape[:2]
    return pl.pallas_call(
        functools.partial(attend_near_kernel, heads, rows_dev),
        out_shape=attend_shapes(heads, rows),
        in_specs=[SMEM] + [VMEM] * 3,
        out_specs=(VMEM,) * 3,
        scratch_shapes=attend_scratch(heads, rows),
        compiler_params=pltpu.CompilerParams(vmem_limit_bytes=58 << 20),
        cost_estimate=SHORT,
        name="attend_near",
    )(info, base, qkv, keys)


def diagonal_sums(values):
    values = jnp.concatenate([jnp.zeros_like(values), values], axis=1)
    count = TILE
    while count > 1:
        count //= 2
        values = values[:count] + pltpu.roll(values[count:], 2 * TILE - count, 1)
    return values


def grad_rows_to(own_ref, send_ref, rows_dev, grad_ref, w_ref):
    slots = grad_ref.shape[1] // rows_dev
    for i in range(slots // 2):
        slot = (slots - 2 * (i + 1)) % slots
        for at, out_ref in ((slot + 1, send_ref), (slot, own_ref)):
            for begin in range(0, rows_dev, TILE):
                cols = slice(at * rows_dev + begin, at * rows_dev + begin + TILE)
                part = contract(grad_ref[:, cols], 0, w_ref[...], 1)
                to = slice(i * rows_dev + begin, i * rows_dev + begin + TILE)
                out_ref[to, :] = part.astype(out_ref.dtype)


def attend_back_kernel(
    heads,
    rows_dev,
    info_ref,
    base_ref,
    qkv_ref,
    key_ref,
    wide0_ref,
    wide1_ref,
    lse0_ref,
    lse1_ref,
    grad0_ref,
    grad1_ref,
    w_ref,
    out_ref,
    diag_ref,
    own_ref,
    send_ref,
    lse_ref,
    inner_ref,
    grad_ref,
    query_ref,
    value_rows,
    query_rows,
    grad_rows,
    key_acc,
    value_acc,
    bias_ref,
    table_ref,
):
    rows = qkv_ref.shape[1]
    cols = heads * HEAD_DIM
    first_len, me = info_ref[0, 0], info_ref[0, 2]
    tiles = rows // TILE
    build_bias(base_ref, bias_ref, heads)
    query_seg = segment_all(rows, rows_dev, first_len, me, 0.0, NEG)
    q_of = [slice(h * HEAD_DIM, (h + 1) * HEAD_DIM) for h in range(heads)]
    k_of = [slice(cols + h * HEAD_DIM, cols + (h + 1) * HEAD_DIM) for h in range(heads)]
    v_of = [slice(2 * cols + h * HEAD_DIM, 2 * cols + (h + 1) * HEAD_DIM) for h in range(heads)]
    lse_ref[:, : rows // 2] = lse0_ref[...]
    lse_ref[:, rows // 2 :] = lse1_ref[...]
    grad_ref[:, : rows // 2] = grad0_ref[...]
    grad_ref[:, rows // 2 :] = grad1_ref[...]
    for h in range(heads):
        queries = qkv_ref[q_of[h], :]
        query_ref[h] = jnp.concatenate([queries, query_seg], axis=0)
        query_rows[h] = queries.T
        value_rows[h] = qkv_ref[v_of[h], :].T
        grad_rows[h] = grad_ref[q_of[h], :].T
        for half, wide_ref in ((0, wide0_ref), (1, wide1_ref)):
            at = slice(half * rows // 2, (half + 1) * rows // 2)
            terms = grad_ref[q_of[h], at].astype(F32) * wide_ref[q_of[h], :]
            inner_ref[h : h + 1, at] = jnp.sum(terms, axis=0, keepdims=True)
    key_acc[...] = jnp.zeros_like(key_acc)
    value_acc[...] = jnp.zeros_like(value_acc)
    table_ref[...] = jnp.zeros_like(table_ref)

    def query_tile(qb, carry):
        qs = pl.ds(tile_start(qb, rows_dev, me), TILE)
        low, high = tile_range(qb, first_len, tiles)
        grads = [grad_ref[q_of[h], qs] for h in range(heads)]
        inner = [inner_ref[h : h + 1, qs] for h in range(heads)]
        lse = [lse_ref[h : h + 1, qs] for h in range(heads)]

        def tiles_at(kbs, sums):
            kss = [pl.ds(tile_start(kb, rows_dev, me), TILE) for kb in kbs]
            kinds = [jnp.clip(kb - qb, -2, 2) + 2 for kb in kbs]
            ss = [[mm(key_ref[h, ks, :], query_ref[h, :, qs]) for h in range(heads)] for ks in kss]
            dps = [[mm(value_rows[h, ks, :], grads[h]) for h in range(heads)] for ks in kss]
            lows = []
            for i in range(len(kbs)):
                for h in range(heads):
                    p = jnp.exp(ss[i][h] + bias_ref[h * KINDS + kinds[i]] - lse[h])
                    ds = p * (dps[i][h] - inner[h])
                    table_ref[h * KINDS + kinds[i]] += ds
                    lows.append((p.astype(BF16), ds.astype(BF16)))
            sums = list(sums)
            for i, ks in enumerate(kss):
                for h in range(heads):
                    low_p, low_ds = lows[i * heads + h]
                    value_acc[h, ks, :] += mm(low_p, grad_rows[h, qs, :])
                    key_acc[h, ks, :] += mm(low_ds, query_rows[h, qs, :])
                    sums[h] = sums[h] + mm(qkv_ref[k_of[h], ks], low_ds)
            return tuple(sums)

        sums = tuple(jnp.zeros((HEAD_DIM, TILE), F32) for _ in range(heads))
        sums = over_tiles(low, high, tiles_at, sums, (2, 1))
        for h in range(heads):
            out_ref[q_of[h], qs] = sums[h].astype(BF16)
        return carry

    lax.fori_loop(0, tiles, query_tile, 0)
    for h in range(heads):
        out_ref[k_of[h], :] = key_acc[h].astype(BF16).T
        out_ref[v_of[h], :] = value_acc[h].astype(BF16).T
    grad_rows_to(own_ref, send_ref, rows_dev, out_ref, w_ref)
    for i in range(heads * KINDS):
        if i % KINDS in (0, KINDS - 1):
            total = jnp.sum(table_ref[i], axis=0, keepdims=True)
            diag_ref[i : i + 1, :] = jnp.concatenate([total, jnp.zeros_like(total)], axis=1)
        else:
            diag_ref[i : i + 1, :] = diagonal_sums(table_ref[i])


def attend_back(info, base, qkv, keys, wide, lse, grad, weights, rows_dev):
    rows = qkv.shape[1]
    width = weights.shape[0]
    heads = qkv.shape[0] // (3 * HEAD_DIM)
    cols = heads * HEAD_DIM
    return pl.pallas_call(
        functools.partial(attend_back_kernel, heads, rows_dev),
        out_shape=(
            jax.ShapeDtypeStruct((3 * cols, rows), BF16),
            jax.ShapeDtypeStruct((heads * KINDS, 2 * TILE), F32),
            jax.ShapeDtypeStruct((rows // 2, width), F32),
            jax.ShapeDtypeStruct((rows // 2, width), BF16),
        ),
        in_specs=[SMEM] + [VMEM] * 10,
        out_specs=(VMEM,) * 4,
        scratch_shapes=[
            pltpu.VMEM((heads, rows), F32),
            pltpu.VMEM((heads, rows), F32),
            pltpu.VMEM((cols, rows), BF16),
            pltpu.VMEM((heads, 2 * HEAD_DIM, rows), BF16),
            pltpu.VMEM((heads, rows, HEAD_DIM), BF16),
            pltpu.VMEM((heads, rows, HEAD_DIM), BF16),
            pltpu.VMEM((heads, rows, HEAD_DIM), BF16),
            pltpu.VMEM((heads, rows, HEAD_DIM), F32),
            pltpu.VMEM((heads, rows, HEAD_DIM), F32),
            pltpu.VMEM((heads * KINDS, TILE, TILE), F32),
            pltpu.VMEM((heads * KINDS, TILE, TILE), F32),
        ],
        compiler_params=pltpu.CompilerParams(vmem_limit_bytes=58 << 20),
        cost_estimate=LONG,
        name="attend_back",
    )(info, base, qkv, keys, *wide, *lse, *grad, weights)


def scaled_rows(values):
    return values * lax.rsqrt(jnp.mean(values * values, axis=-1, keepdims=True) + EPS)


def join_kernel(rows_ref, near_ref, far_ref, gain_ref, middle_ref, low_ref):
    middle = rows_ref[...].astype(F32) + near_ref[...] + far_ref[...].astype(F32)
    middle_ref[...] = middle
    low_ref[...] = (scaled_rows(middle) * gain_ref[...]).astype(BF16)


def norm_back_rows(values, upstream, gain):
    scale = lax.rsqrt(jnp.mean(values * values, axis=-1, keepdims=True) + EPS)
    normed = values * scale
    scaled = upstream * gain
    inner = jnp.mean(scaled * normed, axis=-1, keepdims=True)
    return scale * (scaled - normed * inner)


def middle_back_kernel(middle_ref, near_ref, far_ref, grads_ref, gain_ref, wide_ref, low_ref):
    upstream = near_ref[...] + far_ref[...].astype(F32)
    back = norm_back_rows(middle_ref[...], upstream, gain_ref[...])
    wide = grads_ref[...].astype(F32) + back
    wide_ref[...] = wide
    low_ref[...] = wide.astype(BF16)


def rows_back_kernel(rows_ref, near_ref, core_ref, far_ref, wide_ref, gain_ref, low_ref):
    upstream = near_ref[...] + core_ref[...].astype(F32) + far_ref[...].astype(F32)
    back = norm_back_rows(rows_ref[...].astype(F32), upstream, gain_ref[...])
    low_ref[...] = (wide_ref[...] + back).astype(BF16)


def by_rows(kernel, name, gain, *operands, out, cost=SHORT):
    rows, width = operands[0].shape
    spec = pl.BlockSpec((TILE, width), lambda i: (i, 0))
    once = pl.BlockSpec((1, width), lambda i: (0, 0))
    return pl.pallas_call(
        kernel,
        grid=(rows // TILE,),
        out_shape=tuple(jax.ShapeDtypeStruct((rows, width), kind) for kind in out),
        in_specs=[spec] * len(operands) + [once],
        out_specs=(spec,) * len(out),
        compiler_params=pltpu.CompilerParams(vmem_limit_bytes=58 << 20),
        cost_estimate=cost,
        name=name,
    )(*operands, gain[None])


def out_proj_kernel(own_ref, other_ref, w_own_ref, w_other_ref, near_ref, send_ref):
    half = near_ref.shape[0]
    for begin in range(0, 2 * half, TILE):
        part = contract(own_ref[:, begin : begin + TILE], 0, w_own_ref[...], 0)
        part = part + contract(other_ref[:, begin : begin + TILE], 0, w_other_ref[...], 0)
        if begin < half:
            near_ref[begin : begin + TILE, :] = part
        else:
            send_ref[begin - half : begin - half + TILE, :] = part.astype(BF16)


def out_proj(own, other, w_own, w_other):
    half, width = own.shape[1] // 2, w_own.shape[1]
    return pl.pallas_call(
        out_proj_kernel,
        out_shape=(
            jax.ShapeDtypeStruct((half, width), F32),
            jax.ShapeDtypeStruct((half, width), BF16),
        ),
        in_specs=[VMEM] * 4,
        out_specs=(VMEM, VMEM),
        cost_estimate=SHORT,
        name="out_proj",
    )(own, other, w_own, w_other)


def mixed_grads_kernel(middle0, middle1, w_own_ref, w_other_ref, own_ref, send_ref):
    half = middle0.shape[0]
    for w_ref, out_ref in ((w_other_ref, send_ref), (w_own_ref, own_ref)):
        for i, middle_ref in enumerate((middle0, middle1)):
            part = contract(w_ref[...], 1, middle_ref[...], 1)
            out_ref[:, i * half : (i + 1) * half] = part.astype(BF16)


def mixed_grads(middle, w_own, w_other):
    shape = jax.ShapeDtypeStruct((w_own.shape[0], 2 * middle[0].shape[0]), BF16)
    return pl.pallas_call(
        mixed_grads_kernel,
        out_shape=(shape, shape),
        in_specs=[VMEM] * 4,
        out_specs=(VMEM, VMEM),
        cost_estimate=SHORT,
        name="mixed_grads",
    )(*middle, w_own, w_other)


def ffn_kernel(
    ring,
    normed0,
    normed1,
    grad0,
    grad1,
    inner0,
    inner1,
    outer0,
    outer1,
    own_ref,
    send_ref,
    out_own_ref,
    out_send_ref,
    grads_ref,
    gain_ref,
    hid_ref,
    pre_ref,
    acc_ref,
    out_acc_ref,
    left_ref,
    gain_acc,
):
    half, width = own_ref.shape
    part = inner0.shape[1]
    block = grads_ref.shape[1]
    per_part = part // TILE
    steps = 2 * per_part
    sweeps = 2 * part // block
    step = pl.program_id(0)
    root, cubic = 0.7978845608028654, 0.044715
    places = [
        (normed_ref, grad_ref, begin, i * half + begin)
        for i, (normed_ref, grad_ref) in enumerate(((normed0, grad0), (normed1, grad1)))
        for begin in range(0, half, TILE)
    ]
    weights = ((inner0, outer0), (inner1, outer1))

    def tile(inner_ref, outer_ref, index, offset):
        js = slice(index * TILE, (index + 1) * TILE)
        to = slice(offset + index * TILE, offset + (index + 1) * TILE)
        firsts = []
        for normed_ref, grad_ref, begin, _ in places:
            rs = slice(begin, begin + TILE)
            a = mm(normed_ref[rs, :], inner_ref[:, js])
            firsts.append((a, mm(grad_ref[rs, :], outer_ref[:, js])))
        for (a, dh), (_, _, _, at) in zip(firsts, places):
            rs = slice(at, at + TILE)
            square = a * a
            t = jnp.tanh(root * a * (1.0 + cubic * square))
            cdf = 0.5 * (1.0 + t)
            slope = cdf + 0.5 * a * (1.0 - t * t) * (root * (1.0 + 3.0 * cubic * square))
            hid_ref[rs, to] = (a * cdf).astype(BF16)
            pre_ref[rs, to] = (dh * slope).astype(BF16)

    def rows_out(kept_ref, w_ref, offset, sum_ref, near_ref, far_ref):
        for _, _, _, at in places:
            rs = slice(at, at + TILE)
            back = contract(kept_ref[rs, offset : offset + part], 1, w_ref[...], 1)
            if offset == 0:
                sum_ref[rs, :] = back
            elif at < half:
                near_ref[rs, :] = sum_ref[rs, :] + back
            else:
                far_ref[at - half : at - half + TILE, :] = (sum_ref[rs, :] + back).astype(BF16)

    for i, (inner_ref, outer_ref) in enumerate(weights):
        for index in range(per_part):

            @pl.when(step == i * per_part + index)
            def _(inner_ref=inner_ref, outer_ref=outer_ref, index=index, offset=i * part):
                tile(inner_ref, outer_ref, index, offset)
                if index == per_part - 1:
                    rows_out(pre_ref, inner_ref, offset, acc_ref, own_ref, send_ref)
                    rows_out(hid_ref, outer_ref, offset, out_acc_ref, out_own_ref, out_send_ref)

    def load(first_ref, second_ref):
        left_ref[:, :half] = first_ref[...].T
        left_ref[:, half:] = second_ref[...].T

    for i in range(sweeps):

        @pl.when(step == steps + i)
        def _(i=i):
            if i == 0:
                load(normed0, normed1)
            values = mm(left_ref[...], pre_ref[:, i * block : (i + 1) * block])
            store_ringed(grads_ref, ring, 0, block, values.astype(BF16))
            lanes = gain_acc.shape[1]
            total = jnp.zeros(gain_acc.shape, F32) if i == 0 else gain_acc[...]
            for b in range(0, block, lanes):
                at = i * block + b
                w_ref = inner0 if at < part else inner1
                w = w_ref[:, at % part : at % part + lanes].astype(F32)
                total = total + values[:, b : b + lanes] * w
            gain_acc[...] = total
            if i == sweeps - 1:
                gain_ref[...] = jnp.sum(total.T, axis=0, keepdims=True)

        @pl.when(step == steps + sweeps + i)
        def _(i=i):
            if i == 0:
                load(grad0, grad1)
            values = mm(left_ref[...], hid_ref[:, i * block : (i + 1) * block])
            store_ringed(grads_ref, ring, 0, block, values.astype(BF16))


def ffn(ring, normed, grads, inners, outers):
    half, width = normed[0].shape
    part = inners[0].shape[1]
    rows, hidden = 2 * half, 2 * part
    block = 2 * TILE
    steps = hidden // TILE
    whole = pl.BlockSpec((half, width), lambda j: (0, 0), pipeline_mode=pl.Buffered(1))
    weight = pl.BlockSpec((width, part), lambda j: (0, 0), pipeline_mode=pl.Buffered(1))
    once = pl.BlockSpec((half, width), lambda j: (0, 0))
    return pl.pallas_call(
        functools.partial(ffn_kernel, ring),
        grid=(steps + 2 * (hidden // block),),
        out_shape=(
            jax.ShapeDtypeStruct((half, width), F32),
            jax.ShapeDtypeStruct((half, width), BF16),
            jax.ShapeDtypeStruct((half, width), F32),
            jax.ShapeDtypeStruct((half, width), BF16),
            jax.ShapeDtypeStruct((width, 2 * hidden), BF16),
            jax.ShapeDtypeStruct((1, width), F32),
        ),
        in_specs=[whole] * 4 + [weight] * 4,
        out_specs=(
            once,
            once,
            once,
            once,
            pl.BlockSpec((width, block), lambda j: (0, jnp.maximum(j - steps, 0))),
            pl.BlockSpec((1, width), lambda j: (0, 0)),
        ),
        scratch_shapes=[
            pltpu.VMEM((rows, hidden), BF16),
            pltpu.VMEM((rows, hidden), BF16),
            pltpu.VMEM((rows, width), F32),
            pltpu.VMEM((rows, width), F32),
            pltpu.VMEM((width, rows), BF16),
            pltpu.VMEM((width, 128), F32),
        ],
        compiler_params=pltpu.CompilerParams(vmem_limit_bytes=52 << 20),
        cost_estimate=SHORT,
        name="ffn",
    )(*normed, *grads, *inners, *outers)


def proj_grads_kernel(middle0, middle1, mixed0, mixed1, out_ref):
    half = middle0.shape[0]
    total = 0.0
    for i, middle_ref in enumerate((middle0, middle1)):
        at = slice(i * half, (i + 1) * half)
        mixed = jnp.concatenate([mixed0[:, at], mixed1[:, at]], axis=0)
        total = total + contract(middle_ref[...].T, 1, mixed, 1)
    out_ref[...] = total.astype(BF16)


def proj_grads(middle, mixed):
    shape = (middle[0].shape[1], 2 * mixed[0].shape[0])
    return pl.pallas_call(
        proj_grads_kernel,
        out_shape=jax.ShapeDtypeStruct(shape, BF16),
        in_specs=[VMEM] * 4,
        out_specs=VMEM,
        compiler_params=pltpu.CompilerParams(vmem_limit_bytes=24 << 20),
        cost_estimate=SHORT,
        name="proj_grads",
    )(*middle, *mixed)


def qkv_grads_kernel(
    ring,
    grad_ref,
    slot0_ref,
    slot1_ref,
    slot2_ref,
    slot3_ref,
    w_ref,
    proj_ref,
    out_ref,
    gain_ref,
):
    rows_dev = slot0_ref.shape[0]
    total = 0.0
    for i, slot_ref in enumerate((slot0_ref, slot1_ref, slot2_ref, slot3_ref)):
        total = total + mm(grad_ref[:, i * rows_dev : (i + 1) * rows_dev], slot_ref[...])
    gain_ref[...] = jnp.sum(total * w_ref[:, : total.shape[0]].T.astype(F32), axis=0, keepdims=True)
    both = jnp.concatenate([total.T.astype(BF16), proj_ref[...]], axis=1)
    store_ringed(out_ref, ring, 0, out_ref.shape[1], both)


def qkv_grads(ring, grad_qkv, slots, weights, proj):
    width = slots[0].shape[1]
    cols = grad_qkv.shape[0] + proj.shape[1]
    return pl.pallas_call(
        functools.partial(qkv_grads_kernel, ring),
        out_shape=(
            jax.ShapeDtypeStruct((width, cols), BF16),
            jax.ShapeDtypeStruct((1, width), F32),
        ),
        in_specs=[VMEM] * 7,
        out_specs=(VMEM, VMEM),
        compiler_params=pltpu.CompilerParams(vmem_limit_bytes=58 << 20),
        cost_estimate=SHORT,
        name="qkv_grads",
    )(grad_qkv, *slots, weights, proj)


def finish_kernel(
    pack_ref, taken_ref, last_ref, far_ref, query_ref, key_ref, value_ref, proj_ref, inner_ref, outer_ref
):
    hidden, cols = inner_ref.shape[1], query_ref.shape[1]
    pack, taken, last = pack_ref[...].astype(F32), taken_ref[...].astype(F32), last_ref[...].astype(F32)
    inner_ref[...] = pack[:, :hidden] + taken[:, :hidden]
    outer_ref[...] = pack[:, 2 * hidden : 3 * hidden] + taken[:, hidden:]
    for i, out_ref in enumerate((query_ref, key_ref, value_ref)):
        out_ref[...] = last[:, i * cols : (i + 1) * cols]
    proj_ref[...] = last[:, 3 * cols : 4 * cols] + far_ref[...].astype(F32)


def finish(pack, taken, last, far, hidden):
    rows, cols = far.shape
    shapes = [(rows, cols)] * 4 + [(rows, hidden)] * 2
    return pl.pallas_call(
        finish_kernel,
        out_shape=tuple(jax.ShapeDtypeStruct(shape, F32) for shape in shapes),
        in_specs=[VMEM] * 4,
        out_specs=(VMEM,) * 6,
        cost_estimate=SHORT,
        name="finish",
    )(pack, taken, last, far)


def bias_rows(line):
    heads = line.shape[0]
    pad = 3 * TILE
    rev = jnp.flip(line, axis=1)
    left = jnp.broadcast_to(rev[:, :1], (heads, pad))
    right = jnp.broadcast_to(rev[:, -1:], (heads, pad + 2 * TILE))
    ext = jnp.concatenate([left, rev, right], axis=1)
    begin = [pad + MAXDIST - TILE - TILE * d for d in range(-2, 3)]
    rows = [ext[:, b : b + 2 * TILE] for b in begin]
    return jnp.stack(rows, axis=1).reshape(heads * KINDS, 2 * TILE)


def line_index():
    kind = lax.broadcasted_iota(jnp.int32, (KINDS, 2 * TILE), 0) - 2
    lane = lax.broadcasted_iota(jnp.int32, (KINDS, 2 * TILE), 1)
    near = jnp.clip(TILE + TILE * kind - lane, -MAXDIST, MAXDIST)
    far = jnp.where(kind < 0, -MAXDIST, MAXDIST)
    return (jnp.where(jnp.abs(kind) == 2, far, near) + MAXDIST).reshape(KINDS * 2 * TILE)


def on_device(
    tokens,
    cotangent,
    w_query,
    w_key,
    w_value,
    w_proj,
    w_inner,
    w_outer,
    gain_attn,
    gain_ffn,
    rel_table,
    lengths,
    deal,
    buckets,
):
    rows_dev = tokens.shape[0]
    tensor_size = lax.axis_size("tensor")
    dp_size = lax.axis_size("dp")
    me = lax.axis_index("tensor")
    heads = w_query.shape[1] // HEAD_DIM
    cols = heads * HEAD_DIM
    hidden = w_inner.shape[1]
    width = tokens.shape[1]
    pair = 2 * rows_dev

    def swap(values, bit):
        return lax.ppermute(values, "tensor", [(i, i ^ bit) for i in range(tensor_size)])

    def deal_out(values):
        return lax.all_to_all(values, "dp", split_axis=0, concat_axis=0, tiled=True)

    def pick(values, order):
        return values.at[order].get(mode="promise_in_bounds", unique_indices=True)

    def total_sum(values, passing):
        values = values + swap(values, 1)
        step = 1
        while step < dp_size:
            if 2 * step >= dp_size:
                values, passing = after(values, passing)
                values = values + swap(values, 2)
            values = values + lax.ppermute(values, "dp", [(i, i ^ step) for i in range(dp_size)])
            step *= 2
        return values, passing

    ring = ring_order(dp_size)
    both = ("dp", "tensor")
    ring_groups = [[d * tensor_size + t for d in ring] for t in range(tensor_size)]

    def gather(values, spans):
        found = lax.all_gather(values, both, axis=0, tiled=True, axis_index_groups=ring_groups)
        return unring(found, ring, spans)

    def scatter_sum(values):
        return lax.psum_scatter(
            ringed(values, ring), both, scatter_dimension=0, tiled=True, axis_index_groups=ring_groups
        )

    own_front, own_inner = pack_weights(
        w_inner, w_query, w_key, w_value, w_proj.T, w_outer.T
    )
    own_front, tokens = after(own_front, tokens)
    ends = (3 * cols, 3 * cols + hidden, 4 * cols + hidden)
    front, outer_own, proj_own = gather(
        own_front, ((0, ends[0], False), (ends[0], ends[1], False), (ends[1], ends[2], True))
    )
    low_rows = deal_out(pick(tokens, deal))
    onehot_buckets = (
        buckets[:, None] == jnp.arange(rel_table.shape[0], dtype=jnp.int32)[None, :]
    ).astype(F32)
    head_table = lax.dynamic_slice_in_dim(rel_table, me * heads, heads, 1)
    offset_bias = jnp.dot(onehot_buckets, head_table, precision=lax.Precision.HIGHEST).T
    base = bias_rows(offset_bias)
    info = jnp.concatenate([lengths, jnp.full((1, 1), me, jnp.int32)], axis=1)

    inverse_order = (
        jnp.zeros((rows_dev,), jnp.int32).at[deal].set(jnp.arange(rows_dev, dtype=jnp.int32))
    )
    slot0 = (scaled_rows(low_rows.astype(F32)) * gain_attn).astype(BF16)
    own_inner, slot0 = after(own_inner, slot0)
    inner_own, inner_other = gather(
        jnp.concatenate([own_inner, swap(own_inner, 2)], axis=1),
        ((0, hidden, False), (hidden, 2 * hidden, False)),
    )
    slot2 = swap(slot0, 2)
    slot1 = swap(slot0, 1)
    slot2, front, base, info = after(slot2, front, base, info)
    slot3 = swap(slot2, 1)
    slots = (slot0, slot1, slot2, slot3)
    proj_other, outer_other = swap(proj_own, 2), swap(outer_own, 2)

    low_grads = deal_out(pick(cotangent, deal))

    mixed_far, wide_far, lse_far, qkv, keys = attend_far(info, base, front, slots)
    mixed_other = swap(mixed_far, 2)
    late_qkv, outer_other, low_grads = after(qkv, outer_other, low_grads)
    mixed_own, wide_own, lse_own = attend_near(info, base, late_qkv, keys, rows_dev)
    near, to_core = out_proj(mixed_own, mixed_other, proj_own, proj_other)
    near, inner_own, inner_other = after(near, inner_own, inner_other)
    middle, low_two = by_rows(
        join_kernel, "join", gain_ffn, low_rows, near, swap(to_core, 1), out=(F32, BF16)
    )

    pair_two = (low_two, swap(low_two, 1))
    pair_grads = (low_grads, swap(low_grads, 1))
    back_own, back_send, out_own, out_far, grad_pack, gain_two = ffn(
        ring, pair_two, pair_grads, (inner_own, inner_other), (outer_own, outer_other)
    )
    shard_pack = scatter_sum(grad_pack)
    grad_middle, low_middle = by_rows(
        middle_back_kernel,
        "middle_back",
        gain_ffn,
        middle,
        back_own,
        swap(back_send, 1),
        low_grads,
        out=(F32, BF16),
    )
    pair_middle = (low_middle, swap(low_middle, 1))
    grad_own, to_other = mixed_grads(pair_middle, proj_own, proj_other)

    proj_pack = proj_grads(pair_middle, (mixed_own, mixed_other))

    out_own, to_other = after(out_own, to_other)
    result_rows = (middle + out_own + swap(out_far, 1).astype(F32)).astype(BF16)
    result_rows, proj_pack = after(result_rows, proj_pack)
    back_rows = deal_out(result_rows)

    grad_far, proj_pack = after(swap(to_other, 2), proj_pack)
    grad_qkv, diagonals, rows_own, rows_send = attend_back(
        info,
        base,
        qkv,
        keys,
        (wide_own, wide_far),
        (lse_own, lse_far),
        (grad_own, grad_far),
        front,
        rows_dev,
    )
    rows_send, back_rows = after(rows_send, back_rows)
    rows_core = swap(rows_send, 1)
    grad_later = (rows_own[:rows_dev] + rows_core[:rows_dev].astype(F32)).astype(BF16)
    later_qkv, grad_later = after(grad_qkv, grad_later)
    low_qkv_w, gain_one = qkv_grads(ring, later_qkv, slots, front, proj_pack)
    low_qkv_w, shard_pack = after(low_qkv_w, shard_pack)
    shard_qkv = scatter_sum(low_qkv_w)
    out_rows = pick(back_rows, inverse_order)
    rows_near, out_rows = after(rows_core[rows_dev:], out_rows)
    (low_grad_rows,) = by_rows(
        rows_back_kernel,
        "rows_back",
        gain_attn,
        low_rows,
        rows_own[rows_dev:],
        rows_near,
        swap(grad_later, 2),
        grad_middle,
        out=(BF16,),
        cost=LONG,
    )
    taken = swap(
        jnp.concatenate([shard_pack[:, hidden : 2 * hidden], shard_pack[:, 3 * hidden :]], axis=1),
        2,
    )

    offset_count = 2 * MAXDIST + 1
    onehot_line = (
        line_index()[:, None] == jnp.arange(offset_count, dtype=jnp.int32)[None, :]
    ).astype(F32)
    offset_total = jnp.dot(
        diagonals.reshape(heads, KINDS * 2 * TILE), onehot_line, precision=lax.Precision.HIGHEST
    )
    table_heads = jnp.dot(onehot_buckets.T, offset_total.T, precision=lax.Precision.HIGHEST)
    table_full = lax.dynamic_update_slice_in_dim(
        jnp.zeros(rel_table.shape, F32), table_heads, me * heads, 1
    )
    terms = [gain_one[0] / gain_attn, gain_two[0] / gain_ffn, table_full.reshape(-1)]
    small, taken = total_sum(jnp.concatenate(terms).reshape(-1, 128), taken)
    small = small.reshape(-1)
    back_grads = deal_out(low_grad_rows)
    weight_shards = finish(shard_pack, taken, shard_qkv, swap(shard_qkv[:, 4 * cols :], 2), hidden)
    return (
        out_rows,
        pick(back_grads, inverse_order),
        *weight_shards[:3],
        weight_shards[3].T,
        weight_shards[4],
        weight_shards[5].T,
        small[:width],
        small[width : 2 * width],
        small[2 * width :].reshape(rel_table.shape),
    )


def solution(mesh):
    rows = P(("dp", "tensor"), None)
    inward, outward = P("dp", "tensor"), P("tensor", "dp")
    weights = (inward, inward, inward, outward, inward, outward)
    return jax.shard_map(
        on_device,
        mesh=mesh,
        in_specs=(rows, rows, *weights, P(), P(), P(), P("dp", None), P(("dp", "tensor")), P()),
        out_specs=(rows, rows, *weights, P(), P(), P()),
        check_vma=False,
    )
```

```python
import functools

import jax
import jax.numpy as jnp
from jax import lax
from jax.experimental import pallas as pl
from jax.experimental.pallas import tpu as pltpu
from jax.sharding import PartitionSpec as P

HEAD_DIM = 64
MAXDIST = 128
TILE = 256
KINDS = 5
EPS = 1e-06
NEG = -1000000000.0
BF16 = jnp.bfloat16
F32 = jnp.float32
VMEM = pl.BlockSpec(memory_space=pltpu.VMEM)
SMEM = pl.BlockSpec(memory_space=pltpu.SMEM)


SHORT = pl.CostEstimate(flops=1 << 20, bytes_accessed=1 << 16, transcendentals=0)


LONG = pl.CostEstimate(flops=3 << 33, bytes_accessed=1 << 26, transcendentals=1 << 23)


def mm(left, right):
    return jnp.dot(left, right, preferred_element_type=F32)


def contract(left, left_dim, right, right_dim):
    return lax.dot_general(
        left, right, (((left_dim,), (right_dim,)), ((), ())), preferred_element_type=F32
    )


def after(*values):
    return lax.optimization_barrier(values)


def ring_order(size):
    return [*range(0, size, 2), *range(size - 1, 0, -2)]


def tile_start(tile, rows_dev, me):
    per_slot = rows_dev // TILE
    return pl.multiple_of((((tile // per_slot) ^ me) * per_slot + tile % per_slot) * TILE, TILE)


def build_bias(base_ref, bias_ref, heads):
    for i in range(heads * KINDS):
        row = base_ref[i : i + 1, :]
        if i % KINDS in (0, KINDS - 1):
            bias_ref[i] = jnp.broadcast_to(row[:, :1], (TILE, TILE))
        else:
            full = jnp.broadcast_to(row, (TILE, 2 * TILE))
            bias_ref[i] = pltpu.roll(full, 0, 1, stride=1, stride_axis=0)[:, TILE:]


def pack_kernel(inner_ref, query_ref, key_ref, value_ref, proj_ref, outer_ref, first_ref, rest_ref):
    hidden = inner_ref.shape[1]
    first = [query_ref[...], key_ref[...], value_ref[...], outer_ref[...], proj_ref[...]]
    first_ref[...] = jnp.concatenate(first, axis=1).astype(BF16)
    rest_ref[:, :hidden] = inner_ref[...].astype(BF16)
    rest_ref[:, hidden:] = proj_ref[...].astype(BF16)


def pack_weights(inner, query, key, value, proj, outer):
    rows, hidden = inner.shape
    cols = query.shape[1]
    return pl.pallas_call(
        pack_kernel,
        out_shape=(
            jax.ShapeDtypeStruct((rows, 4 * cols + hidden), BF16),
            jax.ShapeDtypeStruct((rows, hidden + cols), BF16),
        ),
        in_specs=[VMEM] * 6,
        out_specs=(VMEM, VMEM),
        cost_estimate=SHORT,
        name="pack_weights",
    )(inner, query, key, value, proj, outer)


def unring_kernel(ring, spans, found_ref, *out_refs):
    size = found_ref.shape[0] // len(ring)
    for (begin, end, turned), out_ref in zip(spans, out_refs):
        if turned:
            blocks = [
                found_ref[ring.index(d) * size : (ring.index(d) + 1) * size, begin:end]
                for d in range(len(ring))
            ]
            out_ref[...] = jnp.concatenate(blocks, axis=0).T
        else:
            for p, d in enumerate(ring):
                block = found_ref[p * size : (p + 1) * size, begin:end]
                out_ref[d * size : (d + 1) * size, :] = block


def unring(found, ring, spans):
    rows = found.shape[0]
    size = rows // len(ring)
    if size % 16:
        back = [found[ring.index(d) * size :][:size] for d in range(len(ring))]
        whole = jnp.concatenate(back, axis=0)
        parts = [whole[:, begin:end] for begin, end, _ in spans]
        return [part.T if span[2] else part for part, span in zip(parts, spans)]
    shapes = [(end - begin, rows) if turned else (rows, end - begin) for begin, end, turned in spans]
    return pl.pallas_call(
        functools.partial(unring_kernel, ring, spans),
        out_shape=tuple(jax.ShapeDtypeStruct(shape, found.dtype) for shape in shapes),
        in_specs=[VMEM],
        out_specs=(VMEM,) * len(spans),
        cost_estimate=SHORT,
        name="unring",
    )(found)


def store_ringed(out_ref, ring, begin, end, values):
    size = values.shape[0] // len(ring)
    if size % 16:
        out_ref[:, begin:end] = values
    else:
        for p, d in enumerate(ring):
            out_ref[p * size : (p + 1) * size, begin:end] = values[d * size : (d + 1) * size, :]


def ringed(values, ring):
    size = values.shape[0] // len(ring)
    if size % 16 == 0:
        return values
    return jnp.concatenate([values[d * size :][:size] for d in ring], axis=0)


def segment_rows(width, first_len, start, same, other):
    shape = (HEAD_DIM, width)
    low = start + lax.broadcasted_iota(jnp.int32, shape, 1) < first_len
    row = lax.broadcasted_iota(jnp.int32, shape, 0)
    first = jnp.where(low, same, other)
    second = jnp.where(low, other, same)
    return jnp.where(row == 0, first, jnp.where(row == 1, second, 0.0)).astype(BF16)


def segment_all(rows, rows_dev, first_len, me, same, other):
    slots = rows // rows_dev
    return jnp.concatenate(
        [
            segment_rows(rows_dev, first_len, (s ^ me) * rows_dev, same, other)
            for s in range(slots)
        ],
        axis=1,
    )


def tile_range(tile, first_len, tiles):
    start = tile * TILE
    low = jnp.where(start >= first_len, first_len // TILE, 0)
    high = jnp.where(start + TILE <= first_len, (first_len + TILE - 1) // TILE, tiles)
    return low, high


def over_tiles(low, high, body, carry, sizes=(4, 2, 1)):
    at = low
    for size in sizes:
        count = (high - at) // size

        def step(i, c, at=at, size=size):
            return body(tuple(at + size * i + j for j in range(size)), c)

        carry = lax.fori_loop(0, count, step, carry)
        at = at + size * count
    return carry


def attend_rows(
    heads, rows_dev, first_slot, info_ref, qkv_ref, key_ref, out_ref, wide_ref, lse_ref, score_ref, bias_ref
):
    rows = qkv_ref.shape[1]
    cols = heads * HEAD_DIM
    first_len, me = info_ref[0, 0], info_ref[0, 2]
    tiles = rows // TILE
    per_slot = rows_dev // TILE

    def query_tile(i, carry):
        qb = ((first_slot + i // per_slot) ^ me) * per_slot + i % per_slot
        qs = pl.ds(pl.multiple_of(first_slot * rows_dev + i * TILE, TILE), TILE)
        at = pl.ds(pl.multiple_of(i * TILE, TILE), TILE)
        query_seg = segment_rows(TILE, first_len, qb * TILE, 0.0, NEG)
        queries = [
            jnp.concatenate([qkv_ref[h * HEAD_DIM : (h + 1) * HEAD_DIM, qs], query_seg], axis=0)
            for h in range(heads)
        ]
        low, high = tile_range(qb, first_len, tiles)

        def score_tiles(kbs, tops):
            kss = [pl.ds(tile_start(kb, rows_dev, me), TILE) for kb in kbs]
            kinds = [jnp.clip(kb - qb, -2, 2) + 2 for kb in kbs]
            ss = [[mm(key_ref[h, ks, :], queries[h]) for h in range(heads)] for ks in kss]
            tops = list(tops)
            for i, ks in enumerate(kss):
                for h in range(heads):
                    s = ss[i][h] + bias_ref[h * KINDS + kinds[i]]
                    score_ref[h, ks, :] = s
                    tops[h] = jnp.maximum(tops[h], jnp.max(s.reshape(TILE // 8, 8, TILE), axis=0))
            return tuple(tops)

        tops = over_tiles(low, high, score_tiles, (jnp.full((8, TILE), -3e38, F32),) * heads)
        tops = [jnp.max(t, axis=0, keepdims=True) for t in tops]

        def value_tiles(kbs, sums):
            kss = [pl.ds(tile_start(kb, rows_dev, me), TILE) for kb in kbs]
            sums = list(sums)
            ps = []
            for ks in kss:
                for h in range(heads):
                    p = jnp.exp(score_ref[h, ks, :] - tops[h])
                    total, acc = sums[h]
                    sums[h] = (total + jnp.sum(p.reshape(TILE // 8, 8, TILE), axis=0), acc)
                    ps.append(p.astype(BF16))
            for i, ks in enumerate(kss):
                for h in range(heads):
                    values = qkv_ref[2 * cols + h * HEAD_DIM : 2 * cols + (h + 1) * HEAD_DIM, ks]
                    total, acc = sums[h]
                    sums[h] = (total, acc + mm(values, ps[i * heads + h]))
            return tuple(sums)

        zero = (jnp.zeros((8, TILE), F32), jnp.zeros((HEAD_DIM, TILE), F32))
        sums = over_tiles(low, high, value_tiles, (zero,) * heads)
        for h in range(heads):
            total, acc = sums[h]
            total = jnp.sum(total, axis=0, keepdims=True)
            mixed = acc * (1.0 / total)
            hs = slice(h * HEAD_DIM, (h + 1) * HEAD_DIM)
            wide_ref[hs, at] = mixed
            out_ref[hs, at] = mixed.astype(BF16)
            lse_ref[h : h + 1, at] = tops[h] + jnp.log(total)
        return carry

    lax.fori_loop(0, tiles // 2, query_tile, 0)


def attend_far_kernel(
    heads,
    rows_dev,
    info_ref,
    base_ref,
    w_ref,
    slot0_ref,
    slot1_ref,
    slot2_ref,
    slot3_ref,
    out_ref,
    wide_ref,
    lse_ref,
    qkv_ref,
    key_ref,
    score_ref,
    bias_ref,
):
    rows = qkv_ref.shape[1]
    cols = heads * HEAD_DIM
    w_rows = w_ref[:, : 3 * cols].T
    for i, slot_ref in enumerate((slot0_ref, slot1_ref, slot2_ref, slot3_ref)):
        for begin in range(0, rows_dev, TILE):
            part = contract(w_rows, 1, slot_ref[begin : begin + TILE, :], 1)
            at = i * rows_dev + begin
            qkv_ref[:, at : at + TILE] = part.astype(BF16)
    build_bias(base_ref, bias_ref, heads)
    key_seg = segment_all(rows, rows_dev, info_ref[0, 0], info_ref[0, 2], 1.0, 0.0)
    for h in range(heads):
        key_ref[h] = jnp.concatenate(
            [qkv_ref[cols + h * HEAD_DIM : cols + (h + 1) * HEAD_DIM, :], key_seg], axis=0
        ).T
    far = rows // rows_dev // 2
    attend_rows(
        heads, rows_dev, far, info_ref, qkv_ref, key_ref, out_ref, wide_ref, lse_ref, score_ref, bias_ref
    )


def attend_near_kernel(
    heads, rows_dev, info_ref, base_ref, qkv_ref, key_ref, out_ref, wide_ref, lse_ref, score_ref, bias_ref
):
    build_bias(base_ref, bias_ref, heads)
    attend_rows(
        heads, rows_dev, 0, info_ref, qkv_ref, key_ref, out_ref, wide_ref, lse_ref, score_ref, bias_ref
    )


def attend_shapes(heads, rows):
    cols = heads * HEAD_DIM
    return (
        jax.ShapeDtypeStruct((cols, rows // 2), BF16),
        jax.ShapeDtypeStruct((cols, rows // 2), F32),
        jax.ShapeDtypeStruct((heads, rows // 2), F32),
    )


def attend_scratch(heads, rows):
    return [
        pltpu.VMEM((heads, rows, TILE), F32),
        pltpu.VMEM((heads * KINDS, TILE, TILE), F32),
    ]


def attend_far(info, base, weights, slots):
    rows_dev = slots[0].shape[0]
    rows = rows_dev * len(slots)
    cols = weights.shape[1] // 3
    heads = cols // HEAD_DIM
    return pl.pallas_call(
        functools.partial(attend_far_kernel, heads, rows_dev),
        out_shape=attend_shapes(heads, rows)
        + (
            jax.ShapeDtypeStruct((3 * cols, rows), BF16),
            jax.ShapeDtypeStruct((heads, rows, 2 * HEAD_DIM), BF16),
        ),
        in_specs=[SMEM] + [VMEM] * 6,
        out_specs=(VMEM,) * 5,
        scratch_shapes=attend_scratch(heads, rows),
        compiler_params=pltpu.CompilerParams(vmem_limit_bytes=58 << 20),
        cost_estimate=SHORT,
        name="attend_far",
    )(info, base, weights, *slots)


def attend_near(info, base, qkv, keys, rows_dev):
    heads, rows = keys.shape[:2]
    return pl.pallas_call(
        functools.partial(attend_near_kernel, heads, rows_dev),
        out_shape=attend_shapes(heads, rows),
        in_specs=[SMEM] + [VMEM] * 3,
        out_specs=(VMEM,) * 3,
        scratch_shapes=attend_scratch(heads, rows),
        compiler_params=pltpu.CompilerParams(vmem_limit_bytes=58 << 20),
        cost_estimate=SHORT,
        name="attend_near",
    )(info, base, qkv, keys)


def diagonal_sums(values):
    values = jnp.concatenate([jnp.zeros_like(values), values], axis=1)
    count = TILE
    while count > 1:
        count //= 2
        values = values[:count] + pltpu.roll(values[count:], 2 * TILE - count, 1)
    return values


def grad_rows_to(own_ref, send_ref, first_slot, grad_ref, w_ref):
    rows_dev = own_ref.shape[0]
    for slot, out_ref in ((first_slot + 1, send_ref), (first_slot, own_ref)):
        for begin in range(0, rows_dev, TILE):
            at = slot * rows_dev + begin
            part = contract(grad_ref[:, at : at + TILE], 0, w_ref[...], 1)
            out_ref[begin : begin + TILE, :] = part.astype(out_ref.dtype)


def attend_back_kernel(
    heads,
    rows_dev,
    info_ref,
    base_ref,
    qkv_ref,
    key_ref,
    wide0_ref,
    wide1_ref,
    lse0_ref,
    lse1_ref,
    grad0_ref,
    grad1_ref,
    w_ref,
    out_ref,
    diag_ref,
    far_own_ref,
    far_send_ref,
    near_own_ref,
    near_send_ref,
    lse_ref,
    inner_ref,
    grad_ref,
    query_ref,
    value_rows,
    query_rows,
    grad_rows,
    key_acc,
    value_acc,
    bias_ref,
    table_ref,
):
    rows = qkv_ref.shape[1]
    cols = heads * HEAD_DIM
    first_len, me = info_ref[0, 0], info_ref[0, 2]
    tiles = rows // TILE
    build_bias(base_ref, bias_ref, heads)
    query_seg = segment_all(rows, rows_dev, first_len, me, 0.0, NEG)
    q_of = [slice(h * HEAD_DIM, (h + 1) * HEAD_DIM) for h in range(heads)]
    k_of = [slice(cols + h * HEAD_DIM, cols + (h + 1) * HEAD_DIM) for h in range(heads)]
    v_of = [slice(2 * cols + h * HEAD_DIM, 2 * cols + (h + 1) * HEAD_DIM) for h in range(heads)]
    lse_ref[:, : rows // 2] = lse0_ref[...]
    lse_ref[:, rows // 2 :] = lse1_ref[...]
    grad_ref[:, : rows // 2] = grad0_ref[...]
    grad_ref[:, rows // 2 :] = grad1_ref[...]
    for h in range(heads):
        queries = qkv_ref[q_of[h], :]
        query_ref[h] = jnp.concatenate([queries, query_seg], axis=0)
        query_rows[h] = queries.T
        value_rows[h] = qkv_ref[v_of[h], :].T
        grad_rows[h] = grad_ref[q_of[h], :].T
        for half, wide_ref in ((0, wide0_ref), (1, wide1_ref)):
            at = slice(half * rows // 2, (half + 1) * rows // 2)
            terms = grad_ref[q_of[h], at].astype(F32) * wide_ref[q_of[h], :]
            inner_ref[h : h + 1, at] = jnp.sum(terms, axis=0, keepdims=True)
    key_acc[...] = jnp.zeros_like(key_acc)
    value_acc[...] = jnp.zeros_like(value_acc)
    table_ref[...] = jnp.zeros_like(table_ref)

    def query_tile(qb, carry):
        qs = pl.ds(tile_start(qb, rows_dev, me), TILE)
        low, high = tile_range(qb, first_len, tiles)
        grads = [grad_ref[q_of[h], qs] for h in range(heads)]
        inner = [inner_ref[h : h + 1, qs] for h in range(heads)]
        lse = [lse_ref[h : h + 1, qs] for h in range(heads)]

        def tiles_at(kbs, sums):
            kss = [pl.ds(tile_start(kb, rows_dev, me), TILE) for kb in kbs]
            kinds = [jnp.clip(kb - qb, -2, 2) + 2 for kb in kbs]
            ss = [[mm(key_ref[h, ks, :], query_ref[h, :, qs]) for h in range(heads)] for ks in kss]
            dps = [[mm(value_rows[h, ks, :], grads[h]) for h in range(heads)] for ks in kss]
            lows = []
            for i in range(len(kbs)):
                for h in range(heads):
                    p = jnp.exp(ss[i][h] + bias_ref[h * KINDS + kinds[i]] - lse[h])
                    ds = p * (dps[i][h] - inner[h])
                    table_ref[h * KINDS + kinds[i]] += ds
                    lows.append((p.astype(BF16), ds.astype(BF16)))
            sums = list(sums)
            for i, ks in enumerate(kss):
                for h in range(heads):
                    low_p, low_ds = lows[i * heads + h]
                    value_acc[h, ks, :] += mm(low_p, grad_rows[h, qs, :])
                    key_acc[h, ks, :] += mm(low_ds, query_rows[h, qs, :])
                    sums[h] = sums[h] + mm(qkv_ref[k_of[h], ks], low_ds)
            return tuple(sums)

        sums = tuple(jnp.zeros((HEAD_DIM, TILE), F32) for _ in range(heads))
        sums = over_tiles(low, high, tiles_at, sums, (2, 1))
        for h in range(heads):
            out_ref[q_of[h], qs] = sums[h].astype(BF16)
        return carry

    lax.fori_loop(0, tiles, query_tile, 0)
    for h in range(heads):
        out_ref[k_of[h], :] = key_acc[h].astype(BF16).T
        out_ref[v_of[h], :] = value_acc[h].astype(BF16).T
    grad_rows_to(far_own_ref, far_send_ref, rows // rows_dev // 2, out_ref, w_ref)
    grad_rows_to(near_own_ref, near_send_ref, 0, out_ref, w_ref)
    for i in range(heads * KINDS):
        if i % KINDS in (0, KINDS - 1):
            total = jnp.sum(table_ref[i], axis=0, keepdims=True)
            diag_ref[i : i + 1, :] = jnp.concatenate([total, jnp.zeros_like(total)], axis=1)
        else:
            diag_ref[i : i + 1, :] = diagonal_sums(table_ref[i])


def attend_back(info, base, qkv, keys, wide, lse, grad, weights, rows_dev):
    rows = qkv.shape[1]
    width = weights.shape[0]
    heads = qkv.shape[0] // (3 * HEAD_DIM)
    cols = heads * HEAD_DIM
    return pl.pallas_call(
        functools.partial(attend_back_kernel, heads, rows_dev),
        out_shape=(
            jax.ShapeDtypeStruct((3 * cols, rows), BF16),
            jax.ShapeDtypeStruct((heads * KINDS, 2 * TILE), F32),
            jax.ShapeDtypeStruct((rows_dev, width), F32),
            jax.ShapeDtypeStruct((rows_dev, width), BF16),
            jax.ShapeDtypeStruct((rows_dev, width), F32),
            jax.ShapeDtypeStruct((rows_dev, width), BF16),
        ),
        in_specs=[SMEM] + [VMEM] * 10,
        out_specs=(VMEM,) * 6,
        scratch_shapes=[
            pltpu.VMEM((heads, rows), F32),
            pltpu.VMEM((heads, rows), F32),
            pltpu.VMEM((cols, rows), BF16),
            pltpu.VMEM((heads, 2 * HEAD_DIM, rows), BF16),
            pltpu.VMEM((heads, rows, HEAD_DIM), BF16),
            pltpu.VMEM((heads, rows, HEAD_DIM), BF16),
            pltpu.VMEM((heads, rows, HEAD_DIM), BF16),
            pltpu.VMEM((heads, rows, HEAD_DIM), F32),
            pltpu.VMEM((heads, rows, HEAD_DIM), F32),
            pltpu.VMEM((heads * KINDS, TILE, TILE), F32),
            pltpu.VMEM((heads * KINDS, TILE, TILE), F32),
        ],
        compiler_params=pltpu.CompilerParams(vmem_limit_bytes=58 << 20),
        cost_estimate=LONG,
        name="attend_back",
    )(info, base, qkv, keys, *wide, *lse, *grad, weights)


def scaled_rows(values):
    return values * lax.rsqrt(jnp.mean(values * values, axis=-1, keepdims=True) + EPS)


def join_kernel(rows_ref, near_ref, far_ref, gain_ref, middle_ref, low_ref):
    for rs in row_blocks(rows_ref.shape[0]):
        middle = rows_ref[rs, :].astype(F32) + near_ref[rs, :] + far_ref[rs, :].astype(F32)
        middle_ref[rs, :] = middle
        low_ref[rs, :] = (scaled_rows(middle) * gain_ref[...]).astype(BF16)


def row_blocks(rows):
    return [slice(begin, begin + TILE // 4) for begin in range(0, rows, TILE // 4)]


def norm_back_rows(values, upstream, gain):
    scale = lax.rsqrt(jnp.mean(values * values, axis=-1, keepdims=True) + EPS)
    normed = values * scale
    scaled = upstream * gain
    inner = jnp.mean(scaled * normed, axis=-1, keepdims=True)
    return scale * (scaled - normed * inner)


def middle_back_kernel(middle_ref, near_ref, far_ref, grads_ref, gain_ref, wide_ref, low_ref):
    for rs in row_blocks(middle_ref.shape[0]):
        upstream = near_ref[rs, :] + far_ref[rs, :].astype(F32)
        back = norm_back_rows(middle_ref[rs, :], upstream, gain_ref[...])
        wide = grads_ref[rs, :].astype(F32) + back
        wide_ref[rs, :] = wide
        low_ref[rs, :] = wide.astype(BF16)


def rows_back_kernel(rows_ref, near_ref, core_ref, far_ref, wide_ref, gain_ref, low_ref):
    for rs in row_blocks(rows_ref.shape[0]):
        upstream = near_ref[rs, :] + core_ref[rs, :].astype(F32) + far_ref[rs, :].astype(F32)
        back = norm_back_rows(rows_ref[rs, :].astype(F32), upstream, gain_ref[...])
        low_ref[rs, :] = (wide_ref[rs, :] + back).astype(BF16)


def by_rows(kernel, name, gain, *operands, out, cost=SHORT):
    shape = operands[0].shape
    return pl.pallas_call(
        kernel,
        out_shape=tuple(jax.ShapeDtypeStruct(shape, kind) for kind in out),
        in_specs=[VMEM] * (len(operands) + 1),
        out_specs=(VMEM,) * len(out),
        compiler_params=pltpu.CompilerParams(vmem_limit_bytes=16 << 20),
        cost_estimate=cost,
        name=name,
    )(*operands, gain[None])


def out_proj_kernel(own_ref, other_ref, w_own_ref, w_other_ref, near_ref, send_ref):
    half = near_ref.shape[0]
    for begin in range(0, 2 * half, TILE):
        part = contract(own_ref[:, begin : begin + TILE], 0, w_own_ref[...], 0)
        part = part + contract(other_ref[:, begin : begin + TILE], 0, w_other_ref[...], 0)
        if begin < half:
            near_ref[begin : begin + TILE, :] = part
        else:
            send_ref[begin - half : begin - half + TILE, :] = part.astype(BF16)


def out_proj(own, other, w_own, w_other):
    half, width = own.shape[1] // 2, w_own.shape[1]
    return pl.pallas_call(
        out_proj_kernel,
        out_shape=(
            jax.ShapeDtypeStruct((half, width), F32),
            jax.ShapeDtypeStruct((half, width), BF16),
        ),
        in_specs=[VMEM] * 4,
        out_specs=(VMEM, VMEM),
        compiler_params=pltpu.CompilerParams(vmem_limit_bytes=16 << 20),
        cost_estimate=SHORT,
        name="out_proj",
    )(own, other, w_own, w_other)


def mixed_grads_kernel(middle0, middle1, w_own_ref, w_other_ref, own_ref, send_ref):
    half = middle0.shape[0]
    for w_ref, out_ref in ((w_other_ref, send_ref), (w_own_ref, own_ref)):
        for i, middle_ref in enumerate((middle0, middle1)):
            part = contract(w_ref[...], 1, middle_ref[...], 1)
            out_ref[:, i * half : (i + 1) * half] = part.astype(BF16)


def mixed_grads(middle, w_own, w_other):
    shape = jax.ShapeDtypeStruct((w_own.shape[0], 2 * middle[0].shape[0]), BF16)
    return pl.pallas_call(
        mixed_grads_kernel,
        out_shape=(shape, shape),
        in_specs=[VMEM] * 4,
        out_specs=(VMEM, VMEM),
        compiler_params=pltpu.CompilerParams(vmem_limit_bytes=16 << 20),
        cost_estimate=SHORT,
        name="mixed_grads",
    )(*middle, w_own, w_other)


def ffn_kernel(
    ring,
    normed0,
    normed1,
    grad0,
    grad1,
    inner0,
    inner1,
    outer0,
    outer1,
    own_ref,
    send_ref,
    out_own_ref,
    out_send_ref,
    grads_ref,
    gain_ref,
    hid_ref,
    pre_ref,
    acc_ref,
    out_acc_ref,
    left_ref,
    gain_acc,
):
    half, width = own_ref.shape
    part = inner0.shape[1]
    block = grads_ref.shape[1]
    per_part = part // TILE
    steps = 2 * per_part
    sweeps = 2 * part // block
    step = pl.program_id(0)
    root, cubic = 0.7978845608028654, 0.044715
    places = [
        (normed_ref, grad_ref, begin, i * half + begin)
        for i, (normed_ref, grad_ref) in enumerate(((normed0, grad0), (normed1, grad1)))
        for begin in range(0, half, TILE)
    ]
    weights = ((inner0, outer0), (inner1, outer1))

    def tile(inner_ref, outer_ref, index, offset):
        js = slice(index * TILE, (index + 1) * TILE)
        to = slice(offset + index * TILE, offset + (index + 1) * TILE)
        firsts = []
        for normed_ref, grad_ref, begin, _ in places:
            rs = slice(begin, begin + TILE)
            a = mm(normed_ref[rs, :], inner_ref[:, js])
            firsts.append((a, mm(grad_ref[rs, :], outer_ref[:, js])))
        for (a, dh), (_, _, _, at) in zip(firsts, places):
            rs = slice(at, at + TILE)
            square = a * a
            t = jnp.tanh(root * a * (1.0 + cubic * square))
            cdf = 0.5 * (1.0 + t)
            slope = cdf + 0.5 * a * (1.0 - t * t) * (root * (1.0 + 3.0 * cubic * square))
            hid_ref[rs, to] = (a * cdf).astype(BF16)
            pre_ref[rs, to] = (dh * slope).astype(BF16)

    def rows_out(kept_ref, w_ref, offset, sum_ref, near_ref, far_ref):
        for _, _, _, at in places:
            rs = slice(at, at + TILE)
            back = contract(kept_ref[rs, offset : offset + part], 1, w_ref[...], 1)
            if offset == 0:
                sum_ref[rs, :] = back
            elif at < half:
                near_ref[rs, :] = sum_ref[rs, :] + back
            else:
                far_ref[at - half : at - half + TILE, :] = (sum_ref[rs, :] + back).astype(BF16)

    for i, (inner_ref, outer_ref) in enumerate(weights):
        for index in range(per_part):

            @pl.when(step == i * per_part + index)
            def _(inner_ref=inner_ref, outer_ref=outer_ref, index=index, offset=i * part):
                tile(inner_ref, outer_ref, index, offset)
                if index == per_part - 1:
                    rows_out(pre_ref, inner_ref, offset, acc_ref, own_ref, send_ref)
                    rows_out(hid_ref, outer_ref, offset, out_acc_ref, out_own_ref, out_send_ref)

    def load(first_ref, second_ref):
        left_ref[:, :half] = first_ref[...].T
        left_ref[:, half:] = second_ref[...].T

    for i in range(sweeps):

        @pl.when(step == steps + i)
        def _(i=i):
            if i == 0:
                load(normed0, normed1)
            values = mm(left_ref[...], pre_ref[:, i * block : (i + 1) * block])
            store_ringed(grads_ref, ring, 0, block, values.astype(BF16))
            lanes = gain_acc.shape[1]
            total = jnp.zeros(gain_acc.shape, F32) if i == 0 else gain_acc[...]
            for b in range(0, block, lanes):
                at = i * block + b
                w_ref = inner0 if at < part else inner1
                w = w_ref[:, at % part : at % part + lanes].astype(F32)
                total = total + values[:, b : b + lanes] * w
            gain_acc[...] = total
            if i == sweeps - 1:
                gain_ref[...] = jnp.sum(total.T, axis=0, keepdims=True)

        @pl.when(step == steps + sweeps + i)
        def _(i=i):
            if i == 0:
                load(grad0, grad1)
            values = mm(left_ref[...], hid_ref[:, i * block : (i + 1) * block])
            store_ringed(grads_ref, ring, 0, block, values.astype(BF16))


def ffn(ring, normed, grads, inners, outers):
    half, width = normed[0].shape
    part = inners[0].shape[1]
    rows, hidden = 2 * half, 2 * part
    block = 2 * TILE
    steps = hidden // TILE
    return pl.pallas_call(
        functools.partial(ffn_kernel, ring),
        grid=(steps + 2 * (hidden // block),),
        out_shape=(
            jax.ShapeDtypeStruct((half, width), F32),
            jax.ShapeDtypeStruct((half, width), BF16),
            jax.ShapeDtypeStruct((half, width), F32),
            jax.ShapeDtypeStruct((half, width), BF16),
            jax.ShapeDtypeStruct((width, 2 * hidden), BF16),
            jax.ShapeDtypeStruct((1, width), F32),
        ),
        in_specs=[VMEM] * 8,
        out_specs=(
            VMEM,
            VMEM,
            VMEM,
            VMEM,
            pl.BlockSpec((width, block), lambda j: (0, jnp.maximum(j - steps, 0))),
            pl.BlockSpec((1, width), lambda j: (0, 0)),
        ),
        scratch_shapes=[
            pltpu.VMEM((rows, hidden), BF16),
            pltpu.VMEM((rows, hidden), BF16),
            pltpu.VMEM((rows, width), F32),
            pltpu.VMEM((rows, width), F32),
            pltpu.VMEM((width, rows), BF16),
            pltpu.VMEM((width, 128), F32),
        ],
        compiler_params=pltpu.CompilerParams(vmem_limit_bytes=44 << 20),
        cost_estimate=SHORT,
        name="ffn",
    )(*normed, *grads, *inners, *outers)


def proj_grads_kernel(middle0, middle1, mixed0, mixed1, out_ref):
    half = middle0.shape[0]
    total = 0.0
    for i, middle_ref in enumerate((middle0, middle1)):
        at = slice(i * half, (i + 1) * half)
        mixed = jnp.concatenate([mixed0[:, at], mixed1[:, at]], axis=0)
        total = total + contract(middle_ref[...].T, 1, mixed, 1)
    out_ref[...] = total.astype(BF16)


def proj_grads(middle, mixed):
    shape = (middle[0].shape[1], 2 * mixed[0].shape[0])
    return pl.pallas_call(
        proj_grads_kernel,
        out_shape=jax.ShapeDtypeStruct(shape, BF16),
        in_specs=[VMEM] * 4,
        out_specs=VMEM,
        compiler_params=pltpu.CompilerParams(vmem_limit_bytes=24 << 20),
        cost_estimate=SHORT,
        name="proj_grads",
    )(*middle, *mixed)


def qkv_grads_kernel(
    ring,
    grad_ref,
    slot0_ref,
    slot1_ref,
    slot2_ref,
    slot3_ref,
    w_ref,
    proj_ref,
    out_ref,
    gain_ref,
):
    rows_dev = slot0_ref.shape[0]
    total = 0.0
    for i, slot_ref in enumerate((slot0_ref, slot1_ref, slot2_ref, slot3_ref)):
        total = total + mm(grad_ref[:, i * rows_dev : (i + 1) * rows_dev], slot_ref[...])
    gain_ref[...] = jnp.sum(total * w_ref[:, : total.shape[0]].T.astype(F32), axis=0, keepdims=True)
    both = jnp.concatenate([total.T.astype(BF16), proj_ref[...]], axis=1)
    store_ringed(out_ref, ring, 0, out_ref.shape[1], both)


def qkv_grads(ring, grad_qkv, slots, weights, proj):
    width = slots[0].shape[1]
    cols = grad_qkv.shape[0] + proj.shape[1]
    return pl.pallas_call(
        functools.partial(qkv_grads_kernel, ring),
        out_shape=(
            jax.ShapeDtypeStruct((width, cols), BF16),
            jax.ShapeDtypeStruct((1, width), F32),
        ),
        in_specs=[VMEM] * 7,
        out_specs=(VMEM, VMEM),
        compiler_params=pltpu.CompilerParams(vmem_limit_bytes=24 << 20),
        cost_estimate=SHORT,
        name="qkv_grads",
    )(grad_qkv, *slots, weights, proj)


def finish_kernel(
    pack_ref, taken_ref, last_ref, far_ref, query_ref, key_ref, value_ref, proj_ref, inner_ref, outer_ref
):
    hidden, cols = inner_ref.shape[1], query_ref.shape[1]
    pack, taken, last = pack_ref[...].astype(F32), taken_ref[...].astype(F32), last_ref[...].astype(F32)
    inner_ref[...] = pack[:, :hidden] + taken[:, :hidden]
    outer_ref[...] = pack[:, 2 * hidden : 3 * hidden] + taken[:, hidden:]
    for i, out_ref in enumerate((query_ref, key_ref, value_ref)):
        out_ref[...] = last[:, i * cols : (i + 1) * cols]
    proj_ref[...] = last[:, 3 * cols : 4 * cols] + far_ref[...].astype(F32)


def finish(pack, taken, last, far, hidden):
    rows, cols = far.shape
    shapes = [(rows, cols)] * 4 + [(rows, hidden)] * 2
    return pl.pallas_call(
        finish_kernel,
        out_shape=tuple(jax.ShapeDtypeStruct(shape, F32) for shape in shapes),
        in_specs=[VMEM] * 4,
        out_specs=(VMEM,) * 6,
        cost_estimate=SHORT,
        name="finish",
    )(pack, taken, last, far)


def bias_rows(line):
    heads = line.shape[0]
    pad = 3 * TILE
    rev = jnp.flip(line, axis=1)
    left = jnp.broadcast_to(rev[:, :1], (heads, pad))
    right = jnp.broadcast_to(rev[:, -1:], (heads, pad + 2 * TILE))
    ext = jnp.concatenate([left, rev, right], axis=1)
    begin = [pad + MAXDIST - TILE - TILE * d for d in range(-2, 3)]
    rows = [ext[:, b : b + 2 * TILE] for b in begin]
    return jnp.stack(rows, axis=1).reshape(heads * KINDS, 2 * TILE)


def line_index():
    kind = lax.broadcasted_iota(jnp.int32, (KINDS, 2 * TILE), 0) - 2
    lane = lax.broadcasted_iota(jnp.int32, (KINDS, 2 * TILE), 1)
    near = jnp.clip(TILE + TILE * kind - lane, -MAXDIST, MAXDIST)
    far = jnp.where(kind < 0, -MAXDIST, MAXDIST)
    return (jnp.where(jnp.abs(kind) == 2, far, near) + MAXDIST).reshape(KINDS * 2 * TILE)


def on_device(
    tokens,
    cotangent,
    w_query,
    w_key,
    w_value,
    w_proj,
    w_inner,
    w_outer,
    gain_attn,
    gain_ffn,
    rel_table,
    lengths,
    deal,
    buckets,
):
    rows_dev = tokens.shape[0]
    tensor_size = lax.axis_size("tensor")
    dp_size = lax.axis_size("dp")
    me = lax.axis_index("tensor")
    heads = w_query.shape[1] // HEAD_DIM
    cols = heads * HEAD_DIM
    hidden = w_inner.shape[1]
    width = tokens.shape[1]
    pair = 2 * rows_dev

    def swap(values, bit):
        return lax.ppermute(values, "tensor", [(i, i ^ bit) for i in range(tensor_size)])

    def deal_out(values):
        return lax.all_to_all(values, "dp", split_axis=0, concat_axis=0, tiled=True)

    def pick(values, order):
        return values.at[order].get(mode="promise_in_bounds", unique_indices=True)

    def sum_groups(values):
        step = 1
        while step < dp_size:
            values = values + lax.ppermute(values, "dp", [(i, i ^ step) for i in range(dp_size)])
            step *= 2
        return values

    ring = ring_order(dp_size)
    both = ("dp", "tensor")
    ring_groups = [[d * tensor_size + t for d in ring] for t in range(tensor_size)]

    def gather(values, spans):
        found = lax.all_gather(values, both, axis=0, tiled=True, axis_index_groups=ring_groups)
        return unring(found, ring, spans)

    def scatter_sum(values):
        return lax.psum_scatter(
            ringed(values, ring), both, scatter_dimension=0, tiled=True, axis_index_groups=ring_groups
        )

    own_front, own_rest = pack_weights(
        w_inner, w_query, w_key, w_value, w_proj.T, w_outer.T
    )
    own_front, tokens = after(own_front, tokens)
    ends = (3 * cols, 3 * cols + hidden, 4 * cols + hidden)
    front, outer_own, proj_own = gather(
        own_front, ((0, ends[0], False), (ends[0], ends[1], False), (ends[1], ends[2], True))
    )
    low_rows = deal_out(pick(tokens, deal))
    other_rest, low_rows = after(swap(own_rest, 2), low_rows)
    inner_own, inner_other, proj_other = gather(
        jnp.concatenate([own_rest[:, :hidden], other_rest], axis=1),
        (
            (0, hidden, False),
            (hidden, 2 * hidden, False),
            (2 * hidden, 2 * hidden + cols, True),
        ),
    )
    onehot_buckets = (
        buckets[:, None] == jnp.arange(rel_table.shape[0], dtype=jnp.int32)[None, :]
    ).astype(F32)
    head_table = lax.dynamic_slice_in_dim(rel_table, me * heads, heads, 1)
    offset_bias = jnp.dot(onehot_buckets, head_table, precision=lax.Precision.HIGHEST).T
    base = bias_rows(offset_bias)
    info = jnp.concatenate([lengths, jnp.full((1, 1), me, jnp.int32)], axis=1)

    inverse_order = (
        jnp.zeros((rows_dev,), jnp.int32).at[deal].set(jnp.arange(rows_dev, dtype=jnp.int32))
    )
    slot0 = (scaled_rows(low_rows.astype(F32)) * gain_attn).astype(BF16)
    slot2 = swap(slot0, 2)
    slot1 = swap(slot0, 1)
    slot2, front, base, info, inverse_order = after(slot2, front, base, info, inverse_order)
    slot3 = swap(slot2, 1)
    slots = (slot0, slot1, slot2, slot3)
    outer_other = swap(outer_own, 2)

    low_grads = deal_out(pick(cotangent, deal))

    mixed_far, wide_far, lse_far, qkv, keys = attend_far(info, base, front, slots)
    mixed_other = swap(mixed_far, 2)
    late_qkv, low_grads = after(qkv, low_grads)
    mixed_own, wide_own, lse_own = attend_near(info, base, late_qkv, keys, rows_dev)
    mixed_own, outer_other, inner_own = after(mixed_own, outer_other, inner_own)
    near, to_core = out_proj(mixed_own, mixed_other, proj_own, proj_other)
    middle, low_two = by_rows(
        join_kernel, "join", gain_ffn, low_rows, near, swap(to_core, 1), out=(F32, BF16)
    )

    pair_two = (low_two, swap(low_two, 1))
    pair_grads = (low_grads, swap(low_grads, 1))
    back_own, back_send, out_own, out_far, grad_pack, gain_two = ffn(
        ring, pair_two, pair_grads, (inner_own, inner_other), (outer_own, outer_other)
    )
    shard_pack = scatter_sum(grad_pack)
    grad_middle, low_middle = by_rows(
        middle_back_kernel,
        "middle_back",
        gain_ffn,
        middle,
        back_own,
        swap(back_send, 1),
        low_grads,
        out=(F32, BF16),
    )
    pair_middle = (low_middle, swap(low_middle, 1))
    grad_own, to_other = mixed_grads(pair_middle, proj_own, proj_other)

    proj_pack = proj_grads(pair_middle, (mixed_own, mixed_other))

    out_own, to_other = after(out_own, to_other)
    result_rows = (middle + out_own + swap(out_far, 1).astype(F32)).astype(BF16)
    result_rows, proj_pack = after(result_rows, proj_pack)
    back_rows = deal_out(result_rows)

    grad_far, proj_pack = after(swap(to_other, 2), proj_pack)
    grad_qkv, diagonals, far_own, far_send, near_own, near_send = attend_back(
        info,
        base,
        qkv,
        keys,
        (wide_own, wide_far),
        (lse_own, lse_far),
        (grad_own, grad_far),
        front,
        rows_dev,
    )
    far_send, back_rows = after(far_send, back_rows)
    grad_later = (far_own + swap(far_send, 1).astype(F32)).astype(BF16)
    grad_later, near_send = after(grad_later, near_send)
    later_qkv, grad_later = after(grad_qkv, grad_later)
    low_qkv_w, gain_one = qkv_grads(ring, later_qkv, slots, front, proj_pack)
    low_qkv_w, shard_pack = after(low_qkv_w, shard_pack)
    low_qkv_w, diagonals = after(low_qkv_w, diagonals)
    shard_qkv = scatter_sum(low_qkv_w)
    taken = swap(
        jnp.concatenate([shard_pack[:, hidden : 2 * hidden], shard_pack[:, 3 * hidden :]], axis=1),
        2,
    )
    offset_count = 2 * MAXDIST + 1
    onehot_line = (
        line_index()[:, None] == jnp.arange(offset_count, dtype=jnp.int32)[None, :]
    ).astype(F32)
    offset_total = jnp.dot(
        diagonals.reshape(heads, KINDS * 2 * TILE), onehot_line, precision=lax.Precision.HIGHEST
    )
    table_heads = jnp.dot(onehot_buckets.T, offset_total.T, precision=lax.Precision.HIGHEST)
    table_full = lax.dynamic_update_slice_in_dim(
        jnp.zeros(rel_table.shape, F32), table_heads, me * heads, 1
    )
    terms = [gain_one[0] / gain_attn, gain_two[0] / gain_ffn, table_full.reshape(-1)]
    small = sum_groups(jnp.concatenate(terms).reshape(-1, 128))
    grad_two_rows, small = after(swap(grad_later, 2), small)
    small = small + swap(small, 1)
    small, taken = after(small, taken)
    small = small + swap(small, 2)

    near_core = swap(near_send, 1)
    (low_grad_rows,) = by_rows(
        rows_back_kernel,
        "rows_back",
        gain_attn,
        low_rows,
        near_own,
        near_core,
        grad_two_rows,
        grad_middle,
        out=(BF16,),
        cost=pl.CostEstimate(flops=(3<<33)//2, bytes_accessed=(1<<26)//2, transcendentals=(1<<23)//2),
    )

    shard_far = swap(shard_qkv[:, 4 * cols :], 2)
    weight_shards = finish(shard_pack, taken, shard_qkv, shard_far, hidden)
    out_rows = pick(back_rows, inverse_order)
    small = small.reshape(-1)
    back_grads = deal_out(low_grad_rows)
    back_grads, out_rows, *weight_shards = after(back_grads, out_rows, *weight_shards)
    return (
        out_rows,
        pick(back_grads, inverse_order),
        *weight_shards[:3],
        weight_shards[3].T,
        weight_shards[4],
        weight_shards[5].T,
        small[:width],
        small[width : 2 * width],
        small[2 * width :].reshape(rel_table.shape),
    )


def solution(mesh):
    rows = P(("dp", "tensor"), None)
    inward, outward = P("dp", "tensor"), P("tensor", "dp")
    weights = (inward, inward, inward, outward, inward, outward)
    return jax.shard_map(
        on_device,
        mesh=mesh,
        in_specs=(rows, rows, *weights, P(), P(), P(), P("dp", None), P(("dp", "tensor")), P()),
        out_specs=(rows, rows, *weights, P(), P(), P()),
        check_vma=False,
    )
```

```python
import functools

import jax
import jax.numpy as jnp
from jax import lax
from jax.experimental import pallas as pl
from jax.experimental.pallas import tpu as pltpu
from jax.sharding import PartitionSpec as P

HEAD_DIM = 64
MAXDIST = 128
TILE = 256
KINDS = 5
EPS = 1e-06
NEG = -1000000000.0
BF16 = jnp.bfloat16
F32 = jnp.float32
VMEM = pl.BlockSpec(memory_space=pltpu.VMEM)
SMEM = pl.BlockSpec(memory_space=pltpu.SMEM)


SHORT = pl.CostEstimate(flops=1 << 20, bytes_accessed=1 << 16, transcendentals=0)


LONG = pl.CostEstimate(flops=3 << 33, bytes_accessed=1 << 26, transcendentals=1 << 23)


def mm(left, right):
    return jnp.dot(left, right, preferred_element_type=F32)


def contract(left, left_dim, right, right_dim):
    return lax.dot_general(
        left, right, (((left_dim,), (right_dim,)), ((), ())), preferred_element_type=F32
    )


def after(*values):
    return lax.optimization_barrier(values)


def ring_order(size):
    return [*range(0, size, 2), *range(size - 1, 0, -2)]


def tile_start(tile, rows_dev, me):
    per_slot = rows_dev // TILE
    return pl.multiple_of((((tile // per_slot) ^ me) * per_slot + tile % per_slot) * TILE, TILE)


def build_bias(base_ref, bias_ref, heads):
    for i in range(heads * KINDS):
        row = base_ref[i : i + 1, :]
        if i % KINDS in (0, KINDS - 1):
            bias_ref[i] = jnp.broadcast_to(row[:, :1], (TILE, TILE))
        else:
            full = jnp.broadcast_to(row, (TILE, 2 * TILE))
            bias_ref[i] = pltpu.roll(full, 0, 1, stride=1, stride_axis=0)[:, TILE:]


def deal_kernel(back, order_ref, values_ref, out_ref):
    rows = values_ref.shape[0]
    place = lax.broadcasted_iota(jnp.int32, (rows, rows), 0)
    chosen = jnp.where(place == order_ref[...], 1.0, 0.0).astype(BF16)
    dealt = mm(chosen, values_ref[...]) if back else contract(chosen, 0, values_ref[...], 0)
    out_ref[...] = dealt.astype(BF16)


def deal_rows(values, order, back):
    return pl.pallas_call(
        functools.partial(deal_kernel, back),
        out_shape=jax.ShapeDtypeStruct(values.shape, BF16),
        in_specs=[VMEM, VMEM],
        out_specs=VMEM,
        compiler_params=pltpu.CompilerParams(vmem_limit_bytes=16 << 20),
        cost_estimate=SHORT,
        name="deal_back" if back else "deal_rows",
    )(order[None], values)


def pack_kernel(inner_ref, query_ref, key_ref, value_ref, proj_ref, outer_ref, first_ref, rest_ref):
    hidden = inner_ref.shape[1]
    proj = proj_ref[...].T.astype(BF16)
    first = [query_ref[...], key_ref[...], value_ref[...], outer_ref[...]]
    first_ref[...] = jnp.concatenate([part.astype(BF16) for part in first] + [proj], axis=1)
    rest_ref[:, :hidden] = inner_ref[...].astype(BF16)
    rest_ref[:, hidden:] = proj


def pack_weights(inner, query, key, value, proj, outer):
    rows, hidden = inner.shape
    cols = query.shape[1]
    return pl.pallas_call(
        pack_kernel,
        out_shape=(
            jax.ShapeDtypeStruct((rows, 4 * cols + hidden), BF16),
            jax.ShapeDtypeStruct((rows, hidden + cols), BF16),
        ),
        in_specs=[VMEM] * 6,
        out_specs=(VMEM, VMEM),
        cost_estimate=SHORT,
        name="pack_weights",
    )(inner, query, key, value, proj, outer)


def unring_kernel(ring, spans, found_ref, *out_refs):
    size = found_ref.shape[0] // len(ring)
    for (begin, end, turned), out_ref in zip(spans, out_refs):
        if turned:
            blocks = [
                found_ref[ring.index(d) * size : (ring.index(d) + 1) * size, begin:end]
                for d in range(len(ring))
            ]
            out_ref[...] = jnp.concatenate(blocks, axis=0).T
        else:
            for p, d in enumerate(ring):
                block = found_ref[p * size : (p + 1) * size, begin:end]
                out_ref[d * size : (d + 1) * size, :] = block


def unring(found, ring, spans):
    rows = found.shape[0]
    size = rows // len(ring)
    if size % 16:
        back = [found[ring.index(d) * size :][:size] for d in range(len(ring))]
        whole = jnp.concatenate(back, axis=0)
        parts = [whole[:, begin:end] for begin, end, _ in spans]
        return [part.T if span[2] else part for part, span in zip(parts, spans)]
    shapes = [(end - begin, rows) if turned else (rows, end - begin) for begin, end, turned in spans]
    return pl.pallas_call(
        functools.partial(unring_kernel, ring, spans),
        out_shape=tuple(jax.ShapeDtypeStruct(shape, found.dtype) for shape in shapes),
        in_specs=[VMEM],
        out_specs=(VMEM,) * len(spans),
        cost_estimate=SHORT,
        name="unring",
    )(found)


def store_ringed(out_ref, ring, begin, end, values):
    size = values.shape[0] // len(ring)
    if size % 16:
        out_ref[:, begin:end] = values
    else:
        for p, d in enumerate(ring):
            out_ref[p * size : (p + 1) * size, begin:end] = values[d * size : (d + 1) * size, :]


def ringed(values, ring):
    size = values.shape[0] // len(ring)
    if size % 16 == 0:
        return values
    return jnp.concatenate([values[d * size :][:size] for d in ring], axis=0)


def segment_rows(width, first_len, start, same, other):
    shape = (HEAD_DIM, width)
    low = start + lax.broadcasted_iota(jnp.int32, shape, 1) < first_len
    row = lax.broadcasted_iota(jnp.int32, shape, 0)
    first = jnp.where(low, same, other)
    second = jnp.where(low, other, same)
    return jnp.where(row == 0, first, jnp.where(row == 1, second, 0.0)).astype(BF16)


def segment_all(rows, rows_dev, first_len, me, same, other):
    slots = rows // rows_dev
    return jnp.concatenate(
        [
            segment_rows(rows_dev, first_len, (s ^ me) * rows_dev, same, other)
            for s in range(slots)
        ],
        axis=1,
    )


def tile_range(tile, first_len, tiles):
    start = tile * TILE
    low = jnp.where(start >= first_len, first_len // TILE, 0)
    high = jnp.where(start + TILE <= first_len, (first_len + TILE - 1) // TILE, tiles)
    return low, high


def over_tiles(low, high, body, carry, sizes=(4, 2, 1)):
    at = low
    for size in sizes:
        count = (high - at) // size

        def step(i, c, at=at, size=size):
            return body(tuple(at + size * i + j for j in range(size)), c)

        carry = lax.fori_loop(0, count, step, carry)
        at = at + size * count
    return carry


def attend_rows(
    heads, rows_dev, first_slot, info_ref, qkv_ref, key_ref, out_ref, wide_ref, lse_ref, score_ref, bias_ref
):
    rows = qkv_ref.shape[1]
    cols = heads * HEAD_DIM
    first_len, me = info_ref[0, 0], info_ref[0, 2]
    tiles = rows // TILE
    per_slot = rows_dev // TILE

    def query_tile(i, carry):
        qb = ((first_slot + i // per_slot) ^ me) * per_slot + i % per_slot
        qs = pl.ds(pl.multiple_of(first_slot * rows_dev + i * TILE, TILE), TILE)
        at = pl.ds(pl.multiple_of(i * TILE, TILE), TILE)
        query_seg = segment_rows(TILE, first_len, qb * TILE, 0.0, NEG)
        queries = [
            jnp.concatenate([qkv_ref[h * HEAD_DIM : (h + 1) * HEAD_DIM, qs], query_seg], axis=0)
            for h in range(heads)
        ]
        low, high = tile_range(qb, first_len, tiles)

        def score_tiles(kbs, tops):
            kss = [pl.ds(tile_start(kb, rows_dev, me), TILE) for kb in kbs]
            kinds = [jnp.clip(kb - qb, -2, 2) + 2 for kb in kbs]
            ss = [[mm(key_ref[h, ks, :], queries[h]) for h in range(heads)] for ks in kss]
            tops = list(tops)
            for i, ks in enumerate(kss):
                for h in range(heads):
                    s = ss[i][h] + bias_ref[h * KINDS + kinds[i]]
                    score_ref[h, ks, :] = s
                    tops[h] = jnp.maximum(tops[h], jnp.max(s.reshape(TILE // 8, 8, TILE), axis=0))
            return tuple(tops)

        tops = over_tiles(low, high, score_tiles, (jnp.full((8, TILE), -3e38, F32),) * heads)
        tops = [jnp.max(t, axis=0, keepdims=True) for t in tops]

        def value_tiles(kbs, sums):
            kss = [pl.ds(tile_start(kb, rows_dev, me), TILE) for kb in kbs]
            sums = list(sums)
            ps = []
            for ks in kss:
                for h in range(heads):
                    p = jnp.exp(score_ref[h, ks, :] - tops[h])
                    total, acc = sums[h]
                    sums[h] = (total + jnp.sum(p.reshape(TILE // 8, 8, TILE), axis=0), acc)
                    ps.append(p.astype(BF16))
            for i, ks in enumerate(kss):
                for h in range(heads):
                    values = qkv_ref[2 * cols + h * HEAD_DIM : 2 * cols + (h + 1) * HEAD_DIM, ks]
                    total, acc = sums[h]
                    sums[h] = (total, acc + mm(values, ps[i * heads + h]))
            return tuple(sums)

        zero = (jnp.zeros((8, TILE), F32), jnp.zeros((HEAD_DIM, TILE), F32))
        sums = over_tiles(low, high, value_tiles, (zero,) * heads)
        for h in range(heads):
            total, acc = sums[h]
            total = jnp.sum(total, axis=0, keepdims=True)
            mixed = acc * (1.0 / total)
            hs = slice(h * HEAD_DIM, (h + 1) * HEAD_DIM)
            wide_ref[hs, at] = mixed
            out_ref[hs, at] = mixed.astype(BF16)
            lse_ref[h : h + 1, at] = tops[h] + jnp.log(total)
        return carry

    lax.fori_loop(0, tiles // 2, query_tile, 0)


def attend_far_kernel(
    heads,
    rows_dev,
    info_ref,
    base_ref,
    w_ref,
    slot0_ref,
    slot1_ref,
    slot2_ref,
    slot3_ref,
    out_ref,
    wide_ref,
    lse_ref,
    qkv_ref,
    key_ref,
    score_ref,
    bias_ref,
):
    rows = qkv_ref.shape[1]
    cols = heads * HEAD_DIM
    w_rows = w_ref[:, : 3 * cols].T
    for i, slot_ref in enumerate((slot0_ref, slot1_ref, slot2_ref, slot3_ref)):
        for begin in range(0, rows_dev, TILE):
            part = contract(w_rows, 1, slot_ref[begin : begin + TILE, :], 1)
            at = i * rows_dev + begin
            qkv_ref[:, at : at + TILE] = part.astype(BF16)
    build_bias(base_ref, bias_ref, heads)
    key_seg = segment_all(rows, rows_dev, info_ref[0, 0], info_ref[0, 2], 1.0, 0.0)
    for h in range(heads):
        key_ref[h] = jnp.concatenate(
            [qkv_ref[cols + h * HEAD_DIM : cols + (h + 1) * HEAD_DIM, :], key_seg], axis=0
        ).T
    far = rows // rows_dev // 2
    attend_rows(
        heads, rows_dev, far, info_ref, qkv_ref, key_ref, out_ref, wide_ref, lse_ref, score_ref, bias_ref
    )


def attend_near_kernel(
    heads, rows_dev, info_ref, base_ref, qkv_ref, key_ref, out_ref, wide_ref, lse_ref, score_ref, bias_ref
):
    build_bias(base_ref, bias_ref, heads)
    attend_rows(
        heads, rows_dev, 0, info_ref, qkv_ref, key_ref, out_ref, wide_ref, lse_ref, score_ref, bias_ref
    )


def attend_shapes(heads, rows):
    cols = heads * HEAD_DIM
    return (
        jax.ShapeDtypeStruct((cols, rows // 2), BF16),
        jax.ShapeDtypeStruct((cols, rows // 2), F32),
        jax.ShapeDtypeStruct((heads, rows // 2), F32),
    )


def attend_scratch(heads, rows):
    return [
        pltpu.VMEM((heads, rows, TILE), F32),
        pltpu.VMEM((heads * KINDS, TILE, TILE), F32),
    ]


def attend_far(info, base, weights, slots):
    rows_dev = slots[0].shape[0]
    rows = rows_dev * len(slots)
    cols = weights.shape[1] // 3
    heads = cols // HEAD_DIM
    return pl.pallas_call(
        functools.partial(attend_far_kernel, heads, rows_dev),
        out_shape=attend_shapes(heads, rows)
        + (
            jax.ShapeDtypeStruct((3 * cols, rows), BF16),
            jax.ShapeDtypeStruct((heads, rows, 2 * HEAD_DIM), BF16),
        ),
        in_specs=[SMEM] + [VMEM] * 6,
        out_specs=(VMEM,) * 5,
        scratch_shapes=attend_scratch(heads, rows),
        compiler_params=pltpu.CompilerParams(vmem_limit_bytes=58 << 20),
        cost_estimate=SHORT,
        name="attend_far",
    )(info, base, weights, *slots)


def attend_near(info, base, qkv, keys, rows_dev):
    heads, rows = keys.shape[:2]
    return pl.pallas_call(
        functools.partial(attend_near_kernel, heads, rows_dev),
        out_shape=attend_shapes(heads, rows),
        in_specs=[SMEM] + [VMEM] * 3,
        out_specs=(VMEM,) * 3,
        scratch_shapes=attend_scratch(heads, rows),
        compiler_params=pltpu.CompilerParams(vmem_limit_bytes=58 << 20),
        cost_estimate=SHORT,
        name="attend_near",
    )(info, base, qkv, keys)


def diagonal_sums(values):
    values = jnp.concatenate([jnp.zeros_like(values), values], axis=1)
    count = TILE
    while count > 1:
        count //= 2
        values = values[:count] + pltpu.roll(values[count:], 2 * TILE - count, 1)
    return values


def grad_rows_to(own_ref, send_ref, first_slot, grad_ref, w_ref):
    rows_dev = own_ref.shape[0]
    for slot, out_ref in ((first_slot + 1, send_ref), (first_slot, own_ref)):
        for begin in range(0, rows_dev, TILE):
            at = slot * rows_dev + begin
            part = contract(grad_ref[:, at : at + TILE], 0, w_ref[...], 1)
            out_ref[begin : begin + TILE, :] = part.astype(out_ref.dtype)


def attend_back_kernel(
    heads,
    rows_dev,
    info_ref,
    base_ref,
    qkv_ref,
    key_ref,
    wide0_ref,
    wide1_ref,
    lse0_ref,
    lse1_ref,
    grad0_ref,
    grad1_ref,
    w_ref,
    out_ref,
    diag_ref,
    far_own_ref,
    far_send_ref,
    near_own_ref,
    near_send_ref,
    lse_ref,
    inner_ref,
    grad_ref,
    query_ref,
    value_rows,
    query_rows,
    grad_rows,
    key_acc,
    value_acc,
    bias_ref,
    table_ref,
):
    rows = qkv_ref.shape[1]
    cols = heads * HEAD_DIM
    first_len, me = info_ref[0, 0], info_ref[0, 2]
    tiles = rows // TILE
    build_bias(base_ref, bias_ref, heads)
    query_seg = segment_all(rows, rows_dev, first_len, me, 0.0, NEG)
    q_of = [slice(h * HEAD_DIM, (h + 1) * HEAD_DIM) for h in range(heads)]
    k_of = [slice(cols + h * HEAD_DIM, cols + (h + 1) * HEAD_DIM) for h in range(heads)]
    v_of = [slice(2 * cols + h * HEAD_DIM, 2 * cols + (h + 1) * HEAD_DIM) for h in range(heads)]
    lse_ref[:, : rows // 2] = lse0_ref[...]
    lse_ref[:, rows // 2 :] = lse1_ref[...]
    grad_ref[:, : rows // 2] = grad0_ref[...]
    grad_ref[:, rows // 2 :] = grad1_ref[...]
    for h in range(heads):
        queries = qkv_ref[q_of[h], :]
        query_ref[h] = jnp.concatenate([queries, query_seg], axis=0)
        query_rows[h] = queries.T
        value_rows[h] = qkv_ref[v_of[h], :].T
        grad_rows[h] = grad_ref[q_of[h], :].T
        for half, wide_ref in ((0, wide0_ref), (1, wide1_ref)):
            at = slice(half * rows // 2, (half + 1) * rows // 2)
            terms = grad_ref[q_of[h], at].astype(F32) * wide_ref[q_of[h], :]
            inner_ref[h : h + 1, at] = jnp.sum(terms, axis=0, keepdims=True)
    key_acc[...] = jnp.zeros_like(key_acc)
    value_acc[...] = jnp.zeros_like(value_acc)
    table_ref[...] = jnp.zeros_like(table_ref)

    def query_tile(qb, carry):
        qs = pl.ds(tile_start(qb, rows_dev, me), TILE)
        low, high = tile_range(qb, first_len, tiles)
        grads = [grad_ref[q_of[h], qs] for h in range(heads)]
        inner = [inner_ref[h : h + 1, qs] for h in range(heads)]
        lse = [lse_ref[h : h + 1, qs] for h in range(heads)]

        def tiles_at(kbs, sums):
            kss = [pl.ds(tile_start(kb, rows_dev, me), TILE) for kb in kbs]
            kinds = [jnp.clip(kb - qb, -2, 2) + 2 for kb in kbs]
            ss = [[mm(key_ref[h, ks, :], query_ref[h, :, qs]) for h in range(heads)] for ks in kss]
            dps = [[mm(value_rows[h, ks, :], grads[h]) for h in range(heads)] for ks in kss]
            lows = []
            for i in range(len(kbs)):
                for h in range(heads):
                    p = jnp.exp(ss[i][h] + bias_ref[h * KINDS + kinds[i]] - lse[h])
                    ds = p * (dps[i][h] - inner[h])
                    table_ref[h * KINDS + kinds[i]] += ds
                    lows.append((p.astype(BF16), ds.astype(BF16)))
            sums = list(sums)
            for i, ks in enumerate(kss):
                for h in range(heads):
                    low_p, low_ds = lows[i * heads + h]
                    value_acc[h, ks, :] += mm(low_p, grad_rows[h, qs, :])
                    key_acc[h, ks, :] += mm(low_ds, query_rows[h, qs, :])
                    sums[h] = sums[h] + mm(qkv_ref[k_of[h], ks], low_ds)
            return tuple(sums)

        sums = tuple(jnp.zeros((HEAD_DIM, TILE), F32) for _ in range(heads))
        sums = over_tiles(low, high, tiles_at, sums, (2, 1))
        for h in range(heads):
            out_ref[q_of[h], qs] = sums[h].astype(BF16)
        return carry

    lax.fori_loop(0, tiles, query_tile, 0)
    for h in range(heads):
        out_ref[k_of[h], :] = key_acc[h].astype(BF16).T
        out_ref[v_of[h], :] = value_acc[h].astype(BF16).T
    grad_rows_to(far_own_ref, far_send_ref, rows // rows_dev // 2, out_ref, w_ref)
    grad_rows_to(near_own_ref, near_send_ref, 0, out_ref, w_ref)
    for i in range(heads * KINDS):
        if i % KINDS in (0, KINDS - 1):
            total = jnp.sum(table_ref[i], axis=0, keepdims=True)
            diag_ref[i : i + 1, :] = jnp.concatenate([total, jnp.zeros_like(total)], axis=1)
        else:
            diag_ref[i : i + 1, :] = diagonal_sums(table_ref[i])


def attend_back(info, base, qkv, keys, wide, lse, grad, weights, rows_dev):
    rows = qkv.shape[1]
    width = weights.shape[0]
    heads = qkv.shape[0] // (3 * HEAD_DIM)
    cols = heads * HEAD_DIM
    return pl.pallas_call(
        functools.partial(attend_back_kernel, heads, rows_dev),
        out_shape=(
            jax.ShapeDtypeStruct((3 * cols, rows), BF16),
            jax.ShapeDtypeStruct((heads * KINDS, 2 * TILE), F32),
            *[jax.ShapeDtypeStruct((rows_dev, width), BF16)] * 4,
        ),
        in_specs=[SMEM] + [VMEM] * 10,
        out_specs=(VMEM,) * 6,
        scratch_shapes=[
            pltpu.VMEM((heads, rows), F32),
            pltpu.VMEM((heads, rows), F32),
            pltpu.VMEM((cols, rows), BF16),
            pltpu.VMEM((heads, 2 * HEAD_DIM, rows), BF16),
            pltpu.VMEM((heads, rows, HEAD_DIM), BF16),
            pltpu.VMEM((heads, rows, HEAD_DIM), BF16),
            pltpu.VMEM((heads, rows, HEAD_DIM), BF16),
            pltpu.VMEM((heads, rows, HEAD_DIM), F32),
            pltpu.VMEM((heads, rows, HEAD_DIM), F32),
            pltpu.VMEM((heads * KINDS, TILE, TILE), F32),
            pltpu.VMEM((heads * KINDS, TILE, TILE), F32),
        ],
        compiler_params=pltpu.CompilerParams(vmem_limit_bytes=58 << 20),
        cost_estimate=LONG,
        name="attend_back",
    )(info, base, qkv, keys, *wide, *lse, *grad, weights)


def scaled_rows(values):
    return values * lax.rsqrt(jnp.mean(values * values, axis=-1, keepdims=True) + EPS)


def join_kernel(rows_ref, near_ref, far_ref, gain_ref, middle_ref, low_ref):
    for rs in row_blocks(rows_ref.shape[0]):
        middle = rows_ref[rs, :].astype(F32) + near_ref[rs, :] + far_ref[rs, :].astype(F32)
        middle_ref[rs, :] = middle
        low_ref[rs, :] = (scaled_rows(middle) * gain_ref[...]).astype(BF16)


def row_blocks(rows):
    return [slice(begin, begin + TILE // 4) for begin in range(0, rows, TILE // 4)]


def norm_back_rows(values, upstream, gain):
    scale = lax.rsqrt(jnp.mean(values * values, axis=-1, keepdims=True) + EPS)
    normed = values * scale
    scaled = upstream * gain
    inner = jnp.mean(scaled * normed, axis=-1, keepdims=True)
    return scale * (scaled - normed * inner)


def middle_back_kernel(middle_ref, near_ref, far_ref, grads_ref, gain_ref, low_ref):
    for rs in row_blocks(middle_ref.shape[0]):
        upstream = near_ref[rs, :].astype(F32) + far_ref[rs, :].astype(F32)
        back = norm_back_rows(middle_ref[rs, :], upstream, gain_ref[...])
        low_ref[rs, :] = (grads_ref[rs, :].astype(F32) + back).astype(BF16)


def rows_back_kernel(rows_ref, near_ref, core_ref, far_ref, after_ref, gain_ref, low_ref):
    for rs in row_blocks(rows_ref.shape[0]):
        upstream = near_ref[rs, :].astype(F32) + core_ref[rs, :].astype(F32)
        upstream = upstream + far_ref[rs, :].astype(F32)
        back = norm_back_rows(rows_ref[rs, :].astype(F32), upstream, gain_ref[...])
        low_ref[rs, :] = (after_ref[rs, :].astype(F32) + back).astype(BF16)


def by_rows(kernel, name, gain, *operands, out, cost=SHORT):
    shape = operands[0].shape
    return pl.pallas_call(
        kernel,
        out_shape=tuple(jax.ShapeDtypeStruct(shape, kind) for kind in out),
        in_specs=[VMEM] * (len(operands) + 1),
        out_specs=(VMEM,) * len(out),
        compiler_params=pltpu.CompilerParams(vmem_limit_bytes=16 << 20),
        cost_estimate=cost,
        name=name,
    )(*operands, gain[None])


def out_proj_kernel(own_ref, other_ref, w_own_ref, w_other_ref, near_ref, send_ref):
    half = near_ref.shape[0]
    for begin in range(0, 2 * half, TILE):
        part = contract(own_ref[:, begin : begin + TILE], 0, w_own_ref[...], 0)
        part = part + contract(other_ref[:, begin : begin + TILE], 0, w_other_ref[...], 0)
        if begin < half:
            near_ref[begin : begin + TILE, :] = part
        else:
            send_ref[begin - half : begin - half + TILE, :] = part.astype(BF16)


def out_proj(own, other, w_own, w_other):
    half, width = own.shape[1] // 2, w_own.shape[1]
    return pl.pallas_call(
        out_proj_kernel,
        out_shape=(
            jax.ShapeDtypeStruct((half, width), F32),
            jax.ShapeDtypeStruct((half, width), BF16),
        ),
        in_specs=[VMEM] * 4,
        out_specs=(VMEM, VMEM),
        compiler_params=pltpu.CompilerParams(vmem_limit_bytes=16 << 20),
        cost_estimate=SHORT,
        name="out_proj",
    )(own, other, w_own, w_other)


def mixed_grads_kernel(middle0, middle1, w_own_ref, w_other_ref, own_ref, send_ref):
    half = middle0.shape[0]
    for w_ref, out_ref in ((w_other_ref, send_ref), (w_own_ref, own_ref)):
        for i, middle_ref in enumerate((middle0, middle1)):
            part = contract(w_ref[...], 1, middle_ref[...], 1)
            out_ref[:, i * half : (i + 1) * half] = part.astype(BF16)


def mixed_grads(middle, w_own, w_other):
    shape = jax.ShapeDtypeStruct((w_own.shape[0], 2 * middle[0].shape[0]), BF16)
    return pl.pallas_call(
        mixed_grads_kernel,
        out_shape=(shape, shape),
        in_specs=[VMEM] * 4,
        out_specs=(VMEM, VMEM),
        compiler_params=pltpu.CompilerParams(vmem_limit_bytes=16 << 20),
        cost_estimate=SHORT,
        name="mixed_grads",
    )(*middle, w_own, w_other)


def ffn_kernel(
    ring,
    normed0,
    normed1,
    grad0,
    grad1,
    inner0,
    inner1,
    outer0,
    outer1,
    own_ref,
    send_ref,
    out_own_ref,
    out_send_ref,
    grads_ref,
    gain_ref,
    hid_ref,
    pre_ref,
    acc_ref,
    out_acc_ref,
    left_ref,
    gain_acc,
):
    half, width = own_ref.shape
    part = inner0.shape[1]
    block = grads_ref.shape[1]
    per_part = part // TILE
    steps = 2
    sweeps = 2 * part // block
    step = pl.program_id(0)
    root, cubic = 0.7978845608028654, 0.044715
    places = [
        (normed_ref, grad_ref, begin, i * half + begin)
        for i, (normed_ref, grad_ref) in enumerate(((normed0, grad0), (normed1, grad1)))
        for begin in range(0, half, TILE)
    ]
    weights = ((inner0, outer0), (inner1, outer1))

    def products(inner_ref, outer_ref, index, place):
        normed_ref, grad_ref, begin, _ = place
        rs, js = slice(begin, begin + TILE), slice(index * TILE, (index + 1) * TILE)
        return mm(normed_ref[rs, :], inner_ref[:, js]), mm(grad_ref[rs, :], outer_ref[:, js])

    def hidden_part(inner_ref, outer_ref, offset):
        work = [(index, place) for index in range(per_part) for place in places]
        ahead = products(inner_ref, outer_ref, *work[0])
        for n, (index, place) in enumerate(work):
            a, dh = ahead
            if n + 1 < len(work):
                ahead = products(inner_ref, outer_ref, *work[n + 1])
            rs = slice(place[3], place[3] + TILE)
            to = slice(offset + index * TILE, offset + (index + 1) * TILE)
            square = a * a
            t = jnp.tanh(a * (root + (root * cubic) * square))
            half_a = 0.5 * a
            cdf = 0.5 + 0.5 * t
            slope = cdf + half_a * (1.0 - t * t) * (root + (3.0 * root * cubic) * square)
            hid_ref[rs, to] = (a * cdf).astype(BF16)
            pre_ref[rs, to] = (dh * slope).astype(BF16)

    def rows_out(kept_ref, w_ref, offset, sum_ref, near_ref, far_ref):
        for _, _, _, at in places:
            rs = slice(at, at + TILE)
            back = contract(kept_ref[rs, offset : offset + part], 1, w_ref[...], 1)
            if offset == 0:
                sum_ref[rs, :] = back
            elif at < half:
                near_ref[rs, :] = (sum_ref[rs, :] + back).astype(BF16)
            else:
                far_ref[at - half : at - half + TILE, :] = (sum_ref[rs, :] + back).astype(BF16)

    for i, (inner_ref, outer_ref) in enumerate(weights):

        @pl.when(step == i)
        def _(inner_ref=inner_ref, outer_ref=outer_ref, offset=i * part):
            hidden_part(inner_ref, outer_ref, offset)
            rows_out(pre_ref, inner_ref, offset, acc_ref, own_ref, send_ref)
            rows_out(hid_ref, outer_ref, offset, out_acc_ref, out_own_ref, out_send_ref)

    def load(first_ref, second_ref):
        left_ref[:, :half] = first_ref[...].T
        left_ref[:, half:] = second_ref[...].T

    for i in range(sweeps):

        @pl.when(step == steps + i)
        def _(i=i):
            if i == 0:
                load(normed0, normed1)
            values = mm(left_ref[...], pre_ref[:, i * block : (i + 1) * block])
            store_ringed(grads_ref, ring, 0, block, values.astype(BF16))
            lanes = gain_acc.shape[1]
            total = jnp.zeros(gain_acc.shape, F32) if i == 0 else gain_acc[...]
            for b in range(0, block, lanes):
                at = i * block + b
                w_ref = inner0 if at < part else inner1
                w = w_ref[:, at % part : at % part + lanes].astype(F32)
                total = total + values[:, b : b + lanes] * w
            gain_acc[...] = total
            if i == sweeps - 1:
                gain_ref[...] = jnp.sum(total.T, axis=0, keepdims=True)

        @pl.when(step == steps + sweeps + i)
        def _(i=i):
            if i == 0:
                load(grad0, grad1)
            values = mm(left_ref[...], hid_ref[:, i * block : (i + 1) * block])
            store_ringed(grads_ref, ring, 0, block, values.astype(BF16))


def ffn(ring, normed, grads, inners, outers):
    half, width = normed[0].shape
    part = inners[0].shape[1]
    rows, hidden = 2 * half, 2 * part
    block = 2 * TILE
    steps = 2
    return pl.pallas_call(
        functools.partial(ffn_kernel, ring),
        grid=(steps + 2 * (hidden // block),),
        out_shape=(
            *[pltpu.HBM((half, width), BF16)] * 4,
            pltpu.HBM((width, 2 * hidden), BF16),
            pltpu.HBM((1, width), F32),
        ),
        in_specs=[VMEM] * 8,
        out_specs=(
            VMEM,
            VMEM,
            VMEM,
            VMEM,
            pl.BlockSpec((width, block), lambda j: (0, jnp.maximum(j - steps, 0))),
            pl.BlockSpec((1, width), lambda j: (0, 0)),
        ),
        scratch_shapes=[
            pltpu.VMEM((rows, hidden), BF16),
            pltpu.VMEM((rows, hidden), BF16),
            pltpu.VMEM((rows, width), F32),
            pltpu.VMEM((rows, width), F32),
            pltpu.VMEM((width, rows), BF16),
            pltpu.VMEM((width, 128), F32),
        ],
        compiler_params=pltpu.CompilerParams(vmem_limit_bytes=44 << 20),
        cost_estimate=SHORT,
        name="ffn",
    )(*normed, *grads, *inners, *outers)


def proj_grads_kernel(middle0, middle1, mixed0, mixed1, out_ref):
    half = middle0.shape[0]
    total = 0.0
    for i, middle_ref in enumerate((middle0, middle1)):
        at = slice(i * half, (i + 1) * half)
        mixed = jnp.concatenate([mixed0[:, at], mixed1[:, at]], axis=0)
        total = total + contract(middle_ref[...].T, 1, mixed, 1)
    out_ref[...] = total.astype(BF16)


def proj_grads(middle, mixed):
    shape = (middle[0].shape[1], 2 * mixed[0].shape[0])
    return pl.pallas_call(
        proj_grads_kernel,
        out_shape=jax.ShapeDtypeStruct(shape, BF16),
        in_specs=[VMEM] * 4,
        out_specs=VMEM,
        compiler_params=pltpu.CompilerParams(vmem_limit_bytes=24 << 20),
        cost_estimate=SHORT,
        name="proj_grads",
    )(*middle, *mixed)


def qkv_grads_kernel(
    ring,
    grad_ref,
    slot0_ref,
    slot1_ref,
    slot2_ref,
    slot3_ref,
    w_ref,
    proj_ref,
    out_ref,
    gain_ref,
):
    rows_dev = slot0_ref.shape[0]
    total = 0.0
    for i, slot_ref in enumerate((slot0_ref, slot1_ref, slot2_ref, slot3_ref)):
        total = total + mm(grad_ref[:, i * rows_dev : (i + 1) * rows_dev], slot_ref[...])
    gain_ref[...] = jnp.sum(total * w_ref[:, : total.shape[0]].T.astype(F32), axis=0, keepdims=True)
    both = jnp.concatenate([total.T.astype(BF16), proj_ref[...]], axis=1)
    store_ringed(out_ref, ring, 0, out_ref.shape[1], both)


def qkv_grads(ring, grad_qkv, slots, weights, proj):
    width = slots[0].shape[1]
    cols = grad_qkv.shape[0] + proj.shape[1]
    return pl.pallas_call(
        functools.partial(qkv_grads_kernel, ring),
        out_shape=(
            jax.ShapeDtypeStruct((width, cols), BF16),
            jax.ShapeDtypeStruct((1, width), F32),
        ),
        in_specs=[VMEM] * 7,
        out_specs=(VMEM, VMEM),
        compiler_params=pltpu.CompilerParams(vmem_limit_bytes=58 << 20),
        cost_estimate=SHORT,
        name="qkv_grads",
    )(grad_qkv, *slots, weights, proj)


def finish_kernel(pack_ref, taken_ref, inner_ref, outer_ref):
    hidden = inner_ref.shape[1]
    pack, taken = pack_ref[...].astype(F32), taken_ref[...].astype(F32)
    inner_ref[...] = pack[:, :hidden] + taken[:, :hidden]
    outer_ref[...] = pack[:, 2 * hidden : 3 * hidden] + taken[:, hidden:]


def finish(pack, taken):
    shape = jax.ShapeDtypeStruct((taken.shape[0], taken.shape[1] // 2), F32)
    return pl.pallas_call(
        finish_kernel,
        out_shape=(shape, shape),
        in_specs=[VMEM] * 2,
        out_specs=(VMEM,) * 2,
        cost_estimate=SHORT,
        name="finish",
    )(pack, taken)


def finish_last_kernel(last_ref, far_ref, query_ref, key_ref, value_ref, proj_ref):
    cols = query_ref.shape[1]
    last = last_ref[...].astype(F32)
    for i, out_ref in enumerate((query_ref, key_ref, value_ref)):
        out_ref[...] = last[:, i * cols : (i + 1) * cols]
    proj_ref[...] = (last[:, 3 * cols : 4 * cols] + far_ref[...].astype(F32)).T


def finish_last(last, far):
    rows, cols = far.shape
    shapes = [(rows, cols)] * 3 + [(cols, rows)]
    return pl.pallas_call(
        finish_last_kernel,
        out_shape=tuple(jax.ShapeDtypeStruct(shape, F32) for shape in shapes),
        in_specs=[VMEM] * 2,
        out_specs=(VMEM,) * 4,
        cost_estimate=SHORT,
        name="finish_last",
    )(last, far)


def bias_rows(line):
    heads = line.shape[0]
    pad = 3 * TILE
    rev = jnp.flip(line, axis=1)
    left = jnp.broadcast_to(rev[:, :1], (heads, pad))
    right = jnp.broadcast_to(rev[:, -1:], (heads, pad + 2 * TILE))
    ext = jnp.concatenate([left, rev, right], axis=1)
    begin = [pad + MAXDIST - TILE - TILE * d for d in range(-2, 3)]
    rows = [ext[:, b : b + 2 * TILE] for b in begin]
    return jnp.stack(rows, axis=1).reshape(heads * KINDS, 2 * TILE)


def line_index():
    kind = lax.broadcasted_iota(jnp.int32, (KINDS, 2 * TILE), 0) - 2
    lane = lax.broadcasted_iota(jnp.int32, (KINDS, 2 * TILE), 1)
    near = jnp.clip(TILE + TILE * kind - lane, -MAXDIST, MAXDIST)
    far = jnp.where(kind < 0, -MAXDIST, MAXDIST)
    return (jnp.where(jnp.abs(kind) == 2, far, near) + MAXDIST).reshape(KINDS * 2 * TILE)


def on_device(
    tokens,
    cotangent,
    w_query,
    w_key,
    w_value,
    w_proj,
    w_inner,
    w_outer,
    gain_attn,
    gain_ffn,
    rel_table,
    lengths,
    deal,
    buckets,
):
    rows_dev = tokens.shape[0]
    tensor_size = lax.axis_size("tensor")
    dp_size = lax.axis_size("dp")
    me = lax.axis_index("tensor")
    heads = w_query.shape[1] // HEAD_DIM
    cols = heads * HEAD_DIM
    hidden = w_inner.shape[1]
    width = tokens.shape[1]
    pair = 2 * rows_dev

    def swap(values, bit):
        return lax.ppermute(values, "tensor", [(i, i ^ bit) for i in range(tensor_size)])

    def deal_out(values):
        return lax.all_to_all(values, "dp", split_axis=0, concat_axis=0, tiled=True)

    def sum_groups(values):
        step = 1
        while step < dp_size:
            values = values + lax.ppermute(values, "dp", [(i, i ^ step) for i in range(dp_size)])
            step *= 2
        return values

    ring = ring_order(dp_size)
    both = ("dp", "tensor")
    ring_groups = [[d * tensor_size + t for d in ring] for t in range(tensor_size)]

    def gather(values, spans):
        found = lax.all_gather(values, both, axis=0, tiled=True, axis_index_groups=ring_groups)
        return unring(found, ring, spans)

    def scatter_sum(values):
        return lax.psum_scatter(
            ringed(values, ring), both, scatter_dimension=0, tiled=True, axis_index_groups=ring_groups
        )

    own_front, own_rest = pack_weights(
        w_inner, w_query, w_key, w_value, w_proj, w_outer.T
    )
    own_front, tokens = after(own_front, tokens)
    ends = (3 * cols, 3 * cols + hidden, 4 * cols + hidden)
    front, outer_own, proj_own = gather(
        own_front, ((0, ends[0], False), (ends[0], ends[1], False), (ends[1], ends[2], True))
    )
    low_rows = deal_out(tokens.at[deal].get(mode="promise_in_bounds", unique_indices=True))
    other_rest, low_rows = after(swap(own_rest, 2), low_rows)
    inner_own, inner_other, proj_other = gather(
        jnp.concatenate([own_rest[:, :hidden], other_rest], axis=1),
        (
            (0, hidden, False),
            (hidden, 2 * hidden, False),
            (2 * hidden, 2 * hidden + cols, True),
        ),
    )
    onehot_buckets = (
        buckets[:, None] == jnp.arange(rel_table.shape[0], dtype=jnp.int32)[None, :]
    ).astype(F32)
    head_table = lax.dynamic_slice_in_dim(rel_table, me * heads, heads, 1)
    offset_bias = jnp.dot(onehot_buckets, head_table, precision=lax.Precision.HIGHEST).T
    base = bias_rows(offset_bias)
    info = jnp.concatenate([lengths, jnp.full((1, 1), me, jnp.int32)], axis=1)

    slot0 = (scaled_rows(low_rows.astype(F32)) * gain_attn).astype(BF16)
    slot2 = swap(slot0, 2)
    slot1 = swap(slot0, 1)
    slot2, front, base, info = after(slot2, front, base, info)
    slot3 = swap(slot2, 1)
    slots = (slot0, slot1, slot2, slot3)
    outer_other = swap(outer_own, 2)

    low_grads = deal_out(cotangent.at[deal].get(mode="promise_in_bounds", unique_indices=True))

    mixed_far, wide_far, lse_far, qkv, keys = attend_far(info, base, front, slots)
    mixed_other = swap(mixed_far, 2)
    late_qkv, low_grads = after(qkv, low_grads)
    mixed_own, wide_own, lse_own = attend_near(info, base, late_qkv, keys, rows_dev)
    mixed_own, outer_other, inner_own = after(mixed_own, outer_other, inner_own)
    near, to_core = out_proj(mixed_own, mixed_other, proj_own, proj_other)
    middle, low_two = by_rows(
        join_kernel, "join", gain_ffn, low_rows, near, swap(to_core, 1), out=(F32, BF16)
    )

    pair_two = (low_two, swap(low_two, 1))
    pair_grads = (low_grads, swap(low_grads, 1))
    back_own, back_send, out_own, out_far, grad_pack, gain_two = ffn(
        ring, pair_two, pair_grads, (inner_own, inner_other), (outer_own, outer_other)
    )
    shard_pack = scatter_sum(grad_pack)
    (low_middle,) = by_rows(
        middle_back_kernel,
        "middle_back",
        gain_ffn,
        middle,
        back_own,
        swap(back_send, 1),
        low_grads,
        out=(BF16,),
    )
    pair_middle = (low_middle, swap(low_middle, 1))
    grad_own, to_other = mixed_grads(pair_middle, proj_own, proj_other)

    proj_pack = proj_grads(pair_middle, (mixed_own, mixed_other))

    out_own, to_other = after(out_own, to_other)
    result_rows = (middle + out_own.astype(F32) + swap(out_far, 1).astype(F32)).astype(BF16)
    result_rows, proj_pack = after(result_rows, proj_pack)
    back_rows = deal_out(result_rows)

    grad_far, proj_pack = after(swap(to_other, 2), proj_pack)
    grad_qkv, diagonals, far_own, far_send, near_own, near_send = attend_back(
        info,
        base,
        qkv,
        keys,
        (wide_own, wide_far),
        (lse_own, lse_far),
        (grad_own, grad_far),
        front,
        rows_dev,
    )
    far_send, back_rows = after(far_send, back_rows)
    grad_later = (far_own.astype(F32) + swap(far_send, 1).astype(F32)).astype(BF16)
    offset_count = 2 * MAXDIST + 1
    onehot_line = (
        line_index()[:, None] == jnp.arange(offset_count, dtype=jnp.int32)[None, :]
    ).astype(F32)
    offset_total = jnp.dot(
        diagonals.reshape(heads, KINDS * 2 * TILE), onehot_line, precision=lax.Precision.HIGHEST
    )
    table_heads = jnp.dot(onehot_buckets.T, offset_total.T, precision=lax.Precision.HIGHEST)
    table_full = lax.dynamic_update_slice_in_dim(
        jnp.zeros(rel_table.shape, F32), table_heads, me * heads, 1
    )
    grad_later, near_send, table_full = after(grad_later, near_send, table_full)
    later_qkv, grad_later = after(grad_qkv, grad_later)
    low_qkv_w, gain_one = qkv_grads(ring, later_qkv, slots, front, proj_pack)
    low_qkv_w, shard_pack = after(low_qkv_w, shard_pack)
    shard_qkv = scatter_sum(low_qkv_w)
    taken = swap(
        jnp.concatenate([shard_pack[:, hidden : 2 * hidden], shard_pack[:, 3 * hidden :]], axis=1),
        2,
    )
    terms = [gain_one[0] / gain_attn, gain_two[0] / gain_ffn, table_full.reshape(-1)]
    small = sum_groups(jnp.concatenate(terms).reshape(-1, 128))
    grad_two_rows, small = after(swap(grad_later, 2), small)
    small = small + swap(small, 1)
    small, taken = after(small, taken)
    small = small + swap(small, 2)

    near_core = swap(near_send, 1)
    (low_grad_rows,) = by_rows(
        rows_back_kernel,
        "rows_back",
        gain_attn,
        low_rows,
        near_own,
        near_core,
        grad_two_rows,
        low_middle,
        out=(BF16,),
        cost=pl.CostEstimate(flops=(3<<33)//2, bytes_accessed=(1<<26)//2, transcendentals=(1<<23)//2),
    )

    shard_far = swap(shard_qkv[:, 4 * cols :], 2)
    weight_shards = [*finish_last(shard_qkv, shard_far), *finish(shard_pack, taken)]
    out_rows = deal_rows(back_rows, deal, True)
    small = small.reshape(-1)
    back_grads = deal_out(low_grad_rows)
    back_grads, out_rows, *weight_shards = after(back_grads, out_rows, *weight_shards)
    return (
        out_rows,
        deal_rows(back_grads, deal, True),
        *weight_shards[:3],
        *weight_shards[3:5],
        weight_shards[5].T,
        small[:width],
        small[width : 2 * width],
        small[2 * width :].reshape(rel_table.shape),
    )


def solution(mesh):
    rows = P(("dp", "tensor"), None)
    inward, outward = P("dp", "tensor"), P("tensor", "dp")
    weights = (inward, inward, inward, outward, inward, outward)
    return jax.shard_map(
        on_device,
        mesh=mesh,
        in_specs=(rows, rows, *weights, P(), P(), P(), P("dp", None), P(("dp", "tensor")), P()),
        out_specs=(rows, rows, *weights, P(), P(), P()),
        check_vma=False,
    )
```

```python
import functools

import jax
import jax.numpy as jnp
from jax import lax
from jax.experimental import pallas as pl
from jax.experimental.pallas import tpu as pltpu
from jax.sharding import PartitionSpec as P

HEAD_DIM = 64
MAXDIST = 128
TILE = 256
KINDS = 5
EPS = 1e-06
NEG = -1000000000.0
BF16 = jnp.bfloat16
F32 = jnp.float32
VMEM = pl.BlockSpec(memory_space=pltpu.VMEM)
SMEM = pl.BlockSpec(memory_space=pltpu.SMEM)


SHORT = pl.CostEstimate(flops=1 << 20, bytes_accessed=1 << 16, transcendentals=0)


LONG = pl.CostEstimate(flops=3 << 33, bytes_accessed=1 << 26, transcendentals=1 << 23)


def mm(left, right):
    return jnp.dot(left, right, preferred_element_type=F32)


def contract(left, left_dim, right, right_dim):
    return lax.dot_general(
        left, right, (((left_dim,), (right_dim,)), ((), ())), preferred_element_type=F32
    )


def after(*values):
    return lax.optimization_barrier(values)


def ring_order(size):
    return [*range(0, size, 2), *range(size - 1, 0, -2)]


def tile_start(tile, rows_dev, me):
    per_slot = rows_dev // TILE
    return pl.multiple_of((((tile // per_slot) ^ me) * per_slot + tile % per_slot) * TILE, TILE)


def build_bias(base_ref, bias_ref, heads):
    for i in range(heads * KINDS):
        row = base_ref[i : i + 1, :]
        if i % KINDS in (0, KINDS - 1):
            bias_ref[i] = jnp.broadcast_to(row[:, :1], (TILE, TILE))
        else:
            full = jnp.broadcast_to(row, (TILE, 2 * TILE))
            bias_ref[i] = pltpu.roll(full, 0, 1, stride=1, stride_axis=0)[:, TILE:]


def deal_kernel(back, order_ref, values_ref, out_ref):
    rows = values_ref.shape[0]
    place = lax.broadcasted_iota(jnp.int32, (rows, rows), 0)
    chosen = jnp.where(place == order_ref[...], 1.0, 0.0).astype(BF16)
    dealt = mm(chosen, values_ref[...]) if back else contract(chosen, 0, values_ref[...], 0)
    out_ref[...] = dealt.astype(BF16)


def deal_rows(values, order, back):
    return pl.pallas_call(
        functools.partial(deal_kernel, back),
        out_shape=jax.ShapeDtypeStruct(values.shape, BF16),
        in_specs=[VMEM, VMEM],
        out_specs=VMEM,
        compiler_params=pltpu.CompilerParams(vmem_limit_bytes=16 << 20),
        cost_estimate=SHORT,
        name="deal_back" if back else "deal_rows",
    )(order[None], values)


def pack_kernel(inner_ref, query_ref, key_ref, value_ref, proj_ref, outer_ref, first_ref, rest_ref):
    hidden = inner_ref.shape[1]
    proj = proj_ref[...].T.astype(BF16)
    first = [query_ref[...], key_ref[...], value_ref[...], outer_ref[...]]
    first_ref[...] = jnp.concatenate([part.astype(BF16) for part in first] + [proj], axis=1)
    rest_ref[:, :hidden] = inner_ref[...].astype(BF16)
    rest_ref[:, hidden:] = proj


def pack_weights(inner, query, key, value, proj, outer):
    rows, hidden = inner.shape
    cols = query.shape[1]
    return pl.pallas_call(
        pack_kernel,
        out_shape=(
            jax.ShapeDtypeStruct((rows, 4 * cols + hidden), BF16),
            jax.ShapeDtypeStruct((rows, hidden + cols), BF16),
        ),
        in_specs=[VMEM] * 6,
        out_specs=(VMEM, VMEM),
        cost_estimate=SHORT,
        name="pack_weights",
    )(inner, query, key, value, proj, outer)


def unring_kernel(ring, spans, found_ref, *out_refs):
    size = found_ref.shape[0] // len(ring)
    for (begin, end, turned), out_ref in zip(spans, out_refs):
        if turned:
            blocks = [
                found_ref[ring.index(d) * size : (ring.index(d) + 1) * size, begin:end]
                for d in range(len(ring))
            ]
            out_ref[...] = jnp.concatenate(blocks, axis=0).T
        else:
            for p, d in enumerate(ring):
                block = found_ref[p * size : (p + 1) * size, begin:end]
                out_ref[d * size : (d + 1) * size, :] = block


def unring(found, ring, spans):
    rows = found.shape[0]
    size = rows // len(ring)
    if size % 16:
        back = [found[ring.index(d) * size :][:size] for d in range(len(ring))]
        whole = jnp.concatenate(back, axis=0)
        parts = [whole[:, begin:end] for begin, end, _ in spans]
        return [part.T if span[2] else part for part, span in zip(parts, spans)]
    shapes = [(end - begin, rows) if turned else (rows, end - begin) for begin, end, turned in spans]
    return pl.pallas_call(
        functools.partial(unring_kernel, ring, spans),
        out_shape=tuple(jax.ShapeDtypeStruct(shape, found.dtype) for shape in shapes),
        in_specs=[VMEM],
        out_specs=(VMEM,) * len(spans),
        cost_estimate=SHORT,
        name="unring",
    )(found)


def store_ringed(out_ref, ring, begin, end, values):
    size = values.shape[0] // len(ring)
    if size % 16:
        out_ref[:, begin:end] = values
    else:
        for p, d in enumerate(ring):
            out_ref[p * size : (p + 1) * size, begin:end] = values[d * size : (d + 1) * size, :]


def ringed(values, ring):
    size = values.shape[0] // len(ring)
    if size % 16 == 0:
        return values
    return jnp.concatenate([values[d * size :][:size] for d in ring], axis=0)


def segment_rows(width, first_len, start, same, other):
    shape = (HEAD_DIM, width)
    low = start + lax.broadcasted_iota(jnp.int32, shape, 1) < first_len
    row = lax.broadcasted_iota(jnp.int32, shape, 0)
    first = jnp.where(low, same, other)
    second = jnp.where(low, other, same)
    return jnp.where(row == 0, first, jnp.where(row == 1, second, 0.0)).astype(BF16)


def segment_all(rows, rows_dev, first_len, me, same, other):
    slots = rows // rows_dev
    return jnp.concatenate(
        [
            segment_rows(rows_dev, first_len, (s ^ me) * rows_dev, same, other)
            for s in range(slots)
        ],
        axis=1,
    )


def tile_range(tile, first_len, tiles):
    start = tile * TILE
    low = jnp.where(start >= first_len, first_len // TILE, 0)
    high = jnp.where(start + TILE <= first_len, (first_len + TILE - 1) // TILE, tiles)
    return low, high


def over_tiles(low, high, body, carry, sizes=(4, 2, 1)):
    at = low
    for size in sizes:
        count = (high - at) // size

        def step(i, c, at=at, size=size):
            return body(tuple(at + size * i + j for j in range(size)), c)

        carry = lax.fori_loop(0, count, step, carry)
        at = at + size * count
    return carry


def attend_rows(
    heads, rows_dev, first_slot, info_ref, qkv_ref, key_ref, out_ref, wide_ref, lse_ref, score_ref, bias_ref
):
    rows = qkv_ref.shape[1]
    cols = heads * HEAD_DIM
    first_len, me = info_ref[0, 0], info_ref[0, 2]
    tiles = rows // TILE
    per_slot = rows_dev // TILE

    def query_tile(i, carry):
        qb = ((first_slot + i // per_slot) ^ me) * per_slot + i % per_slot
        qs = pl.ds(pl.multiple_of(first_slot * rows_dev + i * TILE, TILE), TILE)
        at = pl.ds(pl.multiple_of(i * TILE, TILE), TILE)
        query_seg = segment_rows(TILE, first_len, qb * TILE, 0.0, NEG)
        queries = [
            jnp.concatenate([qkv_ref[h * HEAD_DIM : (h + 1) * HEAD_DIM, qs], query_seg], axis=0)
            for h in range(heads)
        ]
        low, high = tile_range(qb, first_len, tiles)

        def score_tiles(kbs, tops):
            kss = [pl.ds(tile_start(kb, rows_dev, me), TILE) for kb in kbs]
            kinds = [jnp.clip(kb - qb, -2, 2) + 2 for kb in kbs]
            ss = [[mm(key_ref[h, ks, :], queries[h]) for h in range(heads)] for ks in kss]
            tops = list(tops)
            for i, ks in enumerate(kss):
                for h in range(heads):
                    s = ss[i][h] + bias_ref[h * KINDS + kinds[i]]
                    score_ref[h, ks, :] = s
                    tops[h] = jnp.maximum(tops[h], jnp.max(s.reshape(TILE // 8, 8, TILE), axis=0))
            return tuple(tops)

        tops = over_tiles(low, high, score_tiles, (jnp.full((8, TILE), -3e38, F32),) * heads)
        tops = [jnp.max(t, axis=0, keepdims=True) for t in tops]

        def value_tiles(kbs, sums):
            kss = [pl.ds(tile_start(kb, rows_dev, me), TILE) for kb in kbs]
            sums = list(sums)
            ps = []
            for ks in kss:
                for h in range(heads):
                    p = jnp.exp(score_ref[h, ks, :] - tops[h])
                    total, acc = sums[h]
                    sums[h] = (total + jnp.sum(p.reshape(TILE // 8, 8, TILE), axis=0), acc)
                    ps.append(p.astype(BF16))
            for i, ks in enumerate(kss):
                for h in range(heads):
                    values = qkv_ref[2 * cols + h * HEAD_DIM : 2 * cols + (h + 1) * HEAD_DIM, ks]
                    total, acc = sums[h]
                    sums[h] = (total, acc + mm(values, ps[i * heads + h]))
            return tuple(sums)

        zero = (jnp.zeros((8, TILE), F32), jnp.zeros((HEAD_DIM, TILE), F32))
        sums = over_tiles(low, high, value_tiles, (zero,) * heads)
        for h in range(heads):
            total, acc = sums[h]
            total = jnp.sum(total, axis=0, keepdims=True)
            mixed = acc * (1.0 / total)
            hs = slice(h * HEAD_DIM, (h + 1) * HEAD_DIM)
            wide_ref[hs, at] = mixed
            out_ref[hs, at] = mixed.astype(BF16)
            lse_ref[h : h + 1, at] = tops[h] + jnp.log(total)
        return carry

    lax.fori_loop(0, tiles // 2, query_tile, 0)


def attend_far_kernel(
    heads,
    rows_dev,
    info_ref,
    base_ref,
    w_ref,
    slot0_ref,
    slot1_ref,
    slot2_ref,
    slot3_ref,
    out_ref,
    wide_ref,
    lse_ref,
    qkv_ref,
    key_ref,
    score_ref,
    bias_ref,
):
    rows = qkv_ref.shape[1]
    cols = heads * HEAD_DIM
    w_rows = w_ref[:, : 3 * cols].T
    for i, slot_ref in enumerate((slot0_ref, slot1_ref, slot2_ref, slot3_ref)):
        for begin in range(0, rows_dev, TILE):
            part = contract(w_rows, 1, slot_ref[begin : begin + TILE, :], 1)
            at = i * rows_dev + begin
            qkv_ref[:, at : at + TILE] = part.astype(BF16)
    build_bias(base_ref, bias_ref, heads)
    key_seg = segment_all(rows, rows_dev, info_ref[0, 0], info_ref[0, 2], 1.0, 0.0)
    for h in range(heads):
        key_ref[h] = jnp.concatenate(
            [qkv_ref[cols + h * HEAD_DIM : cols + (h + 1) * HEAD_DIM, :], key_seg], axis=0
        ).T
    far = rows // rows_dev // 2
    attend_rows(
        heads, rows_dev, far, info_ref, qkv_ref, key_ref, out_ref, wide_ref, lse_ref, score_ref, bias_ref
    )


def attend_near_kernel(
    heads, rows_dev, info_ref, base_ref, qkv_ref, key_ref, out_ref, wide_ref, lse_ref, score_ref, bias_ref
):
    build_bias(base_ref, bias_ref, heads)
    attend_rows(
        heads, rows_dev, 0, info_ref, qkv_ref, key_ref, out_ref, wide_ref, lse_ref, score_ref, bias_ref
    )


def attend_shapes(heads, rows):
    cols = heads * HEAD_DIM
    return (
        jax.ShapeDtypeStruct((cols, rows // 2), BF16),
        jax.ShapeDtypeStruct((cols, rows // 2), F32),
        jax.ShapeDtypeStruct((heads, rows // 2), F32),
    )


def attend_scratch(heads, rows):
    return [
        pltpu.VMEM((heads, rows, TILE), F32),
        pltpu.VMEM((heads * KINDS, TILE, TILE), F32),
    ]


def attend_far(info, base, weights, slots):
    rows_dev = slots[0].shape[0]
    rows = rows_dev * len(slots)
    cols = weights.shape[1] // 3
    heads = cols // HEAD_DIM
    return pl.pallas_call(
        functools.partial(attend_far_kernel, heads, rows_dev),
        out_shape=attend_shapes(heads, rows)
        + (
            jax.ShapeDtypeStruct((3 * cols, rows), BF16),
            jax.ShapeDtypeStruct((heads, rows, 2 * HEAD_DIM), BF16),
        ),
        in_specs=[SMEM] + [VMEM] * 6,
        out_specs=(VMEM,) * 5,
        scratch_shapes=attend_scratch(heads, rows),
        compiler_params=pltpu.CompilerParams(vmem_limit_bytes=58 << 20),
        cost_estimate=SHORT,
        name="attend_far",
    )(info, base, weights, *slots)


def attend_near(info, base, qkv, keys, rows_dev):
    heads, rows = keys.shape[:2]
    return pl.pallas_call(
        functools.partial(attend_near_kernel, heads, rows_dev),
        out_shape=attend_shapes(heads, rows),
        in_specs=[SMEM] + [VMEM] * 3,
        out_specs=(VMEM,) * 3,
        scratch_shapes=attend_scratch(heads, rows),
        compiler_params=pltpu.CompilerParams(vmem_limit_bytes=58 << 20),
        cost_estimate=SHORT,
        name="attend_near",
    )(info, base, qkv, keys)


def diagonal_sums(values):
    values = jnp.concatenate([jnp.zeros_like(values), values], axis=1)
    count = TILE
    while count > 1:
        count //= 2
        values = values[:count] + pltpu.roll(values[count:], 2 * TILE - count, 1)
    return values


def grad_rows_to(own_ref, send_ref, first_slot, grad_ref, w_ref):
    rows_dev = own_ref.shape[0]
    for slot, out_ref in ((first_slot + 1, send_ref), (first_slot, own_ref)):
        for begin in range(0, rows_dev, TILE):
            at = slot * rows_dev + begin
            part = contract(grad_ref[:, at : at + TILE], 0, w_ref[...], 1)
            out_ref[begin : begin + TILE, :] = part.astype(out_ref.dtype)


def attend_back_kernel(
    heads,
    rows_dev,
    info_ref,
    base_ref,
    lse0_ref,
    lse1_ref,
    grad0_ref,
    grad1_ref,
    qkv_far,
    wide0_far,
    wide1_far,
    key_far,
    w_far,
    diag_ref,
    out_far,
    far_send_far,
    far_own_far,
    near_send_far,
    near_own_far,
    qkv_ref,
    wide0_ref,
    wide1_ref,
    key_ref,
    w_ref,
    out_ref,
    far_send_ref,
    far_own_ref,
    near_send_ref,
    near_own_ref,
    sems,
    lse_ref,
    inner_ref,
    grad_ref,
    query_ref,
    value_rows,
    query_rows,
    grad_rows,
    key_acc,
    value_acc,
    bias_ref,
    table_ref,
):
    rows = qkv_ref.shape[1]
    cols = heads * HEAD_DIM
    first_len, me = info_ref[0, 0], info_ref[0, 2]
    tiles = rows // TILE
    moves = [
        pltpu.make_async_copy(source, target, sems.at[n])
        for n, (source, target) in enumerate(
            (
                (qkv_far, qkv_ref),
                (wide0_far, wide0_ref),
                (wide1_far, wide1_ref),
                (key_far, key_ref),
                (w_far, w_ref),
                (out_ref, out_far),
                (far_send_ref, far_send_far),
                (far_own_ref, far_own_far),
                (near_send_ref, near_send_far),
                (near_own_ref, near_own_far),
            )
        )
    ]
    for move in moves[:5]:
        move.start()
    key_acc[...] = jnp.zeros_like(key_acc)
    value_acc[...] = jnp.zeros_like(value_acc)
    table_ref[...] = jnp.zeros_like(table_ref)
    build_bias(base_ref, bias_ref, heads)
    query_seg = segment_all(rows, rows_dev, first_len, me, 0.0, NEG)
    q_of = [slice(h * HEAD_DIM, (h + 1) * HEAD_DIM) for h in range(heads)]
    k_of = [slice(cols + h * HEAD_DIM, cols + (h + 1) * HEAD_DIM) for h in range(heads)]
    v_of = [slice(2 * cols + h * HEAD_DIM, 2 * cols + (h + 1) * HEAD_DIM) for h in range(heads)]
    lse_ref[:, : rows // 2] = lse0_ref[...]
    lse_ref[:, rows // 2 :] = lse1_ref[...]
    grad_ref[:, : rows // 2] = grad0_ref[...]
    grad_ref[:, rows // 2 :] = grad1_ref[...]
    for move in moves[:3]:
        move.wait()
    for h in range(heads):
        queries = qkv_ref[q_of[h], :]
        query_ref[h] = jnp.concatenate([queries, query_seg], axis=0)
        query_rows[h] = queries.T
        value_rows[h] = qkv_ref[v_of[h], :].T
        grad_rows[h] = grad_ref[q_of[h], :].T
        for half, wide_ref in ((0, wide0_ref), (1, wide1_ref)):
            at = slice(half * rows // 2, (half + 1) * rows // 2)
            terms = grad_ref[q_of[h], at].astype(F32) * wide_ref[q_of[h], :]
            inner_ref[h : h + 1, at] = jnp.sum(terms, axis=0, keepdims=True)
    moves[3].wait()

    def query_tile(qb, carry):
        qs = pl.ds(tile_start(qb, rows_dev, me), TILE)
        low, high = tile_range(qb, first_len, tiles)
        grads = [grad_ref[q_of[h], qs] for h in range(heads)]
        inner = [inner_ref[h : h + 1, qs] for h in range(heads)]
        lse = [lse_ref[h : h + 1, qs] for h in range(heads)]

        def tiles_at(kbs, sums):
            kss = [pl.ds(tile_start(kb, rows_dev, me), TILE) for kb in kbs]
            kinds = [jnp.clip(kb - qb, -2, 2) + 2 for kb in kbs]
            ss = [[mm(key_ref[h, ks, :], query_ref[h, :, qs]) for h in range(heads)] for ks in kss]
            dps = [[mm(value_rows[h, ks, :], grads[h]) for h in range(heads)] for ks in kss]
            lows = []
            for i in range(len(kbs)):
                for h in range(heads):
                    p = jnp.exp(ss[i][h] + bias_ref[h * KINDS + kinds[i]] - lse[h])
                    ds = p * (dps[i][h] - inner[h])
                    table_ref[h * KINDS + kinds[i]] += ds
                    lows.append((p.astype(BF16), ds.astype(BF16)))
            sums = list(sums)
            for i, ks in enumerate(kss):
                for h in range(heads):
                    low_p, low_ds = lows[i * heads + h]
                    value_acc[h, ks, :] += mm(low_p, grad_rows[h, qs, :])
                    key_acc[h, ks, :] += mm(low_ds, query_rows[h, qs, :])
                    sums[h] = sums[h] + mm(qkv_ref[k_of[h], ks], low_ds)
            return tuple(sums)

        sums = tuple(jnp.zeros((HEAD_DIM, TILE), F32) for _ in range(heads))
        sums = over_tiles(low, high, tiles_at, sums, (4, 2, 1))
        for h in range(heads):
            out_ref[q_of[h], qs] = sums[h].astype(BF16)
        return carry

    lax.fori_loop(0, tiles, query_tile, 0)
    for h in range(heads):
        out_ref[k_of[h], :] = key_acc[h].astype(BF16).T
        out_ref[v_of[h], :] = value_acc[h].astype(BF16).T
    moves[5].start()
    moves[4].wait()
    grad_rows_to(far_own_ref, far_send_ref, rows // rows_dev // 2, out_ref, w_ref)
    moves[6].start()
    moves[7].start()
    grad_rows_to(near_own_ref, near_send_ref, 0, out_ref, w_ref)
    moves[8].start()
    moves[9].start()
    for i in range(heads * KINDS):
        if i % KINDS in (0, KINDS - 1):
            total = jnp.sum(table_ref[i], axis=0, keepdims=True)
            diag_ref[i : i + 1, :] = jnp.concatenate([total, jnp.zeros_like(total)], axis=1)
        else:
            diag_ref[i : i + 1, :] = diagonal_sums(table_ref[i])
    for move in moves[5:]:
        move.wait()


def attend_back(info, base, qkv, keys, wide, lse, grad, weights, rows_dev):
    rows = qkv.shape[1]
    width = weights.shape[0]
    heads = qkv.shape[0] // (3 * HEAD_DIM)
    cols = heads * HEAD_DIM
    far = pl.BlockSpec(memory_space=pl.ANY)
    half = [pltpu.VMEM((rows_dev, width), BF16)] * 4
    out = pl.pallas_call(
        functools.partial(attend_back_kernel, heads, rows_dev),
        out_shape=(
            jax.ShapeDtypeStruct((heads * KINDS, 2 * TILE), F32),
            jax.ShapeDtypeStruct((3 * cols, rows), BF16),
            *[jax.ShapeDtypeStruct((rows_dev, width), BF16)] * 4,
        ),
        in_specs=[SMEM] + [VMEM] * 5 + [far] * 5,
        out_specs=(VMEM,) + (far,) * 5,
        scratch_shapes=[
            pltpu.VMEM(qkv.shape, BF16),
            pltpu.VMEM(wide[0].shape, F32),
            pltpu.VMEM(wide[1].shape, F32),
            pltpu.VMEM(keys.shape, BF16),
            pltpu.VMEM(weights.shape, BF16),
            pltpu.VMEM((3 * cols, rows), BF16),
            *half,
            pltpu.SemaphoreType.DMA((10,)),
            pltpu.VMEM((heads, rows), F32),
            pltpu.VMEM((heads, rows), F32),
            pltpu.VMEM((cols, rows), BF16),
            pltpu.VMEM((heads, 2 * HEAD_DIM, rows), BF16),
            pltpu.VMEM((heads, rows, HEAD_DIM), BF16),
            pltpu.VMEM((heads, rows, HEAD_DIM), BF16),
            pltpu.VMEM((heads, rows, HEAD_DIM), BF16),
            pltpu.VMEM((heads, rows, HEAD_DIM), F32),
            pltpu.VMEM((heads, rows, HEAD_DIM), F32),
            pltpu.VMEM((heads * KINDS, TILE, TILE), F32),
            pltpu.VMEM((heads * KINDS, TILE, TILE), F32),
        ],
        compiler_params=pltpu.CompilerParams(vmem_limit_bytes=60 << 20),
        cost_estimate=LONG,
        name="attend_back",
    )(info, base, *lse, *grad, qkv, *wide, keys, weights)
    diagonals, grad_qkv, far_send, far_own, near_send, near_own = out
    return grad_qkv, diagonals, far_own, far_send, near_own, near_send


def scaled_rows(values):
    return values * lax.rsqrt(jnp.mean(values * values, axis=-1, keepdims=True) + EPS)


def join_kernel(rows_ref, near_ref, far_ref, gain_ref, middle_ref, low_ref):
    for rs in row_blocks(rows_ref.shape[0]):
        middle = rows_ref[rs, :].astype(F32) + near_ref[rs, :] + far_ref[rs, :].astype(F32)
        middle_ref[rs, :] = middle
        low_ref[rs, :] = (scaled_rows(middle) * gain_ref[...]).astype(BF16)


def row_blocks(rows):
    return [slice(begin, begin + TILE // 4) for begin in range(0, rows, TILE // 4)]


def norm_back_rows(values, upstream, gain):
    scale = lax.rsqrt(jnp.mean(values * values, axis=-1, keepdims=True) + EPS)
    normed = values * scale
    scaled = upstream * gain
    inner = jnp.mean(scaled * normed, axis=-1, keepdims=True)
    return scale * (scaled - normed * inner)


def middle_back_kernel(middle_ref, near_ref, far_ref, grads_ref, gain_ref, low_ref):
    for rs in row_blocks(middle_ref.shape[0]):
        upstream = near_ref[rs, :].astype(F32) + far_ref[rs, :].astype(F32)
        back = norm_back_rows(middle_ref[rs, :], upstream, gain_ref[...])
        low_ref[rs, :] = (grads_ref[rs, :].astype(F32) + back).astype(BF16)


def rows_back_kernel(rows_ref, near_ref, core_ref, far_ref, after_ref, gain_ref, low_ref):
    for rs in row_blocks(rows_ref.shape[0]):
        upstream = near_ref[rs, :].astype(F32) + core_ref[rs, :].astype(F32)
        upstream = upstream + far_ref[rs, :].astype(F32)
        back = norm_back_rows(rows_ref[rs, :].astype(F32), upstream, gain_ref[...])
        low_ref[rs, :] = (after_ref[rs, :].astype(F32) + back).astype(BF16)


def by_rows(kernel, name, gain, *operands, out, cost=SHORT):
    shape = operands[0].shape
    return pl.pallas_call(
        kernel,
        out_shape=tuple(jax.ShapeDtypeStruct(shape, kind) for kind in out),
        in_specs=[VMEM] * (len(operands) + 1),
        out_specs=(VMEM,) * len(out),
        compiler_params=pltpu.CompilerParams(vmem_limit_bytes=16 << 20),
        cost_estimate=cost,
        name=name,
    )(*operands, gain[None])


def out_proj_kernel(own_ref, other_ref, w_own_ref, w_other_ref, near_ref, send_ref):
    half = near_ref.shape[0]
    for begin in range(0, 2 * half, TILE):
        part = contract(own_ref[:, begin : begin + TILE], 0, w_own_ref[...], 0)
        part = part + contract(other_ref[:, begin : begin + TILE], 0, w_other_ref[...], 0)
        if begin < half:
            near_ref[begin : begin + TILE, :] = part
        else:
            send_ref[begin - half : begin - half + TILE, :] = part.astype(BF16)


def out_proj(own, other, w_own, w_other):
    half, width = own.shape[1] // 2, w_own.shape[1]
    return pl.pallas_call(
        out_proj_kernel,
        out_shape=(
            jax.ShapeDtypeStruct((half, width), F32),
            jax.ShapeDtypeStruct((half, width), BF16),
        ),
        in_specs=[VMEM] * 4,
        out_specs=(VMEM, VMEM),
        compiler_params=pltpu.CompilerParams(vmem_limit_bytes=16 << 20),
        cost_estimate=SHORT,
        name="out_proj",
    )(own, other, w_own, w_other)


def mixed_grads_kernel(middle0, middle1, w_own_ref, w_other_ref, own_ref, send_ref):
    half = middle0.shape[0]
    for w_ref, out_ref in ((w_other_ref, send_ref), (w_own_ref, own_ref)):
        for i, middle_ref in enumerate((middle0, middle1)):
            part = contract(w_ref[...], 1, middle_ref[...], 1)
            out_ref[:, i * half : (i + 1) * half] = part.astype(BF16)


def mixed_grads(middle, w_own, w_other):
    shape = jax.ShapeDtypeStruct((w_own.shape[0], 2 * middle[0].shape[0]), BF16)
    return pl.pallas_call(
        mixed_grads_kernel,
        out_shape=(shape, shape),
        in_specs=[VMEM] * 4,
        out_specs=(VMEM, VMEM),
        compiler_params=pltpu.CompilerParams(vmem_limit_bytes=16 << 20),
        cost_estimate=SHORT,
        name="mixed_grads",
    )(*middle, w_own, w_other)


def ffn_kernel(
    ring,
    normed0,
    normed1,
    grad0,
    grad1,
    inner0,
    inner1,
    outer0,
    outer1,
    own_ref,
    send_ref,
    out_own_ref,
    out_send_ref,
    grads_ref,
    gain_ref,
    hid_ref,
    pre_ref,
    acc_ref,
    out_acc_ref,
    left_ref,
    gain_acc,
):
    half, width = own_ref.shape
    part = inner0.shape[1]
    block = grads_ref.shape[1]
    per_part = part // TILE
    steps = 2
    sweeps = 2 * part // block
    step = pl.program_id(0)
    root, cubic = 0.7978845608028654, 0.044715
    places = [
        (normed_ref, grad_ref, begin, i * half + begin)
        for i, (normed_ref, grad_ref) in enumerate(((normed0, grad0), (normed1, grad1)))
        for begin in range(0, half, TILE)
    ]
    weights = ((inner0, outer0), (inner1, outer1))

    def products(inner_ref, outer_ref, index, place):
        normed_ref, grad_ref, begin, _ = place
        rs, js = slice(begin, begin + TILE), slice(index * TILE, (index + 1) * TILE)
        return mm(normed_ref[rs, :], inner_ref[:, js]), mm(grad_ref[rs, :], outer_ref[:, js])

    def hidden_part(inner_ref, outer_ref, offset):
        work = [(index, place) for index in range(per_part) for place in places]
        ahead = products(inner_ref, outer_ref, *work[0])
        for n, (index, place) in enumerate(work):
            a, dh = ahead
            if n + 1 < len(work):
                ahead = products(inner_ref, outer_ref, *work[n + 1])
            rs = slice(place[3], place[3] + TILE)
            to = slice(offset + index * TILE, offset + (index + 1) * TILE)
            square = a * a
            t = jnp.tanh(a * (root + (root * cubic) * square))
            half_a = 0.5 * a
            cdf = 0.5 + 0.5 * t
            slope = cdf + half_a * (1.0 - t * t) * (root + (3.0 * root * cubic) * square)
            hid_ref[rs, to] = (a * cdf).astype(BF16)
            pre_ref[rs, to] = (dh * slope).astype(BF16)

    def rows_out(kept_ref, w_ref, offset, sum_ref, near_ref, far_ref):
        for _, _, _, at in places:
            rs = slice(at, at + TILE)
            back = contract(kept_ref[rs, offset : offset + part], 1, w_ref[...], 1)
            if offset == 0:
                sum_ref[rs, :] = back
            elif at < half:
                near_ref[rs, :] = (sum_ref[rs, :] + back).astype(BF16)
            else:
                far_ref[at - half : at - half + TILE, :] = (sum_ref[rs, :] + back).astype(BF16)

    for i, (inner_ref, outer_ref) in enumerate(weights):

        @pl.when(step == i)
        def _(inner_ref=inner_ref, outer_ref=outer_ref, offset=i * part):
            hidden_part(inner_ref, outer_ref, offset)
            rows_out(pre_ref, inner_ref, offset, acc_ref, own_ref, send_ref)
            rows_out(hid_ref, outer_ref, offset, out_acc_ref, out_own_ref, out_send_ref)

    def load(first_ref, second_ref):
        left_ref[:, :half] = first_ref[...].T
        left_ref[:, half:] = second_ref[...].T

    for i in range(sweeps):

        @pl.when(step == steps + i)
        def _(i=i):
            if i == 0:
                load(normed0, normed1)
            values = mm(left_ref[...], pre_ref[:, i * block : (i + 1) * block])
            store_ringed(grads_ref, ring, 0, block, values.astype(BF16))
            lanes = gain_acc.shape[1]
            total = jnp.zeros(gain_acc.shape, F32) if i == 0 else gain_acc[...]
            for b in range(0, block, lanes):
                at = i * block + b
                w_ref = inner0 if at < part else inner1
                w = w_ref[:, at % part : at % part + lanes].astype(F32)
                total = total + values[:, b : b + lanes] * w
            gain_acc[...] = total
            if i == sweeps - 1:
                gain_ref[...] = jnp.sum(total.T, axis=0, keepdims=True)

        @pl.when(step == steps + sweeps + i)
        def _(i=i):
            if i == 0:
                load(grad0, grad1)
            values = mm(left_ref[...], hid_ref[:, i * block : (i + 1) * block])
            store_ringed(grads_ref, ring, 0, block, values.astype(BF16))


def ffn(ring, normed, grads, inners, outers):
    half, width = normed[0].shape
    part = inners[0].shape[1]
    rows, hidden = 2 * half, 2 * part
    block = 2 * TILE
    steps = 2
    return pl.pallas_call(
        functools.partial(ffn_kernel, ring),
        grid=(steps + 2 * (hidden // block),),
        out_shape=(
            pltpu.HBM((half, width), BF16),
            pltpu.VMEM((half, width), BF16),
            *[pltpu.HBM((half, width), BF16)] * 2,
            pltpu.HBM((width, 2 * hidden), BF16),
            pltpu.HBM((1, width), F32),
        ),
        in_specs=[VMEM] * 8,
        out_specs=(
            VMEM,
            VMEM,
            VMEM,
            VMEM,
            pl.BlockSpec((width, block), lambda j: (0, jnp.maximum(j - steps, 0))),
            pl.BlockSpec((1, width), lambda j: (0, 0)),
        ),
        scratch_shapes=[
            pltpu.VMEM((rows, hidden), BF16),
            pltpu.VMEM((rows, hidden), BF16),
            pltpu.VMEM((rows, width), F32),
            pltpu.VMEM((rows, width), F32),
            pltpu.VMEM((width, rows), BF16),
            pltpu.VMEM((width, 128), F32),
        ],
        compiler_params=pltpu.CompilerParams(vmem_limit_bytes=44 << 20),
        cost_estimate=SHORT,
        name="ffn",
    )(*normed, *grads, *inners, *outers)


def proj_grads_kernel(middle0, middle1, mixed0, mixed1, out_ref):
    half = middle0.shape[0]
    total = 0.0
    for i, middle_ref in enumerate((middle0, middle1)):
        at = slice(i * half, (i + 1) * half)
        mixed = jnp.concatenate([mixed0[:, at], mixed1[:, at]], axis=0)
        total = total + contract(middle_ref[...].T, 1, mixed, 1)
    out_ref[...] = total.astype(BF16)


def proj_grads(middle, mixed):
    shape = (middle[0].shape[1], 2 * mixed[0].shape[0])
    return pl.pallas_call(
        proj_grads_kernel,
        out_shape=jax.ShapeDtypeStruct(shape, BF16),
        in_specs=[VMEM] * 4,
        out_specs=VMEM,
        compiler_params=pltpu.CompilerParams(vmem_limit_bytes=24 << 20),
        cost_estimate=SHORT,
        name="proj_grads",
    )(*middle, *mixed)


def qkv_grads_kernel(
    ring,
    grad_ref,
    slot0_ref,
    slot1_ref,
    slot2_ref,
    slot3_ref,
    w_ref,
    proj_ref,
    out_ref,
    gain_ref,
):
    rows_dev = slot0_ref.shape[0]
    total = 0.0
    for i, slot_ref in enumerate((slot0_ref, slot1_ref, slot2_ref, slot3_ref)):
        total = total + mm(grad_ref[:, i * rows_dev : (i + 1) * rows_dev], slot_ref[...])
    gain_ref[...] = jnp.sum(total * w_ref[:, : total.shape[0]].T.astype(F32), axis=0, keepdims=True)
    both = jnp.concatenate([total.T.astype(BF16), proj_ref[...]], axis=1)
    store_ringed(out_ref, ring, 0, out_ref.shape[1], both)


def qkv_grads(ring, grad_qkv, slots, weights, proj):
    width = slots[0].shape[1]
    cols = grad_qkv.shape[0] + proj.shape[1]
    return pl.pallas_call(
        functools.partial(qkv_grads_kernel, ring),
        out_shape=(
            jax.ShapeDtypeStruct((width, cols), BF16),
            jax.ShapeDtypeStruct((1, width), F32),
        ),
        in_specs=[VMEM] * 7,
        out_specs=(VMEM, VMEM),
        compiler_params=pltpu.CompilerParams(vmem_limit_bytes=58 << 20),
        cost_estimate=SHORT,
        name="qkv_grads",
    )(grad_qkv, *slots, weights, proj)


def finish_kernel(pack_ref, taken_ref, inner_ref, outer_ref):
    hidden = inner_ref.shape[1]
    pack, taken = pack_ref[...].astype(F32), taken_ref[...].astype(F32)
    inner_ref[...] = pack[:, :hidden] + taken[:, :hidden]
    outer_ref[...] = pack[:, 2 * hidden : 3 * hidden] + taken[:, hidden:]


def finish(pack, taken):
    shape = jax.ShapeDtypeStruct((taken.shape[0], taken.shape[1] // 2), F32)
    return pl.pallas_call(
        finish_kernel,
        out_shape=(shape, shape),
        in_specs=[VMEM] * 2,
        out_specs=(VMEM,) * 2,
        cost_estimate=SHORT,
        name="finish",
    )(pack, taken)


def finish_last_kernel(last_ref, far_ref, query_ref, key_ref, value_ref, proj_ref):
    cols = query_ref.shape[1]
    last = last_ref[...].astype(F32)
    for i, out_ref in enumerate((query_ref, key_ref, value_ref)):
        out_ref[...] = last[:, i * cols : (i + 1) * cols]
    proj_ref[...] = (last[:, 3 * cols : 4 * cols] + far_ref[...].astype(F32)).T


def finish_last(last, far):
    rows, cols = far.shape
    shapes = [(rows, cols)] * 3 + [(cols, rows)]
    return pl.pallas_call(
        finish_last_kernel,
        out_shape=tuple(jax.ShapeDtypeStruct(shape, F32) for shape in shapes),
        in_specs=[VMEM] * 2,
        out_specs=(VMEM,) * 4,
        cost_estimate=SHORT,
        name="finish_last",
    )(last, far)


def bias_rows(line):
    heads = line.shape[0]
    pad = 3 * TILE
    rev = jnp.flip(line, axis=1)
    left = jnp.broadcast_to(rev[:, :1], (heads, pad))
    right = jnp.broadcast_to(rev[:, -1:], (heads, pad + 2 * TILE))
    ext = jnp.concatenate([left, rev, right], axis=1)
    begin = [pad + MAXDIST - TILE - TILE * d for d in range(-2, 3)]
    rows = [ext[:, b : b + 2 * TILE] for b in begin]
    return jnp.stack(rows, axis=1).reshape(heads * KINDS, 2 * TILE)


def line_index():
    kind = lax.broadcasted_iota(jnp.int32, (KINDS, 2 * TILE), 0) - 2
    lane = lax.broadcasted_iota(jnp.int32, (KINDS, 2 * TILE), 1)
    near = jnp.clip(TILE + TILE * kind - lane, -MAXDIST, MAXDIST)
    far = jnp.where(kind < 0, -MAXDIST, MAXDIST)
    return (jnp.where(jnp.abs(kind) == 2, far, near) + MAXDIST).reshape(KINDS * 2 * TILE)


def on_device(
    tokens,
    cotangent,
    w_query,
    w_key,
    w_value,
    w_proj,
    w_inner,
    w_outer,
    gain_attn,
    gain_ffn,
    rel_table,
    lengths,
    deal,
    buckets,
):
    rows_dev = tokens.shape[0]
    tensor_size = lax.axis_size("tensor")
    dp_size = lax.axis_size("dp")
    me = lax.axis_index("tensor")
    heads = w_query.shape[1] // HEAD_DIM
    cols = heads * HEAD_DIM
    hidden = w_inner.shape[1]
    width = tokens.shape[1]
    pair = 2 * rows_dev

    def swap(values, bit):
        return lax.ppermute(values, "tensor", [(i, i ^ bit) for i in range(tensor_size)])

    def deal_out(values):
        return lax.all_to_all(values, "dp", split_axis=0, concat_axis=0, tiled=True)

    def sum_groups(values):
        step = 1
        while step < dp_size:
            values = values + lax.ppermute(values, "dp", [(i, i ^ step) for i in range(dp_size)])
            step *= 2
        return values

    ring = ring_order(dp_size)
    both = ("dp", "tensor")
    ring_groups = [[d * tensor_size + t for d in ring] for t in range(tensor_size)]

    def gather(values, spans):
        found = lax.all_gather(values, both, axis=0, tiled=True, axis_index_groups=ring_groups)
        return unring(found, ring, spans)

    def scatter_sum(values):
        return lax.psum_scatter(
            ringed(values, ring), both, scatter_dimension=0, tiled=True, axis_index_groups=ring_groups
        )

    own_front, own_rest = pack_weights(
        w_inner, w_query, w_key, w_value, w_proj, w_outer.T
    )
    own_front, tokens = after(own_front, tokens)
    ends = (3 * cols, 3 * cols + hidden, 4 * cols + hidden)
    front, outer_own, proj_own = gather(
        own_front, ((0, ends[0], False), (ends[0], ends[1], False), (ends[1], ends[2], True))
    )
    low_rows = deal_out(tokens.at[deal].get(mode="promise_in_bounds", unique_indices=True))
    other_rest, low_rows = after(swap(own_rest, 2), low_rows)
    inner_own, inner_other, proj_other = gather(
        jnp.concatenate([own_rest[:, :hidden], other_rest], axis=1),
        (
            (0, hidden, False),
            (hidden, 2 * hidden, False),
            (2 * hidden, 2 * hidden + cols, True),
        ),
    )
    onehot_buckets = (
        buckets[:, None] == jnp.arange(rel_table.shape[0], dtype=jnp.int32)[None, :]
    ).astype(F32)
    head_table = lax.dynamic_slice_in_dim(rel_table, me * heads, heads, 1)
    offset_bias = jnp.dot(onehot_buckets, head_table, precision=lax.Precision.HIGHEST).T
    base = bias_rows(offset_bias)
    info = jnp.concatenate([lengths, jnp.full((1, 1), me, jnp.int32)], axis=1)

    slot0 = (scaled_rows(low_rows.astype(F32)) * gain_attn).astype(BF16)
    slot2 = swap(slot0, 2)
    slot1 = swap(slot0, 1)
    slot2, front, base, info = after(slot2, front, base, info)
    slot3 = swap(slot2, 1)
    slots = (slot0, slot1, slot2, slot3)
    outer_other = swap(outer_own, 2)

    low_grads = deal_out(cotangent.at[deal].get(mode="promise_in_bounds", unique_indices=True))

    mixed_far, wide_far, lse_far, qkv, keys = attend_far(info, base, front, slots)
    mixed_other = swap(mixed_far, 2)
    late_qkv, low_grads = after(qkv, low_grads)
    mixed_own, wide_own, lse_own = attend_near(info, base, late_qkv, keys, rows_dev)
    mixed_own, outer_other, inner_own = after(mixed_own, outer_other, inner_own)
    near, to_core = out_proj(mixed_own, mixed_other, proj_own, proj_other)
    middle, low_two = by_rows(
        join_kernel, "join", gain_ffn, low_rows, near, swap(to_core, 1), out=(F32, BF16)
    )

    pair_two = (low_two, swap(low_two, 1))
    pair_grads = (low_grads, swap(low_grads, 1))
    back_own, back_send, out_own, out_far, grad_pack, gain_two = ffn(
        ring, pair_two, pair_grads, (inner_own, inner_other), (outer_own, outer_other)
    )
    shard_pack = scatter_sum(grad_pack)
    (low_middle,) = by_rows(
        middle_back_kernel,
        "middle_back",
        gain_ffn,
        middle,
        back_own,
        swap(back_send, 1),
        low_grads,
        out=(BF16,),
    )
    pair_middle = (low_middle, swap(low_middle, 1))
    grad_own, to_other = mixed_grads(pair_middle, proj_own, proj_other)

    proj_pack = proj_grads(pair_middle, (mixed_own, mixed_other))

    out_own, to_other = after(out_own, to_other)
    result_rows = (middle + out_own.astype(F32) + swap(out_far, 1).astype(F32)).astype(BF16)
    result_rows, proj_pack = after(result_rows, proj_pack)
    back_rows = deal_out(result_rows)

    grad_far, proj_pack = after(swap(to_other, 2), proj_pack)
    grad_qkv, diagonals, far_own, far_send, near_own, near_send = attend_back(
        info,
        base,
        qkv,
        keys,
        (wide_own, wide_far),
        (lse_own, lse_far),
        (grad_own, grad_far),
        front,
        rows_dev,
    )
    far_send, back_rows = after(far_send, back_rows)
    grad_later = (far_own.astype(F32) + swap(far_send, 1).astype(F32)).astype(BF16)
    offset_count = 2 * MAXDIST + 1
    onehot_line = (
        line_index()[:, None] == jnp.arange(offset_count, dtype=jnp.int32)[None, :]
    ).astype(F32)
    offset_total = jnp.dot(
        diagonals.reshape(heads, KINDS * 2 * TILE), onehot_line, precision=lax.Precision.HIGHEST
    )
    table_heads = jnp.dot(onehot_buckets.T, offset_total.T, precision=lax.Precision.HIGHEST)
    table_full = lax.dynamic_update_slice_in_dim(
        jnp.zeros(rel_table.shape, F32), table_heads, me * heads, 1
    )
    grad_later, near_send, table_full = after(grad_later, near_send, table_full)
    later_qkv, grad_later = after(grad_qkv, grad_later)
    low_qkv_w, gain_one = qkv_grads(ring, later_qkv, slots, front, proj_pack)
    low_qkv_w, shard_pack = after(low_qkv_w, shard_pack)
    shard_qkv = scatter_sum(low_qkv_w)
    taken = swap(
        jnp.concatenate([shard_pack[:, hidden : 2 * hidden], shard_pack[:, 3 * hidden :]], axis=1),
        2,
    )
    terms = [gain_one[0] / gain_attn, gain_two[0] / gain_ffn, table_full.reshape(-1)]
    small = sum_groups(jnp.concatenate(terms).reshape(-1, 128))
    grad_two_rows, small = after(swap(grad_later, 2), small)
    small = small + swap(small, 1)
    small, taken = after(small, taken)
    small = small + swap(small, 2)

    near_core = swap(near_send, 1)
    (low_grad_rows,) = by_rows(
        rows_back_kernel,
        "rows_back",
        gain_attn,
        low_rows,
        near_own,
        near_core,
        grad_two_rows,
        low_middle,
        out=(BF16,),
        cost=pl.CostEstimate(flops=(3<<33)//2, bytes_accessed=(1<<26)//2, transcendentals=(1<<23)//2),
    )

    shard_far = swap(shard_qkv[:, 4 * cols :], 2)
    weight_shards = [*finish_last(shard_qkv, shard_far), *finish(shard_pack, taken)]
    out_rows = deal_rows(back_rows, deal, True)
    small = small.reshape(-1)
    back_grads = deal_out(low_grad_rows)
    back_grads, out_rows, *weight_shards = after(back_grads, out_rows, *weight_shards)
    return (
        out_rows,
        deal_rows(back_grads, deal, True),
        *weight_shards[:3],
        *weight_shards[3:5],
        weight_shards[5].T,
        small[:width],
        small[width : 2 * width],
        small[2 * width :].reshape(rel_table.shape),
    )


def solution(mesh):
    rows = P(("dp", "tensor"), None)
    inward, outward = P("dp", "tensor"), P("tensor", "dp")
    weights = (inward, inward, inward, outward, inward, outward)
    return jax.shard_map(
        on_device,
        mesh=mesh,
        in_specs=(rows, rows, *weights, P(), P(), P(), P("dp", None), P(("dp", "tensor")), P()),
        out_specs=(rows, rows, *weights, P(), P(), P()),
        check_vma=False,
    )
```

```python
import functools

import jax
import jax.numpy as jnp
from jax import lax
from jax.experimental import pallas as pl
from jax.experimental.pallas import tpu as pltpu
from jax.sharding import PartitionSpec as P

HEAD_DIM = 64
MAXDIST = 128
TILE = 256
KINDS = 5
EPS = 1e-06
NEG = -1000000000.0
BF16 = jnp.bfloat16
F32 = jnp.float32
VMEM = pl.BlockSpec(memory_space=pltpu.VMEM)
SMEM = pl.BlockSpec(memory_space=pltpu.SMEM)


SHORT = pl.CostEstimate(flops=1 << 20, bytes_accessed=1 << 16, transcendentals=0)


LONG = pl.CostEstimate(flops=3 << 33, bytes_accessed=1 << 26, transcendentals=1 << 23)


def mm(left, right):
    return jnp.dot(left, right, preferred_element_type=F32)


def contract(left, left_dim, right, right_dim):
    return lax.dot_general(
        left, right, (((left_dim,), (right_dim,)), ((), ())), preferred_element_type=F32
    )


def chosen(values, order):
    dims = lax.GatherDimensionNumbers((1,), (0,), (0,))
    return lax.gather(
        values,
        order[:, None],
        dims,
        (1, values.shape[1]),
        unique_indices=True,
        mode=lax.GatherScatterMode.PROMISE_IN_BOUNDS,
    )


def after(*values):
    return lax.optimization_barrier(values)


def ring_order(size):
    return [*range(0, size, 2), *range(size - 1, 0, -2)]


def tile_start(tile, rows_dev, me):
    per_slot = rows_dev // TILE
    return pl.multiple_of((((tile // per_slot) ^ me) * per_slot + tile % per_slot) * TILE, TILE)


def build_bias(base_ref, bias_ref, heads):
    for i in range(heads * KINDS):
        row = base_ref[i : i + 1, :]
        if i % KINDS in (0, KINDS - 1):
            bias_ref[i] = jnp.broadcast_to(row[:, :1], (TILE, TILE))
        else:
            full = jnp.broadcast_to(row, (TILE, 2 * TILE))
            bias_ref[i] = pltpu.roll(full, 0, 1, stride=1, stride_axis=0)[:, TILE:]


def deal_kernel(back, order_ref, values_ref, out_ref):
    rows = values_ref.shape[0]
    place = lax.broadcasted_iota(jnp.int32, (rows, rows), 0)
    chosen = jnp.where(place == order_ref[...], 1.0, 0.0).astype(BF16)
    dealt = mm(chosen, values_ref[...]) if back else contract(chosen, 0, values_ref[...], 0)
    out_ref[...] = dealt.astype(BF16)


def deal_rows(values, order, back):
    return pl.pallas_call(
        functools.partial(deal_kernel, back),
        out_shape=jax.ShapeDtypeStruct(values.shape, BF16),
        in_specs=[VMEM, VMEM],
        out_specs=VMEM,
        compiler_params=pltpu.CompilerParams(vmem_limit_bytes=16 << 20),
        cost_estimate=SHORT,
        name="deal_back" if back else "deal_rows",
    )(order[None], values)


def pack_kernel(inner_ref, query_ref, key_ref, value_ref, proj_ref, outer_ref, first_ref, rest_ref):
    hidden = inner_ref.shape[1]
    proj = proj_ref[...].T.astype(BF16)
    first = [query_ref[...], key_ref[...], value_ref[...], outer_ref[...]]
    first_ref[...] = jnp.concatenate([part.astype(BF16) for part in first] + [proj], axis=1)
    rest_ref[:, :hidden] = inner_ref[...].astype(BF16)
    rest_ref[:, hidden:] = proj


def pack_weights(inner, query, key, value, proj, outer):
    rows, hidden = inner.shape
    cols = query.shape[1]
    return pl.pallas_call(
        pack_kernel,
        out_shape=(
            jax.ShapeDtypeStruct((rows, 4 * cols + hidden), BF16),
            jax.ShapeDtypeStruct((rows, hidden + cols), BF16),
        ),
        in_specs=[VMEM] * 6,
        out_specs=(VMEM, VMEM),
        cost_estimate=SHORT,
        name="pack_weights",
    )(inner, query, key, value, proj, outer)


def unring_kernel(ring, spans, found_ref, *out_refs):
    size = found_ref.shape[0] // len(ring)
    for (begin, end, turned), out_ref in zip(spans, out_refs):
        if turned:
            blocks = [
                found_ref[ring.index(d) * size : (ring.index(d) + 1) * size, begin:end]
                for d in range(len(ring))
            ]
            out_ref[...] = jnp.concatenate(blocks, axis=0).T
        else:
            for p, d in enumerate(ring):
                block = found_ref[p * size : (p + 1) * size, begin:end]
                out_ref[d * size : (d + 1) * size, :] = block


def unring(found, ring, spans):
    rows = found.shape[0]
    size = rows // len(ring)
    if size % 16:
        back = [found[ring.index(d) * size :][:size] for d in range(len(ring))]
        whole = jnp.concatenate(back, axis=0)
        parts = [whole[:, begin:end] for begin, end, _ in spans]
        return [part.T if span[2] else part for part, span in zip(parts, spans)]
    shapes = [(end - begin, rows) if turned else (rows, end - begin) for begin, end, turned in spans]
    return pl.pallas_call(
        functools.partial(unring_kernel, ring, spans),
        out_shape=tuple(jax.ShapeDtypeStruct(shape, found.dtype) for shape in shapes),
        in_specs=[VMEM],
        out_specs=(VMEM,) * len(spans),
        cost_estimate=SHORT,
        name="unring",
    )(found)


def store_ringed(out_ref, ring, begin, end, values):
    size = values.shape[0] // len(ring)
    if size % 16:
        out_ref[:, begin:end] = values
    else:
        for p, d in enumerate(ring):
            out_ref[p * size : (p + 1) * size, begin:end] = values[d * size : (d + 1) * size, :]


def ringed(values, ring):
    size = values.shape[0] // len(ring)
    if size % 16 == 0:
        return values
    return jnp.concatenate([values[d * size :][:size] for d in ring], axis=0)


def segment_rows(width, first_len, start, same, other):
    shape = (HEAD_DIM, width)
    low = start + lax.broadcasted_iota(jnp.int32, shape, 1) < first_len
    row = lax.broadcasted_iota(jnp.int32, shape, 0)
    first = jnp.where(low, same, other)
    second = jnp.where(low, other, same)
    return jnp.where(row == 0, first, jnp.where(row == 1, second, 0.0)).astype(BF16)


def segment_all(rows, rows_dev, first_len, me, same, other):
    slots = rows // rows_dev
    return jnp.concatenate(
        [
            segment_rows(rows_dev, first_len, (s ^ me) * rows_dev, same, other)
            for s in range(slots)
        ],
        axis=1,
    )


def tile_range(tile, first_len, tiles):
    start = tile * TILE
    low = jnp.where(start >= first_len, first_len // TILE, 0)
    high = jnp.where(start + TILE <= first_len, (first_len + TILE - 1) // TILE, tiles)
    return low, high


def over_tiles(low, high, body, carry, sizes=(4, 2, 1)):
    at = low
    for size in sizes:
        count = (high - at) // size

        def step(i, c, at=at, size=size):
            return body(tuple(at + size * i + j for j in range(size)), c)

        carry = lax.fori_loop(0, count, step, carry)
        at = at + size * count
    return carry


def attend_rows(
    heads, rows_dev, first_slot, info_ref, qkv_ref, key_ref, out_ref, wide_ref, lse_ref, score_ref, bias_ref
):
    rows = qkv_ref.shape[1]
    cols = heads * HEAD_DIM
    first_len, me = info_ref[0, 0], info_ref[0, 2]
    tiles = rows // TILE
    per_slot = rows_dev // TILE

    def query_tile(i, carry):
        qb = ((first_slot + i // per_slot) ^ me) * per_slot + i % per_slot
        qs = pl.ds(pl.multiple_of(first_slot * rows_dev + i * TILE, TILE), TILE)
        at = pl.ds(pl.multiple_of(i * TILE, TILE), TILE)
        query_seg = segment_rows(TILE, first_len, qb * TILE, 0.0, NEG)
        queries = [
            jnp.concatenate([qkv_ref[h * HEAD_DIM : (h + 1) * HEAD_DIM, qs], query_seg], axis=0)
            for h in range(heads)
        ]
        low, high = tile_range(qb, first_len, tiles)

        def score_tiles(kbs, tops):
            kss = [pl.ds(tile_start(kb, rows_dev, me), TILE) for kb in kbs]
            kinds = [jnp.clip(kb - qb, -2, 2) + 2 for kb in kbs]
            ss = [[mm(key_ref[h, ks, :], queries[h]) for h in range(heads)] for ks in kss]
            tops = list(tops)
            for i, ks in enumerate(kss):
                for h in range(heads):
                    s = ss[i][h] + bias_ref[h * KINDS + kinds[i]]
                    score_ref[h, ks, :] = s
                    tops[h] = jnp.maximum(tops[h], jnp.max(s.reshape(TILE // 8, 8, TILE), axis=0))
            return tuple(tops)

        tops = over_tiles(low, high, score_tiles, (jnp.full((8, TILE), -3e38, F32),) * heads)
        tops = [jnp.max(t, axis=0, keepdims=True) for t in tops]

        def value_tiles(kbs, sums):
            kss = [pl.ds(tile_start(kb, rows_dev, me), TILE) for kb in kbs]
            sums = list(sums)
            ps = []
            for ks in kss:
                for h in range(heads):
                    p = jnp.exp(score_ref[h, ks, :] - tops[h])
                    total, acc = sums[h]
                    sums[h] = (total + jnp.sum(p.reshape(TILE // 8, 8, TILE), axis=0), acc)
                    ps.append(p.astype(BF16))
            for i, ks in enumerate(kss):
                for h in range(heads):
                    values = qkv_ref[2 * cols + h * HEAD_DIM : 2 * cols + (h + 1) * HEAD_DIM, ks]
                    total, acc = sums[h]
                    sums[h] = (total, acc + mm(values, ps[i * heads + h]))
            return tuple(sums)

        zero = (jnp.zeros((8, TILE), F32), jnp.zeros((HEAD_DIM, TILE), F32))
        sums = over_tiles(low, high, value_tiles, (zero,) * heads)
        for h in range(heads):
            total, acc = sums[h]
            total = jnp.sum(total, axis=0, keepdims=True)
            mixed = acc * (1.0 / total)
            hs = slice(h * HEAD_DIM, (h + 1) * HEAD_DIM)
            wide_ref[hs, at] = mixed
            out_ref[hs, at] = mixed.astype(BF16)
            lse_ref[h : h + 1, at] = tops[h] + jnp.log(total)
        return carry

    lax.fori_loop(0, tiles // 2, query_tile, 0)


def attend_far_kernel(
    heads,
    rows_dev,
    info_ref,
    base_ref,
    w_ref,
    slot0_ref,
    slot1_ref,
    slot2_ref,
    slot3_ref,
    out_ref,
    wide_ref,
    lse_ref,
    qkv_ref,
    key_ref,
    score_ref,
    bias_ref,
):
    rows = qkv_ref.shape[1]
    cols = heads * HEAD_DIM
    w_rows = w_ref[:, : 3 * cols].T
    for i, slot_ref in enumerate((slot0_ref, slot1_ref, slot2_ref, slot3_ref)):
        for begin in range(0, rows_dev, TILE):
            part = contract(w_rows, 1, slot_ref[begin : begin + TILE, :], 1)
            at = i * rows_dev + begin
            qkv_ref[:, at : at + TILE] = part.astype(BF16)
    build_bias(base_ref, bias_ref, heads)
    key_seg = segment_all(rows, rows_dev, info_ref[0, 0], info_ref[0, 2], 1.0, 0.0)
    for h in range(heads):
        key_ref[h] = jnp.concatenate(
            [qkv_ref[cols + h * HEAD_DIM : cols + (h + 1) * HEAD_DIM, :], key_seg], axis=0
        ).T
    far = rows // rows_dev // 2
    attend_rows(
        heads, rows_dev, far, info_ref, qkv_ref, key_ref, out_ref, wide_ref, lse_ref, score_ref, bias_ref
    )


def attend_near_kernel(
    heads, rows_dev, info_ref, base_ref, qkv_ref, key_ref, out_ref, wide_ref, lse_ref, score_ref, bias_ref
):
    build_bias(base_ref, bias_ref, heads)
    attend_rows(
        heads, rows_dev, 0, info_ref, qkv_ref, key_ref, out_ref, wide_ref, lse_ref, score_ref, bias_ref
    )


def attend_shapes(heads, rows):
    cols = heads * HEAD_DIM
    return (
        jax.ShapeDtypeStruct((cols, rows // 2), BF16),
        jax.ShapeDtypeStruct((cols, rows // 2), F32),
        jax.ShapeDtypeStruct((heads, rows // 2), F32),
    )


def attend_scratch(heads, rows):
    return [
        pltpu.VMEM((heads, rows, TILE), F32),
        pltpu.VMEM((heads * KINDS, TILE, TILE), F32),
    ]


def attend_far(info, base, weights, slots):
    rows_dev = slots[0].shape[0]
    rows = rows_dev * len(slots)
    cols = weights.shape[1] // 3
    heads = cols // HEAD_DIM
    return pl.pallas_call(
        functools.partial(attend_far_kernel, heads, rows_dev),
        out_shape=attend_shapes(heads, rows)
        + (
            jax.ShapeDtypeStruct((3 * cols, rows), BF16),
            jax.ShapeDtypeStruct((heads, rows, 2 * HEAD_DIM), BF16),
        ),
        in_specs=[SMEM] + [VMEM] * 6,
        out_specs=(VMEM,) * 5,
        scratch_shapes=attend_scratch(heads, rows),
        compiler_params=pltpu.CompilerParams(vmem_limit_bytes=58 << 20),
        cost_estimate=SHORT,
        name="attend_far",
    )(info, base, weights, *slots)


def attend_near(info, base, qkv, keys, rows_dev):
    heads, rows = keys.shape[:2]
    return pl.pallas_call(
        functools.partial(attend_near_kernel, heads, rows_dev),
        out_shape=attend_shapes(heads, rows),
        in_specs=[SMEM] + [VMEM] * 3,
        out_specs=(VMEM,) * 3,
        scratch_shapes=attend_scratch(heads, rows),
        compiler_params=pltpu.CompilerParams(vmem_limit_bytes=58 << 20),
        cost_estimate=SHORT,
        name="attend_near",
    )(info, base, qkv, keys)


def diagonal_sums(values):
    values = jnp.concatenate([jnp.zeros_like(values), values], axis=1)
    count = TILE
    while count > 1:
        count //= 2
        values = values[:count] + pltpu.roll(values[count:], 2 * TILE - count, 1)
    return values


def grad_rows_to(own_ref, send_ref, first_slot, grad_ref, w_ref):
    rows_dev = own_ref.shape[0]
    for slot, out_ref in ((first_slot + 1, send_ref), (first_slot, own_ref)):
        for begin in range(0, rows_dev, TILE):
            at = slot * rows_dev + begin
            part = contract(grad_ref[:, at : at + TILE], 0, w_ref[...], 1)
            out_ref[begin : begin + TILE, :] = part.astype(out_ref.dtype)


def attend_back_kernel(
    heads,
    rows_dev,
    info_ref,
    base_ref,
    lse0_ref,
    lse1_ref,
    grad0_ref,
    grad1_ref,
    qkv_far,
    wide0_far,
    wide1_far,
    key_far,
    w_far,
    diag_ref,
    out_far,
    far_send_far,
    far_own_far,
    near_send_far,
    near_own_far,
    qkv_ref,
    wide0_ref,
    wide1_ref,
    key_ref,
    w_ref,
    out_ref,
    far_send_ref,
    far_own_ref,
    near_send_ref,
    near_own_ref,
    sems,
    lse_ref,
    inner_ref,
    grad_ref,
    query_ref,
    value_rows,
    query_rows,
    grad_rows,
    key_acc,
    value_acc,
    bias_ref,
    table_ref,
):
    rows = qkv_ref.shape[1]
    cols = heads * HEAD_DIM
    first_len, me = info_ref[0, 0], info_ref[0, 2]
    tiles = rows // TILE
    moves = [
        pltpu.make_async_copy(source, target, sems.at[n])
        for n, (source, target) in enumerate(
            (
                (qkv_far, qkv_ref),
                (wide0_far, wide0_ref),
                (wide1_far, wide1_ref),
                (key_far, key_ref),
                (w_far, w_ref),
                (out_ref, out_far),
                (far_send_ref, far_send_far),
                (far_own_ref, far_own_far),
                (near_send_ref, near_send_far),
                (near_own_ref, near_own_far),
            )
        )
    ]
    for move in moves[:5]:
        move.start()
    key_acc[...] = jnp.zeros_like(key_acc)
    value_acc[...] = jnp.zeros_like(value_acc)
    table_ref[...] = jnp.zeros_like(table_ref)
    build_bias(base_ref, bias_ref, heads)
    query_seg = segment_all(rows, rows_dev, first_len, me, 0.0, NEG)
    q_of = [slice(h * HEAD_DIM, (h + 1) * HEAD_DIM) for h in range(heads)]
    k_of = [slice(cols + h * HEAD_DIM, cols + (h + 1) * HEAD_DIM) for h in range(heads)]
    v_of = [slice(2 * cols + h * HEAD_DIM, 2 * cols + (h + 1) * HEAD_DIM) for h in range(heads)]
    lse_ref[:, : rows // 2] = lse0_ref[...]
    lse_ref[:, rows // 2 :] = lse1_ref[...]
    grad_ref[:, : rows // 2] = grad0_ref[...]
    grad_ref[:, rows // 2 :] = grad1_ref[...]
    for move in moves[:3]:
        move.wait()
    for h in range(heads):
        queries = qkv_ref[q_of[h], :]
        query_ref[h] = jnp.concatenate([queries, query_seg], axis=0)
        query_rows[h] = queries.T
        value_rows[h] = qkv_ref[v_of[h], :].T
        grad_rows[h] = grad_ref[q_of[h], :].T
        for half, wide_ref in ((0, wide0_ref), (1, wide1_ref)):
            at = slice(half * rows // 2, (half + 1) * rows // 2)
            terms = grad_ref[q_of[h], at].astype(F32) * wide_ref[q_of[h], :]
            inner_ref[h : h + 1, at] = jnp.sum(terms, axis=0, keepdims=True)
    moves[3].wait()

    def query_tile(qb, carry):
        qs = pl.ds(tile_start(qb, rows_dev, me), TILE)
        low, high = tile_range(qb, first_len, tiles)
        grads = [grad_ref[q_of[h], qs] for h in range(heads)]
        inner = [inner_ref[h : h + 1, qs] for h in range(heads)]
        lse = [lse_ref[h : h + 1, qs] for h in range(heads)]

        def tiles_at(kbs, sums):
            kss = [pl.ds(tile_start(kb, rows_dev, me), TILE) for kb in kbs]
            kinds = [jnp.clip(kb - qb, -2, 2) + 2 for kb in kbs]
            ss = [[mm(key_ref[h, ks, :], query_ref[h, :, qs]) for h in range(heads)] for ks in kss]
            dps = [[mm(value_rows[h, ks, :], grads[h]) for h in range(heads)] for ks in kss]
            lows = []
            for i in range(len(kbs)):
                for h in range(heads):
                    p = jnp.exp(ss[i][h] + bias_ref[h * KINDS + kinds[i]] - lse[h])
                    ds = p * (dps[i][h] - inner[h])
                    table_ref[h * KINDS + kinds[i]] += ds
                    lows.append((p.astype(BF16), ds.astype(BF16)))
            sums = list(sums)
            for i, ks in enumerate(kss):
                for h in range(heads):
                    low_p, low_ds = lows[i * heads + h]
                    value_acc[h, ks, :] += mm(low_p, grad_rows[h, qs, :])
                    key_acc[h, ks, :] += mm(low_ds, query_rows[h, qs, :])
                    sums[h] = sums[h] + mm(qkv_ref[k_of[h], ks], low_ds)
            return tuple(sums)

        sums = tuple(jnp.zeros((HEAD_DIM, TILE), F32) for _ in range(heads))
        sums = over_tiles(low, high, tiles_at, sums, (4, 2, 1))
        for h in range(heads):
            out_ref[q_of[h], qs] = sums[h].astype(BF16)
        return carry

    lax.fori_loop(0, tiles, query_tile, 0)
    for h in range(heads):
        out_ref[k_of[h], :] = key_acc[h].astype(BF16).T
        out_ref[v_of[h], :] = value_acc[h].astype(BF16).T
    moves[5].start()
    moves[4].wait()
    grad_rows_to(far_own_ref, far_send_ref, rows // rows_dev // 2, out_ref, w_ref)
    moves[6].start()
    moves[7].start()
    grad_rows_to(near_own_ref, near_send_ref, 0, out_ref, w_ref)
    moves[8].start()
    moves[9].start()
    for i in range(heads * KINDS):
        if i % KINDS in (0, KINDS - 1):
            total = jnp.sum(table_ref[i], axis=0, keepdims=True)
            diag_ref[i : i + 1, :] = jnp.concatenate([total, jnp.zeros_like(total)], axis=1)
        else:
            diag_ref[i : i + 1, :] = diagonal_sums(table_ref[i])
    for move in moves[5:]:
        move.wait()


def attend_back(info, base, qkv, keys, wide, lse, grad, weights, rows_dev):
    rows = qkv.shape[1]
    width = weights.shape[0]
    heads = qkv.shape[0] // (3 * HEAD_DIM)
    cols = heads * HEAD_DIM
    far = pl.BlockSpec(memory_space=pl.ANY)
    half = [pltpu.VMEM((rows_dev, width), BF16)] * 4
    out = pl.pallas_call(
        functools.partial(attend_back_kernel, heads, rows_dev),
        out_shape=(
            jax.ShapeDtypeStruct((heads * KINDS, 2 * TILE), F32),
            jax.ShapeDtypeStruct((3 * cols, rows), BF16),
            *[jax.ShapeDtypeStruct((rows_dev, width), BF16)] * 4,
        ),
        in_specs=[SMEM] + [VMEM] * 5 + [far] * 5,
        out_specs=(VMEM,) + (far,) * 5,
        scratch_shapes=[
            pltpu.VMEM(qkv.shape, BF16),
            pltpu.VMEM(wide[0].shape, F32),
            pltpu.VMEM(wide[1].shape, F32),
            pltpu.VMEM(keys.shape, BF16),
            pltpu.VMEM(weights.shape, BF16),
            pltpu.VMEM((3 * cols, rows), BF16),
            *half,
            pltpu.SemaphoreType.DMA((10,)),
            pltpu.VMEM((heads, rows), F32),
            pltpu.VMEM((heads, rows), F32),
            pltpu.VMEM((cols, rows), BF16),
            pltpu.VMEM((heads, 2 * HEAD_DIM, rows), BF16),
            pltpu.VMEM((heads, rows, HEAD_DIM), BF16),
            pltpu.VMEM((heads, rows, HEAD_DIM), BF16),
            pltpu.VMEM((heads, rows, HEAD_DIM), BF16),
            pltpu.VMEM((heads, rows, HEAD_DIM), F32),
            pltpu.VMEM((heads, rows, HEAD_DIM), F32),
            pltpu.VMEM((heads * KINDS, TILE, TILE), F32),
            pltpu.VMEM((heads * KINDS, TILE, TILE), F32),
        ],
        compiler_params=pltpu.CompilerParams(vmem_limit_bytes=60 << 20),
        cost_estimate=LONG,
        name="attend_back",
    )(info, base, *lse, *grad, qkv, *wide, keys, weights)
    diagonals, grad_qkv, far_send, far_own, near_send, near_own = out
    return grad_qkv, diagonals, far_own, far_send, near_own, near_send


def scaled_rows(values):
    return values * lax.rsqrt(jnp.mean(values * values, axis=-1, keepdims=True) + EPS)


def join_kernel(rows_ref, near_ref, far_ref, gain_ref, middle_ref, low_ref):
    for rs in row_blocks(rows_ref.shape[0]):
        middle = rows_ref[rs, :].astype(F32) + near_ref[rs, :] + far_ref[rs, :].astype(F32)
        middle_ref[rs, :] = middle
        low_ref[rs, :] = (scaled_rows(middle) * gain_ref[...]).astype(BF16)


def row_blocks(rows):
    return [slice(begin, begin + TILE // 4) for begin in range(0, rows, TILE // 4)]


def norm_back_rows(values, upstream, gain):
    scale = lax.rsqrt(jnp.mean(values * values, axis=-1, keepdims=True) + EPS)
    normed = values * scale
    scaled = upstream * gain
    inner = jnp.mean(scaled * normed, axis=-1, keepdims=True)
    return scale * (scaled - normed * inner)


def middle_back_kernel(middle_ref, near_ref, far_ref, grads_ref, gain_ref, low_ref):
    for rs in row_blocks(middle_ref.shape[0]):
        upstream = near_ref[rs, :].astype(F32) + far_ref[rs, :].astype(F32)
        back = norm_back_rows(middle_ref[rs, :], upstream, gain_ref[...])
        low_ref[rs, :] = (grads_ref[rs, :].astype(F32) + back).astype(BF16)


def rows_back_kernel(rows_ref, near_ref, core_ref, far_ref, after_ref, gain_ref, low_ref):
    for rs in row_blocks(rows_ref.shape[0]):
        upstream = near_ref[rs, :].astype(F32) + core_ref[rs, :].astype(F32)
        upstream = upstream + far_ref[rs, :].astype(F32)
        back = norm_back_rows(rows_ref[rs, :].astype(F32), upstream, gain_ref[...])
        low_ref[rs, :] = (after_ref[rs, :].astype(F32) + back).astype(BF16)


def by_rows(kernel, name, gain, *operands, out, cost=SHORT):
    shape = operands[0].shape
    return pl.pallas_call(
        kernel,
        out_shape=tuple(jax.ShapeDtypeStruct(shape, kind) for kind in out),
        in_specs=[VMEM] * (len(operands) + 1),
        out_specs=(VMEM,) * len(out),
        compiler_params=pltpu.CompilerParams(vmem_limit_bytes=16 << 20),
        cost_estimate=cost,
        name=name,
    )(*operands, gain[None])


def out_proj_kernel(own_ref, other_ref, w_own_ref, w_other_ref, near_ref, send_ref):
    half = near_ref.shape[0]
    for begin in range(0, 2 * half, TILE):
        part = contract(own_ref[:, begin : begin + TILE], 0, w_own_ref[...], 0)
        part = part + contract(other_ref[:, begin : begin + TILE], 0, w_other_ref[...], 0)
        if begin < half:
            near_ref[begin : begin + TILE, :] = part
        else:
            send_ref[begin - half : begin - half + TILE, :] = part.astype(BF16)


def out_proj(own, other, w_own, w_other):
    half, width = own.shape[1] // 2, w_own.shape[1]
    return pl.pallas_call(
        out_proj_kernel,
        out_shape=(
            jax.ShapeDtypeStruct((half, width), F32),
            jax.ShapeDtypeStruct((half, width), BF16),
        ),
        in_specs=[VMEM] * 4,
        out_specs=(VMEM, VMEM),
        compiler_params=pltpu.CompilerParams(vmem_limit_bytes=16 << 20),
        cost_estimate=SHORT,
        name="out_proj",
    )(own, other, w_own, w_other)


def mixed_grads_kernel(middle0, middle1, w_own_ref, w_other_ref, own_ref, send_ref):
    half = middle0.shape[0]
    for w_ref, out_ref in ((w_other_ref, send_ref), (w_own_ref, own_ref)):
        for i, middle_ref in enumerate((middle0, middle1)):
            part = contract(w_ref[...], 1, middle_ref[...], 1)
            out_ref[:, i * half : (i + 1) * half] = part.astype(BF16)


def mixed_grads(middle, w_own, w_other):
    shape = jax.ShapeDtypeStruct((w_own.shape[0], 2 * middle[0].shape[0]), BF16)
    return pl.pallas_call(
        mixed_grads_kernel,
        out_shape=(shape, shape),
        in_specs=[VMEM] * 4,
        out_specs=(VMEM, VMEM),
        compiler_params=pltpu.CompilerParams(vmem_limit_bytes=16 << 20),
        cost_estimate=SHORT,
        name="mixed_grads",
    )(*middle, w_own, w_other)


def ffn_kernel(
    ring,
    normed0,
    normed1,
    grad0,
    grad1,
    inner0,
    inner1,
    outer0,
    outer1,
    own_ref,
    send_ref,
    out_own_ref,
    out_send_ref,
    grads_ref,
    gain_ref,
    hid_ref,
    pre_ref,
    acc_ref,
    out_acc_ref,
    left_ref,
    gain_acc,
):
    half, width = own_ref.shape
    part = inner0.shape[1]
    block = grads_ref.shape[1]
    per_part = part // TILE
    steps = 2
    sweeps = 2 * part // block
    step = pl.program_id(0)
    root, cubic = 0.7978845608028654, 0.044715
    places = [
        (normed_ref, grad_ref, begin, i * half + begin)
        for i, (normed_ref, grad_ref) in enumerate(((normed0, grad0), (normed1, grad1)))
        for begin in range(0, half, TILE)
    ]
    weights = ((inner0, outer0), (inner1, outer1))

    def products(inner_ref, outer_ref, index, place):
        normed_ref, grad_ref, begin, _ = place
        rs, js = slice(begin, begin + TILE), slice(index * TILE, (index + 1) * TILE)
        return mm(normed_ref[rs, :], inner_ref[:, js]), mm(grad_ref[rs, :], outer_ref[:, js])

    def hidden_part(inner_ref, outer_ref, offset):
        work = [(index, place) for index in range(per_part) for place in places]
        ahead = products(inner_ref, outer_ref, *work[0])
        for n, (index, place) in enumerate(work):
            a, dh = ahead
            if n + 1 < len(work):
                ahead = products(inner_ref, outer_ref, *work[n + 1])
            rs = slice(place[3], place[3] + TILE)
            to = slice(offset + index * TILE, offset + (index + 1) * TILE)
            square = a * a
            t = jnp.tanh(a * (root + (root * cubic) * square))
            half_a = 0.5 * a
            cdf = 0.5 + 0.5 * t
            slope = cdf + half_a * (1.0 - t * t) * (root + (3.0 * root * cubic) * square)
            hid_ref[rs, to] = (a * cdf).astype(BF16)
            pre_ref[rs, to] = (dh * slope).astype(BF16)

    def rows_out(kept_ref, w_ref, offset, sum_ref, near_ref, far_ref):
        for _, _, _, at in places:
            rs = slice(at, at + TILE)
            back = contract(kept_ref[rs, offset : offset + part], 1, w_ref[...], 1)
            if offset == 0:
                sum_ref[rs, :] = back
            elif at < half:
                near_ref[rs, :] = (sum_ref[rs, :] + back).astype(BF16)
            else:
                far_ref[at - half : at - half + TILE, :] = (sum_ref[rs, :] + back).astype(BF16)

    for i, (inner_ref, outer_ref) in enumerate(weights):

        @pl.when(step == i)
        def _(inner_ref=inner_ref, outer_ref=outer_ref, offset=i * part):
            hidden_part(inner_ref, outer_ref, offset)
            rows_out(pre_ref, inner_ref, offset, acc_ref, own_ref, send_ref)
            rows_out(hid_ref, outer_ref, offset, out_acc_ref, out_own_ref, out_send_ref)

    def load(first_ref, second_ref):
        left_ref[:, :half] = first_ref[...].T
        left_ref[:, half:] = second_ref[...].T

    for i in range(sweeps):

        @pl.when(step == steps + i)
        def _(i=i):
            if i == 0:
                load(normed0, normed1)
            values = mm(left_ref[...], pre_ref[:, i * block : (i + 1) * block])
            store_ringed(grads_ref, ring, 0, block, values.astype(BF16))
            lanes = gain_acc.shape[1]
            total = jnp.zeros(gain_acc.shape, F32) if i == 0 else gain_acc[...]
            for b in range(0, block, lanes):
                at = i * block + b
                w_ref = inner0 if at < part else inner1
                w = w_ref[:, at % part : at % part + lanes].astype(F32)
                total = total + values[:, b : b + lanes] * w
            gain_acc[...] = total
            if i == sweeps - 1:
                gain_ref[...] = jnp.sum(total.T, axis=0, keepdims=True)

        @pl.when(step == steps + sweeps + i)
        def _(i=i):
            if i == 0:
                load(grad0, grad1)
            values = mm(left_ref[...], hid_ref[:, i * block : (i + 1) * block])
            store_ringed(grads_ref, ring, 0, block, values.astype(BF16))


def ffn(ring, normed, grads, inners, outers):
    half, width = normed[0].shape
    part = inners[0].shape[1]
    rows, hidden = 2 * half, 2 * part
    block = 2 * TILE
    steps = 2
    return pl.pallas_call(
        functools.partial(ffn_kernel, ring),
        grid=(steps + 2 * (hidden // block),),
        out_shape=(
            pltpu.HBM((half, width), BF16),
            pltpu.VMEM((half, width), BF16),
            *[pltpu.HBM((half, width), BF16)] * 2,
            pltpu.HBM((width, 2 * hidden), BF16),
            pltpu.HBM((1, width), F32),
        ),
        in_specs=[VMEM] * 8,
        out_specs=(
            VMEM,
            VMEM,
            VMEM,
            VMEM,
            pl.BlockSpec((width, block), lambda j: (0, jnp.maximum(j - steps, 0))),
            pl.BlockSpec((1, width), lambda j: (0, 0)),
        ),
        scratch_shapes=[
            pltpu.VMEM((rows, hidden), BF16),
            pltpu.VMEM((rows, hidden), BF16),
            pltpu.VMEM((rows, width), F32),
            pltpu.VMEM((rows, width), F32),
            pltpu.VMEM((width, rows), BF16),
            pltpu.VMEM((width, 128), F32),
        ],
        compiler_params=pltpu.CompilerParams(vmem_limit_bytes=44 << 20),
        cost_estimate=SHORT,
        name="ffn",
    )(*normed, *grads, *inners, *outers)


def proj_grads_kernel(middle0, middle1, mixed0, mixed1, out_ref):
    half = middle0.shape[0]
    total = 0.0
    for i, middle_ref in enumerate((middle0, middle1)):
        at = slice(i * half, (i + 1) * half)
        mixed = jnp.concatenate([mixed0[:, at], mixed1[:, at]], axis=0)
        total = total + contract(middle_ref[...].T, 1, mixed, 1)
    out_ref[...] = total.astype(BF16)


def proj_grads(middle, mixed):
    shape = (middle[0].shape[1], 2 * mixed[0].shape[0])
    return pl.pallas_call(
        proj_grads_kernel,
        out_shape=jax.ShapeDtypeStruct(shape, BF16),
        in_specs=[VMEM] * 4,
        out_specs=VMEM,
        compiler_params=pltpu.CompilerParams(vmem_limit_bytes=24 << 20),
        cost_estimate=SHORT,
        name="proj_grads",
    )(*middle, *mixed)


def qkv_grads_kernel(
    ring,
    grad_ref,
    slot0_ref,
    slot1_ref,
    slot2_ref,
    slot3_ref,
    w_ref,
    proj_ref,
    out_ref,
    gain_ref,
):
    rows_dev = slot0_ref.shape[0]
    total = 0.0
    for i, slot_ref in enumerate((slot0_ref, slot1_ref, slot2_ref, slot3_ref)):
        total = total + mm(grad_ref[:, i * rows_dev : (i + 1) * rows_dev], slot_ref[...])
    gain_ref[...] = jnp.sum(total * w_ref[:, : total.shape[0]].T.astype(F32), axis=0, keepdims=True)
    both = jnp.concatenate([total.T.astype(BF16), proj_ref[...]], axis=1)
    store_ringed(out_ref, ring, 0, out_ref.shape[1], both)


def qkv_grads(ring, grad_qkv, slots, weights, proj):
    width = slots[0].shape[1]
    cols = grad_qkv.shape[0] + proj.shape[1]
    return pl.pallas_call(
        functools.partial(qkv_grads_kernel, ring),
        out_shape=(
            jax.ShapeDtypeStruct((width, cols), BF16),
            jax.ShapeDtypeStruct((1, width), F32),
        ),
        in_specs=[VMEM] * 7,
        out_specs=(VMEM, VMEM),
        compiler_params=pltpu.CompilerParams(vmem_limit_bytes=58 << 20),
        cost_estimate=SHORT,
        name="qkv_grads",
    )(grad_qkv, *slots, weights, proj)


def finish_kernel(pack_ref, taken_ref, inner_ref, outer_ref):
    hidden = inner_ref.shape[1]
    pack, taken = pack_ref[...].astype(F32), taken_ref[...].astype(F32)
    inner_ref[...] = pack[:, :hidden] + taken[:, :hidden]
    outer_ref[...] = pack[:, 2 * hidden : 3 * hidden] + taken[:, hidden:]


def finish(pack, taken):
    shape = jax.ShapeDtypeStruct((taken.shape[0], taken.shape[1] // 2), F32)
    return pl.pallas_call(
        finish_kernel,
        out_shape=(shape, shape),
        in_specs=[VMEM] * 2,
        out_specs=(VMEM,) * 2,
        cost_estimate=SHORT,
        name="finish",
    )(pack, taken)


def finish_last_kernel(last_ref, far_ref, query_ref, key_ref, value_ref, proj_ref):
    cols = query_ref.shape[1]
    last = last_ref[...].astype(F32)
    for i, out_ref in enumerate((query_ref, key_ref, value_ref)):
        out_ref[...] = last[:, i * cols : (i + 1) * cols]
    proj_ref[...] = (last[:, 3 * cols : 4 * cols] + far_ref[...].astype(F32)).T


def finish_last(last, far):
    rows, cols = far.shape
    shapes = [(rows, cols)] * 3 + [(cols, rows)]
    return pl.pallas_call(
        finish_last_kernel,
        out_shape=tuple(jax.ShapeDtypeStruct(shape, F32) for shape in shapes),
        in_specs=[VMEM] * 2,
        out_specs=(VMEM,) * 4,
        cost_estimate=SHORT,
        name="finish_last",
    )(last, far)


def bias_rows(line):
    heads = line.shape[0]
    pad = 3 * TILE
    rev = jnp.flip(line, axis=1)
    left = jnp.broadcast_to(rev[:, :1], (heads, pad))
    right = jnp.broadcast_to(rev[:, -1:], (heads, pad + 2 * TILE))
    ext = jnp.concatenate([left, rev, right], axis=1)
    begin = [pad + MAXDIST - TILE - TILE * d for d in range(-2, 3)]
    rows = [ext[:, b : b + 2 * TILE] for b in begin]
    return jnp.stack(rows, axis=1).reshape(heads * KINDS, 2 * TILE)


def line_index():
    kind = lax.broadcasted_iota(jnp.int32, (KINDS, 2 * TILE), 0) - 2
    lane = lax.broadcasted_iota(jnp.int32, (KINDS, 2 * TILE), 1)
    near = jnp.clip(TILE + TILE * kind - lane, -MAXDIST, MAXDIST)
    far = jnp.where(kind < 0, -MAXDIST, MAXDIST)
    return (jnp.where(jnp.abs(kind) == 2, far, near) + MAXDIST).reshape(KINDS * 2 * TILE)


def on_device(
    tokens,
    cotangent,
    w_query,
    w_key,
    w_value,
    w_proj,
    w_inner,
    w_outer,
    gain_attn,
    gain_ffn,
    rel_table,
    lengths,
    deal,
    buckets,
):
    rows_dev = tokens.shape[0]
    tensor_size = lax.axis_size("tensor")
    dp_size = lax.axis_size("dp")
    me = lax.axis_index("tensor")
    heads = w_query.shape[1] // HEAD_DIM
    cols = heads * HEAD_DIM
    hidden = w_inner.shape[1]
    width = tokens.shape[1]
    pair = 2 * rows_dev

    def swap(values, bit):
        return lax.ppermute(values, "tensor", [(i, i ^ bit) for i in range(tensor_size)])

    def deal_out(values):
        return lax.all_to_all(values, "dp", split_axis=0, concat_axis=0, tiled=True)

    def sum_groups(values):
        step = 1
        while step < dp_size:
            values = values + lax.ppermute(values, "dp", [(i, i ^ step) for i in range(dp_size)])
            step *= 2
        return values

    ring = ring_order(dp_size)
    both = ("dp", "tensor")
    ring_groups = [[d * tensor_size + t for d in ring] for t in range(tensor_size)]

    def gather(values, spans):
        found = lax.all_gather(values, both, axis=0, tiled=True, axis_index_groups=ring_groups)
        return unring(found, ring, spans)

    def scatter_sum(values):
        return lax.psum_scatter(
            ringed(values, ring), both, scatter_dimension=0, tiled=True, axis_index_groups=ring_groups
        )

    own_front, own_rest = pack_weights(
        w_inner, w_query, w_key, w_value, w_proj, w_outer.T
    )
    own_front, tokens = after(own_front, tokens)
    ends = (3 * cols, 3 * cols + hidden, 4 * cols + hidden)
    front, outer_own, proj_own = gather(
        own_front, ((0, ends[0], False), (ends[0], ends[1], False), (ends[1], ends[2], True))
    )
    low_rows = deal_out(chosen(tokens, deal))
    other_rest, low_rows = after(swap(own_rest, 2), low_rows)
    inner_own, inner_other, proj_other = gather(
        jnp.concatenate([own_rest[:, :hidden], other_rest], axis=1),
        (
            (0, hidden, False),
            (hidden, 2 * hidden, False),
            (2 * hidden, 2 * hidden + cols, True),
        ),
    )
    onehot_buckets = (
        buckets[:, None] == jnp.arange(rel_table.shape[0], dtype=jnp.int32)[None, :]
    ).astype(F32)
    head_table = lax.dynamic_slice_in_dim(rel_table, me * heads, heads, 1)
    offset_bias = jnp.dot(onehot_buckets, head_table, precision=lax.Precision.HIGHEST).T
    base = bias_rows(offset_bias)
    info = jnp.concatenate([lengths, jnp.full((1, 1), me, jnp.int32)], axis=1)

    slot0 = (scaled_rows(low_rows.astype(F32)) * gain_attn).astype(BF16)
    slot2 = swap(slot0, 2)
    slot1 = swap(slot0, 1)
    slot2, front, base, info = after(slot2, front, base, info)
    slot3 = swap(slot2, 1)
    slots = (slot0, slot1, slot2, slot3)
    outer_other = swap(outer_own, 2)

    low_grads = deal_out(chosen(cotangent, deal))

    mixed_far, wide_far, lse_far, qkv, keys = attend_far(info, base, front, slots)
    mixed_other = swap(mixed_far, 2)
    late_qkv, low_grads = after(qkv, low_grads)
    mixed_own, wide_own, lse_own = attend_near(info, base, late_qkv, keys, rows_dev)
    mixed_own, outer_other, inner_own = after(mixed_own, outer_other, inner_own)
    near, to_core = out_proj(mixed_own, mixed_other, proj_own, proj_other)
    middle, low_two = by_rows(
        join_kernel, "join", gain_ffn, low_rows, near, swap(to_core, 1), out=(F32, BF16)
    )

    pair_two = (low_two, swap(low_two, 1))
    pair_grads = (low_grads, swap(low_grads, 1))
    back_own, back_send, out_own, out_far, grad_pack, gain_two = ffn(
        ring, pair_two, pair_grads, (inner_own, inner_other), (outer_own, outer_other)
    )
    shard_pack = scatter_sum(grad_pack)
    (low_middle,) = by_rows(
        middle_back_kernel,
        "middle_back",
        gain_ffn,
        middle,
        back_own,
        swap(back_send, 1),
        low_grads,
        out=(BF16,),
    )
    pair_middle = (low_middle, swap(low_middle, 1))
    grad_own, to_other = mixed_grads(pair_middle, proj_own, proj_other)

    proj_pack = proj_grads(pair_middle, (mixed_own, mixed_other))

    out_own, to_other = after(out_own, to_other)
    result_rows = (middle + out_own.astype(F32) + swap(out_far, 1).astype(F32)).astype(BF16)
    result_rows, proj_pack = after(result_rows, proj_pack)
    back_rows = deal_out(result_rows)

    grad_far, proj_pack = after(swap(to_other, 2), proj_pack)
    grad_qkv, diagonals, far_own, far_send, near_own, near_send = attend_back(
        info,
        base,
        qkv,
        keys,
        (wide_own, wide_far),
        (lse_own, lse_far),
        (grad_own, grad_far),
        front,
        rows_dev,
    )
    far_send, back_rows = after(far_send, back_rows)
    grad_later = (far_own.astype(F32) + swap(far_send, 1).astype(F32)).astype(BF16)
    offset_count = 2 * MAXDIST + 1
    onehot_line = (
        line_index()[:, None] == jnp.arange(offset_count, dtype=jnp.int32)[None, :]
    ).astype(F32)
    offset_total = jnp.dot(
        diagonals.reshape(heads, KINDS * 2 * TILE), onehot_line, precision=lax.Precision.HIGHEST
    )
    table_heads = jnp.dot(onehot_buckets.T, offset_total.T, precision=lax.Precision.HIGHEST)
    table_full = lax.dynamic_update_slice_in_dim(
        jnp.zeros(rel_table.shape, F32), table_heads, me * heads, 1
    )
    grad_later, near_send, table_full = after(grad_later, near_send, table_full)
    later_qkv, grad_later = after(grad_qkv, grad_later)
    low_qkv_w, gain_one = qkv_grads(ring, later_qkv, slots, front, proj_pack)
    low_qkv_w, shard_pack = after(low_qkv_w, shard_pack)
    shard_qkv = scatter_sum(low_qkv_w)
    taken = swap(
        jnp.concatenate([shard_pack[:, hidden : 2 * hidden], shard_pack[:, 3 * hidden :]], axis=1),
        2,
    )
    terms = [gain_one[0] / gain_attn, gain_two[0] / gain_ffn, table_full.reshape(-1)]
    small = sum_groups(jnp.concatenate(terms).reshape(-1, 128))
    grad_two_rows, small = after(swap(grad_later, 2), small)
    small = small + swap(small, 1)
    small, taken = after(small, taken)
    small = small + swap(small, 2)

    near_core = swap(near_send, 1)
    (low_grad_rows,) = by_rows(
        rows_back_kernel,
        "rows_back",
        gain_attn,
        low_rows,
        near_own,
        near_core,
        grad_two_rows,
        low_middle,
        out=(BF16,),
        cost=pl.CostEstimate(flops=(3<<33)//2, bytes_accessed=(1<<26)//2, transcendentals=(1<<23)//2),
    )

    shard_far = swap(shard_qkv[:, 4 * cols :], 2)
    weight_shards = [*finish_last(shard_qkv, shard_far), *finish(shard_pack, taken)]
    out_rows = deal_rows(back_rows, deal, True)
    small = small.reshape(-1)
    back_grads = deal_out(low_grad_rows)
    back_grads, out_rows, *weight_shards = after(back_grads, out_rows, *weight_shards)
    return (
        out_rows,
        deal_rows(back_grads, deal, True),
        *weight_shards[:3],
        *weight_shards[3:5],
        weight_shards[5].T,
        small[:width],
        small[width : 2 * width],
        small[2 * width :].reshape(rel_table.shape),
    )


def solution(mesh):
    rows = P(("dp", "tensor"), None)
    inward, outward = P("dp", "tensor"), P("tensor", "dp")
    weights = (inward, inward, inward, outward, inward, outward)
    return jax.shard_map(
        on_device,
        mesh=mesh,
        in_specs=(rows, rows, *weights, P(), P(), P(), P("dp", None), P(("dp", "tensor")), P()),
        out_specs=(rows, rows, *weights, P(), P(), P()),
        check_vma=False,
    )
```
